128 devices in a mesh: dp: 2 (over z_hi), space: 64 (over y, z_lo, x, core).
Axes of the slice: x: 4, y: 4, z: 4 (z_hi: 2, z_lo: 2; z = z_hi * 2 + z_lo), core: 2. Of those that a mesh axis runs over, the one named last changes fastest.
Arguments:
- features: bfloat16 [2, 64, 128, 256], P('dp', 'space'), may hold values from -50 to 50
- qkv_weight: bfloat16 [256, 768], replicated, may hold values from -0.75 to 0.75
- out_weight: bfloat16 [256, 256], replicated, may hold values from -0.375 to 0.375
- conv_weight: bfloat16 [3, 3, 256, 128], replicated, may hold values from -0.125 to 0.125
- grad_output: bfloat16 [2, 128, 256, 128], P('dp', 'space'), may hold values from -6 to 6
Outputs:
- grad_features: float32 [2, 64, 128, 256], P('dp', 'space')
- grad_qkv: float32 [256, 768], replicated
- grad_out: float32 [256, 256], replicated
- grad_conv: float32 [3, 3, 256, 128], replicated
The draws below stay inside these ranges and needn't reach their ends.
All inputs are finite; a program needn't handle non-finite values.
Results may differ from the reference program's by a relative error of at most 0.004.
The reference program's roundings to bfloat16 on the way count: a program that leaves them out, or rounds other values in their place, can miss the bound.
Values may be sent and summed in bfloat16 or wider, within the bound.
A program may use at most 128 MiB of HBM per device.

```python
import math
import jax
import jax.numpy as jnp
from jax import lax

C2 = 256
C1 = 128
HDIM = 64
WB = 128
HB = 64
SEQ = 8192
BATCH = 2
H_FINE = 128
W_FINE = 256


def draw_features(key, part):
    key = jax.random.fold_in(key, 11)
    base_key = jax.random.fold_in(key, 0)
    positions = HB * WB
    values = jnp.clip(jax.random.normal(base_key, (BATCH, positions, C2), jnp.float32), -6.0, 6.0)
    return values.reshape(BATCH, HB, WB, C2).astype(jnp.bfloat16)


def draw_qkv_weight(key, part):
    key = jax.random.fold_in(key, 23)
    query_key, key_key, value_key = jax.random.split(key, 3)
    sharp = 1.6 / math.sqrt(C2)
    drawn = 1.0 / math.sqrt(C2)
    queries = jnp.clip(jax.random.normal(query_key, (C2, C2), jnp.float32), -6.0, 6.0) * sharp
    key_part = jnp.clip(jax.random.normal(key_key, (C2, C2), jnp.float32), -6.0, 6.0) * sharp
    value_part = jnp.clip(jax.random.normal(value_key, (C2, C2), jnp.float32), -6.0, 6.0) * drawn
    whole = jnp.concatenate([queries, key_part, value_part], axis=1)
    return jnp.clip(whole, -0.75, 0.75).astype(jnp.bfloat16)


def levels(key, shape, cuts, low, top_value):
    factor_of, own = 1.0, jax.random.fold_in(key, 6)
    for dim, blocks in cuts:
        heights = jnp.exp(jax.random.uniform(jax.random.fold_in(own, dim), (blocks,), jnp.float32, low / len(cuts), top_value / len(cuts)))
        factor_of = factor_of * jnp.repeat(heights, shape[dim] // blocks).reshape([-1 if axis == dim else 1 for axis in range(len(shape))])
    return factor_of


def bell_draw(stream_key, shape, scale, most, cuts=(), kind=jnp.bfloat16):
    drawn = jax.random.normal(stream_key, shape, jnp.float32) * scale
    if len(cuts) > 0:
        drawn = levels(stream_key, shape, cuts, -0.22, 0.18) * drawn
    return jnp.clip(drawn, min=-most, max=most).astype(kind)


def setup_inputs(seed: int = 0) -> dict:
    keys = jax.random.split(jax.random.key(seed), 6)
    return {
        "features": draw_features(jax.random.fold_in(keys[5], 71), 0),
        "qkv_weight": draw_qkv_weight(jax.random.fold_in(keys[5], 71), 0),
        "out_weight": bell_draw(keys[2], (C2, C2), C2 ** -0.5, 0.375),
        "conv_weight": bell_draw(keys[3], (3, 3, C2, C1), (9 * C2) ** -0.5, 0.125),
        "grad_output": bell_draw(keys[4], (BATCH, H_FINE, W_FINE, C1), 1.0, 6.0, ((0, 2), (1, 64))),
    }


def rounded(array):
    return lax.optimization_barrier(array.astype(jnp.bfloat16)).astype(jnp.float32)

def attend_sample(packed):
    projected, grad_attended = packed
    head_count = C2 // HDIM
    block_size = math.gcd(SEQ, 512)
    scaling = 1.0 / math.sqrt(HDIM)
    queries = projected[:, :C2].astype(jnp.float32).reshape(SEQ, head_count, HDIM)
    key_rows = projected[:, C2:2 * C2].astype(jnp.float32).reshape(SEQ, head_count, HDIM)
    value_rows = projected[:, 2 * C2:].astype(jnp.float32).reshape(SEQ, head_count, HDIM)
    grad_rows = grad_attended.astype(jnp.float32).reshape(SEQ, head_count, HDIM)

    def one_block(carried, block_index):
        grad_keys, grad_values = carried
        first_row = block_index * block_size
        query_block = lax.dynamic_slice_in_dim(queries, first_row, block_size, 0)
        grad_block = lax.dynamic_slice_in_dim(grad_rows, first_row, block_size, 0)
        scores = jnp.einsum('qhd,khd->hqk', query_block, key_rows) * scaling
        highest = lax.optimization_barrier(jnp.max(scores, axis=-1, keepdims=True))
        log_total = highest + jnp.log(lax.optimization_barrier(jnp.sum(jnp.exp(scores - highest), axis=-1, keepdims=True)))
        weights = jnp.exp(scores - log_total)
        low_weights = rounded(weights)
        attended = jnp.einsum('hqk,khd->qhd', low_weights, value_rows)
        grad_weights = jnp.einsum('qhd,khd->hqk', grad_block, value_rows)
        row_delta = lax.optimization_barrier(jnp.sum(weights * grad_weights, axis=-1, keepdims=True))
        grad_scores = rounded(weights * (grad_weights - row_delta))
        grad_queries = jnp.einsum('hqk,khd->qhd', grad_scores, key_rows) * scaling
        grad_keys = grad_keys + jnp.einsum('hqk,qhd->khd', grad_scores, query_block) * scaling
        grad_values = grad_values + jnp.einsum('hqk,qhd->khd', low_weights, grad_block)
        return ((grad_keys, grad_values), (attended, grad_queries))
    empty_grads = jnp.zeros((SEQ, head_count, HDIM), jnp.float32)
    (grad_keys, grad_values), (attended, grad_queries) = lax.scan(one_block, (empty_grads, empty_grads), jnp.arange(SEQ // block_size))
    return (attended.reshape(SEQ, C2), grad_queries.reshape(SEQ, C2), grad_keys.reshape(SEQ, C2), grad_values.reshape(SEQ, C2))

def reference(features, qkv_weight, out_weight, conv_weight, grad_output):
    flat = features.astype(jnp.float32).reshape(BATCH, SEQ, C2)
    padded = jnp.pad(grad_output.astype(jnp.float32), ((0, 0), (1, 1), (1, 1), (0, 0)))
    grad_up = jnp.zeros((BATCH, H_FINE, W_FINE, C2), jnp.float32)
    for row_off in range(3):
        for col_off in range(3):
            window = padded[:, 2 - row_off:2 - row_off + H_FINE, 2 - col_off:2 - col_off + W_FINE, :]
            grad_up = grad_up + jnp.einsum('brcy,xy->brcx', window, conv_weight[row_off, col_off].astype(jnp.float32))
    grad_hidden = grad_up.reshape(BATCH, HB, 2, WB, 2, C2).sum(axis=(2, 4))
    grad_hidden_low = rounded(grad_hidden)
    grad_attended = rounded(jnp.einsum('brcy,xy->brcx', grad_hidden_low, out_weight.astype(jnp.float32)))
    grad_attended = grad_attended.reshape(BATCH, SEQ, C2)
    projected = rounded(jnp.einsum('bnx,xy->bny', flat, qkv_weight.astype(jnp.float32)))
    attended, grad_queries, grad_keys, grad_values = lax.map(attend_sample, (projected, grad_attended))
    attended_low = rounded(attended)
    grad_proj = rounded(jnp.concatenate([grad_queries, grad_keys, grad_values], axis=-1))
    coarse_scale = 1.0 / math.sqrt(BATCH * SEQ)
    fine_scale = 1.0 / math.sqrt(BATCH * H_FINE * W_FINE)
    grad_qkv = coarse_scale * jnp.einsum('bnx,bny->xy', flat, grad_proj)
    grad_out = coarse_scale * jnp.einsum('bnx,bny->xy', attended_low, grad_hidden_low.reshape(BATCH, SEQ, C2))
    hidden = rounded(flat + jnp.einsum('bnx,xy->bny', attended_low, out_weight.astype(jnp.float32)))
    upsampled = jnp.repeat(jnp.repeat(hidden.reshape(BATCH, HB, WB, C2), 2, axis=1), 2, axis=2)
    upsampled = jnp.pad(upsampled, ((0, 0), (1, 1), (1, 1), (0, 0)))
    grad_fine = grad_output.astype(jnp.float32)
    grad_conv = jnp.stack([jnp.stack([fine_scale * jnp.einsum('brcx,brcy->xy', upsampled[:, row_off:row_off + H_FINE, col_off:col_off + W_FINE, :], grad_fine) for col_off in range(3)]) for row_off in range(3)])
    grad_features = grad_hidden + jnp.einsum('bny,xy->bnx', grad_proj, qkv_weight.astype(jnp.float32)).reshape(BATCH, HB, WB, C2)
    return (grad_features, grad_qkv, grad_out, grad_conv)
```

```python
import math

import jax
import jax.numpy as jnp
from jax import lax
from jax.experimental import pallas as pl
from jax.experimental.pallas import tpu as pltpu
from jax.sharding import PartitionSpec as P

MESH = pl.DeviceIdType.MESH
F32 = jnp.float32
BF16 = jnp.bfloat16
HDIM = 64
HEADS = 4
CH = 256
CO = 128
ROW = 128
RING = 4
CHUNK = RING * ROW
CHUNKS = 8
STACK = 2 * HEADS * ROW
HALF = STACK // 2
SUB = 32
REST_ROWS = 3072
QKV_ROWS = 1536
AG_MSGS = 41
ST_MSGS = 13
RS_MSGS = 17


def nt(a, b):
    return lax.dot_general(a, b, (((1,), (1,)), ((), ())), preferred_element_type=F32)


def tn(a, b):
    return lax.dot_general(a, b, (((0,), (0,)), ((), ())), preferred_element_type=F32)


def nn(a, b):
    return jnp.dot(a, b, preferred_element_type=F32)


class Message:
    def __init__(self, src, dst, landing, sems, slot, device):
        send, recv = sems
        self.out = pltpu.make_async_remote_copy(
            src_ref=src, dst_ref=dst, send_sem=send.at[slot], recv_sem=recv.at[slot], device_id=device, device_id_type=MESH
        )
        self.into = pltpu.make_async_remote_copy(
            src_ref=landing, dst_ref=landing, send_sem=send.at[slot], recv_sem=recv.at[slot], device_id=device, device_id_type=MESH
        )

    def start(self):
        self.out.start()

    def arrived(self):
        self.into.wait_recv()

    def sent(self):
        self.out.wait_send()


class Place:
    def __init__(self):
        self.d = lax.axis_index("dp")
        self.s = lax.axis_index("space")
        s = self.s
        self.c = lax.rem(s, 2)
        self.x = lax.rem(s // 2, RING)
        self.zl = lax.rem(s // 8, 2)
        self.y = s // 16
        self.zo = 1 - self.zl

    def at(self, d=None, y=None, z=None, x=None, c=None):
        d = self.d if d is None else d
        y = self.y if y is None else y
        z = self.zl if z is None else z
        x = self.x if x is None else x
        c = self.c if c is None else c
        return (d, ((y * 2 + z) * RING + x) * 2 + c)

    def line(self, step):
        return (self.d, lax.rem(self.s + step + 64, 64))

    def ring_x(self, step):
        return self.at(x=lax.rem(self.x + step + RING, RING))

    def ring_y(self, step):
        return self.at(y=lax.rem(self.y + step + RING, RING))

    def first(self, t, step):
        hit = t == 0
        return self.at(
            x=jnp.where(hit, lax.rem(self.x + step + RING, RING), self.x),
            y=jnp.where(hit, self.y, lax.rem(self.y + step + RING, RING)),
        )

    def second(self, t, step):
        return self.first(1 - t, step)

    def coords(self, t):
        return jnp.where(t == 0, self.y, self.x), jnp.where(t == 0, self.x, self.y)


class Gather:
    def __init__(self, place, buf, sems, base):
        self.place, self.buf, self.sems, self.count, self.base = place, buf, sems, 0, base
        half = ROW // 2
        low, high = pl.ds(0, half), pl.ds(half, half)
        s0, f0 = place.coords(place.zl)
        s1, f1 = place.coords(place.zo)
        m = {"z": self.make((place.zl, s0, f0), (place.zo, s1, f1), place.at(z=place.zo))}
        for r in (0, 1):
            t = place.zl if r == 0 else place.zo
            s, f = (s0, f0) if r == 0 else (s1, f1)
            sm, sp, s2 = (lax.rem(s + k, RING) for k in (3, 1, 2))
            fm, fp, f2 = (lax.rem(f + k, RING) for k in (3, 1, 2))
            up, down = place.first(t, 1), place.first(t, -1)
            m[r, "1+"] = self.make((t, s, f), (t, s, fm), up)
            m[r, "1-"] = self.make((t, s, f), (t, s, fp), down)
            m[r, "1f+"] = self.make((t, s, fm, low), (t, s, f2, low), up)
            m[r, "1f-"] = self.make((t, s, fp, high), (t, s, f2, high), down)
            up, down = place.second(t, 1), place.second(t, -1)
            for q, g in enumerate((f, fm, fp, f2)):
                m[r, q, "2+"] = self.make((t, s, g), (t, sm, g), up)
                m[r, q, "2-"] = self.make((t, s, g), (t, sp, g), down)
                m[r, q, "2f+"] = self.make((t, sm, g, low), (t, s2, g, low), up)
                m[r, q, "2f-"] = self.make((t, sp, g, high), (t, s2, g, high), down)
        self.m = m

    def make(self, src, landing, device):
        slot = self.base + self.count
        self.count += 1
        src = self.buf.at[src]
        return Message(src, src, self.buf.at[landing], self.sems, slot, device)

    def go(self, *keys):
        for key in keys:
            self.m[key].start()

    def begin(self):
        self.go("z", (0, "1+"), (0, "1-"), (0, 0, "2+"), (0, 0, "2-"))

    def other(self):
        self.m["z"].arrived()
        self.go((1, "1+"), (1, "1-"), (1, 0, "2+"), (1, 0, "2-"))

    def near(self, r):
        self.m[r, "1+"].arrived()
        self.go((r, "1f+"), (r, 1, "2+"), (r, 1, "2-"))
        self.m[r, "1-"].arrived()
        self.go((r, "1f-"), (r, 2, "2+"), (r, 2, "2-"))

    def pass_on(self, r, *blocks):
        for q in blocks:
            self.m[r, q, "2+"].arrived()
            self.go((r, q, "2f+"))
            self.m[r, q, "2-"].arrived()
            self.go((r, q, "2f-"))

    def far(self, r):
        self.m[r, "1f+"].arrived()
        self.m[r, "1f-"].arrived()
        self.go((r, 3, "2+"), (r, 3, "2-"))

    def last(self, r):
        for q in range(4):
            self.m[r, q, "2f+"].arrived()
            self.m[r, q, "2f-"].arrived()

    def finish(self):
        for message in self.m.values():
            message.sent()


class StatGather:
    def __init__(self, place, buf, sems, base):
        s0, f0 = place.coords(place.zl)
        s1, f1 = place.coords(place.zo)
        src = buf.at[place.zl, s0, f0]
        self.z = Message(src, src, buf.at[place.zo, s1, f1], sems, base, place.at(z=place.zo))
        self.one, self.two = {}, {}
        slot = base + 1
        for r in (0, 1):
            t = place.zl if r == 0 else place.zo
            s, f = (s0, f0) if r == 0 else (s1, f1)
            for k in (1, 3, 2):
                src = buf.at[t, s, f]
                self.one[r, k] = Message(src, src, buf.at[t, s, lax.rem(f + RING - k, RING)], sems, slot, place.first(t, k))
                src = buf.at[t, s]
                self.two[r, k] = Message(src, src, buf.at[t, lax.rem(s + RING - k, RING)], sems, slot + 1, place.second(t, k))
                slot += 2

    def begin(self):
        self.z.start()
        for k in (1, 3, 2):
            self.one[0, k].start()

    def other(self):
        self.z.arrived()
        for k in (1, 3, 2):
            self.one[1, k].start()

    def spread(self, r):
        for k in (1, 3, 2):
            self.one[r, k].arrived()
        for k in (1, 3, 2):
            self.two[r, k].start()

    def last(self):
        for message in self.two.values():
            message.arrived()

    def finish(self):
        for message in (self.z, *self.one.values(), *self.two.values()):
            message.sent()


class Total:
    def __init__(self, place, rows, part, half_out, half_in, mid, mid_out, mid_in, low, low_out, low_in, zed, done, sems, base):
        self.place, self.rows, self.part = place, rows, part
        self.half_out, self.half_in, self.mid, self.mid_out, self.mid_in = half_out, half_in, mid, mid_out, mid_in
        self.low, self.low_out, self.low_in, self.zed, self.done = low, low_out, low_in, zed, done
        n2, n8, n32 = rows // 2, rows // 8, rows // 32
        self.n2, self.n8, self.n32 = n2, n8, n32
        c = place.c
        t = c
        v, u = place.coords(t)
        self.u, self.v = u, v
        self.z = place.d * 2 + place.zl
        sib = place.at(c=1 - c)
        slot = base
        self.core = Message(half_out, half_out_dst(half_in), half_in, sems, slot, sib)
        slot += 1
        self.by_u, self.by_v, self.by_z, self.back_v, self.back_u = {}, {}, {}, {}, {}
        for i, k in enumerate((1, 3, 2)):
            self.by_u[k] = Message(mid_out.at[i], mid_in.at[i], mid_in.at[i], sems, slot, place.first(t, k))
            self.by_v[k] = Message(low_out.at[i], low_in.at[i], low_in.at[i], sems, slot + 1, place.second(t, k))
            zt = lax.rem(self.z + k, 4)
            zs = lax.rem(self.z + 4 - k, 4)
            self.by_z[k] = Message(
                zed.at[self.z], zed.at[self.z], zed.at[zs], sems, slot + 2, place.at(d=zt // 2, z=lax.rem(zt, 2))
            )
            mine = done.at[self.span(c, u, v)]
            self.back_v[k] = Message(
                mine, mine, done.at[self.span(c, u, lax.rem(v + 4 - k, 4))], sems, slot + 3, place.second(t, k)
            )
            mine = done.at[self.span(c, u)]
            self.back_u[k] = Message(
                mine, mine, done.at[self.span(c, lax.rem(u + 4 - k, 4))], sems, slot + 4, place.first(t, k)
            )
            slot += 5
        mine = done.at[self.span(c)]
        self.back_c = Message(mine, mine, done.at[self.span(1 - c)], sems, slot, sib)

    def span(self, c, u=None, v=None):
        if u is None:
            return pl.ds(pl.multiple_of(c * self.n2, 16), self.n2)
        if v is None:
            return pl.ds(pl.multiple_of(c * self.n2 + u * self.n8, 16), self.n8)
        return pl.ds(pl.multiple_of(c * self.n2 + u * self.n8 + v * self.n32, 16), self.n32)

    def begin(self):
        self.half_out[...] = self.part[self.span(1 - self.place.c)].astype(BF16)
        self.core.start()

    def step_u(self):
        self.core.arrived()
        self.mid[...] = self.part[self.span(self.place.c)] + self.half_in[...].astype(F32)
        for i, k in enumerate((1, 3, 2)):
            start = pl.multiple_of(lax.rem(self.u + k, 4) * self.n8, 16)
            self.mid_out[i] = self.mid[pl.ds(start, self.n8)].astype(BF16)
            self.by_u[k].start()

    def step_v(self):
        for k in (1, 3, 2):
            self.by_u[k].arrived()
        start = pl.multiple_of(self.u * self.n8, 16)
        self.low[...] = self.mid[pl.ds(start, self.n8)] + (
            (self.mid_in[0].astype(F32) + self.mid_in[1].astype(F32)) + self.mid_in[2].astype(F32)
        )
        for i, k in enumerate((1, 3, 2)):
            start = pl.multiple_of(lax.rem(self.v + k, 4) * self.n32, 16)
            self.low_out[i] = self.low[pl.ds(start, self.n32)].astype(BF16)
            self.by_v[k].start()

    def step_z(self):
        for k in (1, 3, 2):
            self.by_v[k].arrived()
        start = pl.multiple_of(self.v * self.n32, 16)
        total = self.low[pl.ds(start, self.n32)] + (
            (self.low_in[0].astype(F32) + self.low_in[1].astype(F32)) + self.low_in[2].astype(F32)
        )
        self.zed[self.z] = total.astype(BF16)
        for k in (1, 3, 2):
            self.by_z[k].start()

    def return_v(self):
        for k in (1, 3, 2):
            self.by_z[k].arrived()
        total = (self.zed[0].astype(F32) + self.zed[1].astype(F32)) + (self.zed[2].astype(F32) + self.zed[3].astype(F32))
        self.done[self.span(self.place.c, self.u, self.v)] = total.astype(BF16)
        for k in (1, 3, 2):
            self.back_v[k].start()

    def return_u(self):
        for k in (1, 3, 2):
            self.back_v[k].arrived()
        for k in (1, 3, 2):
            self.back_u[k].start()

    def return_c(self):
        for k in (1, 3, 2):
            self.back_u[k].arrived()
        self.back_c.start()

    def last(self):
        self.back_c.arrived()

    def finish(self):
        self.core.sent()
        for group in (self.by_u, self.by_v, self.by_z, self.back_v, self.back_u):
            for message in group.values():
                message.sent()
        self.back_c.sent()


def half_out_dst(half_in):
    return half_in


def total_scratch(rows):
    return [
        pltpu.VMEM((rows, 128), F32),
        pltpu.VMEM((rows // 2, 128), BF16),
        pltpu.VMEM((rows // 2, 128), BF16),
        pltpu.VMEM((rows // 2, 128), F32),
        pltpu.VMEM((3, rows // 8, 128), BF16),
        pltpu.VMEM((3, rows // 8, 128), BF16),
        pltpu.VMEM((rows // 8, 128), F32),
        pltpu.VMEM((3, rows // 32, 128), BF16),
        pltpu.VMEM((3, rows // 32, 128), BF16),
        pltpu.VMEM((4, rows // 32, 128), BF16),
        pltpu.VMEM((rows, 128), BF16),
    ]


def head_mask(shape, h):
    lane = lax.broadcasted_iota(jnp.int32, shape, len(shape) - 1)
    return jnp.logical_and(lane >= h * HDIM, lane < (h + 1) * HDIM)


def stack_heads(ref, half, rows):
    for h in range(HEADS):
        start = (half * HEADS + h) * ROW
        ref[start : start + ROW] = jnp.where(head_mask(rows.shape, h), rows, jnp.zeros_like(rows))


def unstack_heads(ref, half):
    out = jnp.zeros((ROW, CH), F32)
    for h in range(HEADS):
        start = (half * HEADS + h) * ROW
        out = jnp.where(head_mask((ROW, CH), h), ref[start : start + ROW], out)
    return out


def moved(rows, step):
    n = rows.shape[0]
    index = lax.broadcasted_iota(jnp.int32, rows.shape, 0)
    if step == 1:
        return jnp.where(index == n - 1, 0.0, pltpu.roll(rows, n - 1, 0))
    return jnp.where(index == 0, 0.0, pltpu.roll(rows, 1, 0))


def kernel(
    feat, wqkv, wout, wconv, go,
    gf, gqkv, gout, gconv,
    feats, grads, stats, sib_feat, sib_grad, fine, rim,
    keys, values, qm, dm,
    scores, gweights, low_w, low_g, acc_a, acc_b,
    run_m, run_l, run_d, tri_out, tri_in,
    part_out, part_in, pair_out, pair_in, ghid, glow, gproj, hid,
    *rest,
):
    rest_total, qkv_total, (send, recv) = rest[:11], rest[11:22], rest[22:]
    sems = (send, recv)
    place = Place()
    c, s, zl = place.c, place.s, place.zl
    sib = place.at(c=1 - c)
    above, below = place.line(-1), place.line(1)

    base = 0
    fg = Gather(place, feats, sems, base)
    base += AG_MSGS
    dg = Gather(place, grads, sems, base)
    base += AG_MSGS
    sg = StatGather(place, stats, sems, base)
    base += ST_MSGS
    rest_sum = Total(place, REST_ROWS, *rest_total, sems, base)
    base += RS_MSGS
    qkv_sum = Total(place, QKV_ROWS, *qkv_total, sems, base)
    base += RS_MSGS
    sib_f = Message(feat, sib_feat, sib_feat, sems, base, sib)
    down_fine = Message(fine.at[2], fine.at[0], fine.at[0], sems, base + 1, below)
    up_fine = Message(fine.at[1], fine.at[3], fine.at[3], sems, base + 2, above)
    s0, f0 = place.coords(zl)
    own = (zl, s0, f0)
    sib_g = Message(grads.at[own], sib_grad, sib_grad, sems, base + 3, sib)
    tri = Message(tri_out, tri_in, tri_in, sems, base + 4, sib)
    parts = Message(part_out, part_in, part_in, sems, base + 5, sib)
    down_hid = Message(hid, rim.at[0], rim.at[0], sems, base + 6, below)
    up_hid = Message(hid, rim.at[1], rim.at[1], sems, base + 7, above)
    pairs = Message(pair_out, pair_in, pair_in, sems, base + 8, sib)

    barrier = pltpu.get_barrier_semaphore()
    peers = [sib, place.at(z=place.zo), above, below]
    peers += [place.ring_x(k) for k in (1, 2, 3)] + [place.ring_y(k) for k in (1, 2, 3)]
    peers += [place.at(d=1 - place.d), place.at(d=1 - place.d, z=place.zo)]
    for peer in peers:
        pl.semaphore_signal(barrier, inc=1, device_id=peer, device_id_type=MESH)
    pl.semaphore_wait(barrier, len(peers))

    feats[own] = feat[...]
    fine[1] = go[0]
    fine[2] = go[1]
    down_fine.start()
    up_fine.start()
    fg.begin()
    sib_f.start()

    down_fine.arrived()
    up_fine.arrived()
    rows = fine[...]
    top = jnp.where(s > 0, rows[0], jnp.zeros_like(rows[0]))
    bottom = jnp.where(s < 63, rows[3], jnp.zeros_like(rows[3]))
    lines = [top, rows[1], rows[2], bottom]
    main = jnp.zeros((2 * ROW, CH), F32)
    plus = jnp.zeros((2 * ROW, CH), F32)
    minus = jnp.zeros((2 * ROW, CH), F32)
    for a in range(3):
        both = jnp.concatenate([lines[2 - a], lines[3 - a]], axis=0)
        w0, w1, w2 = wconv[3 * a], wconv[3 * a + 1], wconv[3 * a + 2]
        main = main + nt(both, jnp.concatenate([w1, w0], axis=1)) + nt(both, jnp.concatenate([w2, w1], axis=1))
        plus = plus + nt(both[:, :CO], w0)
        minus = minus + nt(both[:, CO:], w2)
    main, plus, minus = (m[:ROW] + m[ROW:] for m in (main, plus, minus))
    hidden_grad = main + moved(plus, 1) + moved(minus, -1)
    ghid[...] = hidden_grad
    hidden_low = hidden_grad.astype(BF16)
    glow[...] = hidden_low
    own_grad = nt(hidden_low, wout[...]).astype(BF16)
    grads[own] = own_grad
    sib_g.start()
    fg.other()
    fg.near(0)
    fg.pass_on(0, 0)
    dg.begin()

    def scaled_queries(rows):
        whole = nn(rows, wqkv[:, :CH]).astype(BF16)
        return (whole.astype(F32) * (1.0 / math.sqrt(HDIM))).astype(BF16)

    def stack_keys(rows, half):
        whole = nn(rows, wqkv[:, CH:]).astype(BF16)
        stack_heads(qm, half, whole[:, :CH])
        stack_heads(dm, half, whole[:, CH:])

    stack_heads(qm, 0, scaled_queries(feat[...]))
    stack_heads(dm, 0, own_grad)
    fg.near(1)
    fg.pass_on(1, 0)
    sib_f.arrived()
    stack_heads(qm, 1, scaled_queries(sib_feat[...]))
    sib_g.arrived()
    stack_heads(dm, 1, sib_grad[...])

    run_m[...] = jnp.full((STACK, 128), -1e30, F32)
    run_l[...] = jnp.zeros((STACK, 128), F32)
    run_d[...] = jnp.zeros((STACK, 128), F32)

    def where_is(j):
        role, order = lax.rem(j, 2), j // 2
        t = jnp.where(role == 0, zl, place.zo)
        offset = jnp.where(order == 0, 0, jnp.where(order == 1, 3, jnp.where(order == 2, 1, 2)))
        second, _ = place.coords(t)
        return t, lax.rem(second + offset, RING)

    def at_step(j, steps):
        for when, act in steps.items():
            pl.when(j == when)(act)

    def stat_steps():
        def first(j, unused):
            def act0():
                fg.far(0)

            def act1():
                fg.far(1)

            def act2():
                fg.pass_on(0, 1, 2, 3)
                dg.other()

            def act3():
                fg.pass_on(1, 1, 2, 3)
                dg.near(0)
                dg.pass_on(0, 0)

            def act4():
                dg.near(1)
                dg.pass_on(1, 0)

            def act6():
                fg.last(0)
                dg.far(0)

            def act7():
                fg.last(1)
                dg.far(1)

            at_step(j, {0: act0, 1: act1, 2: act2, 3: act3, 4: act4, 6: act6, 7: act7})
            t, second = where_is(j)
            block = feats[t, second].reshape(CHUNK, CH)
            whole = nn(block, wqkv[:, CH:]).astype(BF16)
            keys[j] = whole[:, :CH]
            values[j] = whole[:, CH:]
            scores[j] = nt(qm[...], keys[j])
            gweights[j] = nt(dm[...], values[j])

            def tile(i, unused):
                span = pl.ds(pl.multiple_of(i * SUB, SUB), SUB)
                cut = [pl.ds(b * 128, 128) for b in range(RING)]
                sc = [scores[j, span, k] for k in cut]
                old = run_m[span]
                new = jnp.maximum(jnp.maximum(jnp.maximum(sc[0], sc[1]), jnp.maximum(sc[2], sc[3])), old)
                shrink = jnp.exp(old - new)
                total, dot = run_l[span] * shrink, run_d[span] * shrink
                for k in range(RING):
                    w = jnp.exp(sc[k] - new)
                    total = total + w
                    dot = dot + w * gweights[j, span, cut[k]]
                run_m[span] = new
                run_l[span] = total
                run_d[span] = dot
                return unused

            lax.fori_loop(0, STACK // SUB, tile, 0, unroll=4)
            return unused

        lax.fori_loop(0, CHUNKS, first, 0)

    stat_steps()

    lane = lax.broadcasted_iota(jnp.int32, (ROW, 128), 1)
    mine = [jnp.zeros((ROW, 128), F32), jnp.ones((ROW, 128), F32), jnp.zeros((ROW, 128), F32)]
    theirs = list(mine)
    for half in (0, 1):
        for h in range(HEADS):
            g = half * HEADS + h
            span = slice(g * ROW, (g + 1) * ROW)
            m = run_m[span]
            top = jnp.max(m, axis=1, keepdims=True)
            e = jnp.exp(m - top)
            cols = [
                top,
                jnp.sum(run_l[span] * e, axis=1, keepdims=True),
                jnp.sum(run_d[span] * e, axis=1, keepdims=True),
            ]
            for k in range(3):
                mine[k] = jnp.where(lane == g, cols[k], mine[k])
                theirs[k] = jnp.where(lane == (1 - half) * HEADS + h, cols[k], theirs[k])
    for k in range(3):
        tri_out[k] = theirs[k]
    tri.start()
    tri.arrived()
    top = jnp.maximum(mine[0], tri_in[0])
    ea, eb = jnp.exp(mine[0] - top), jnp.exp(tri_in[0] - top)
    total = mine[1] * ea + tri_in[1] * eb
    delta = (mine[2] * ea + tri_in[2] * eb) / total
    lse = top + jnp.log(total)
    stats[own] = jnp.concatenate([jnp.transpose(lse)[:HEADS], jnp.transpose(delta)[:HEADS]], axis=0)
    sg.begin()
    for g in range(2 * HEADS):
        span = slice(g * ROW, (g + 1) * ROW)
        run_m[span] = jnp.broadcast_to(lse[:, g : g + 1], (ROW, 128))
        run_l[span] = jnp.broadcast_to(delta[:, g : g + 1], (ROW, 128))

    acc_a[...] = jnp.zeros((STACK, CH), F32)
    acc_b[...] = jnp.zeros((STACK, CH), F32)

    def forward(j, unused):
        def act0():
            sg.other()
            dg.pass_on(0, 1, 2)

        def act1():
            dg.pass_on(1, 1, 2)
            sg.spread(0)

        def act2():
            dg.pass_on(0, 3)
            sg.spread(1)

        def act3():
            dg.pass_on(1, 3)

        at_step(j, {0: act0, 1: act1, 2: act2, 3: act3})

        for half in (0, 1):

            def tile(i, unused, half=half):
                own_span = pl.ds(pl.multiple_of(i * SUB, SUB), SUB)
                span = pl.ds(pl.multiple_of(half * HALF + i * SUB, SUB), SUB)
                lse_t, delta_t = run_m[span], run_l[span]
                for b in range(RING):
                    cut = pl.ds(b * 128, 128)
                    w = jnp.exp(scores[j, span, cut] - lse_t)
                    low_w[own_span, cut] = w.astype(BF16)
                    low_g[own_span, cut] = (w * (gweights[j, span, cut] - delta_t)).astype(BF16)
                return unused

            lax.fori_loop(0, HALF // SUB, tile, 0, unroll=4)
            into = slice(half * HALF, (half + 1) * HALF)
            acc_a[into] += nn(low_w[...], values[j])
            acc_b[into] += nn(low_g[...], keys[j])
        return unused

    lax.fori_loop(0, CHUNKS, forward, 0)
    part_out[0] = unstack_heads(acc_a, 1)
    part_out[1] = unstack_heads(acc_b, 1)
    parts.start()
    attended_mine = unstack_heads(acc_a, 0)
    gq_mine = unstack_heads(acc_b, 0)
    parts.arrived()
    attended = (attended_mine + part_in[0]).astype(BF16)
    gproj[:, :CH] = ((gq_mine + part_in[1]) * (1.0 / math.sqrt(HDIM))).astype(BF16)
    hid[...] = (feat[...].astype(F32) + nn(attended, wout[...])).astype(BF16)
    down_hid.start()
    up_hid.start()
    out_part = tn(attended, glow[...])
    rest_sum.part[2304:2560] = out_part[:, :128]
    rest_sum.part[2560:2816] = out_part[:, 128:]
    rest_sum.part[2816:] = jnp.zeros((REST_ROWS - 2816, 128), F32)

    down_hid.arrived()
    up_hid.arrived()
    mid = hid[...]
    over = jnp.where(s > 0, rim[0], jnp.zeros_like(mid))
    under = jnp.where(s < 63, rim[1], jnp.zeros_like(mid))
    sides = []
    for r in (0, 1):
        wide = go[r].astype(F32)
        even, odd = wide[:, :CO], wide[:, CO:]
        sides.append(jnp.concatenate([even, odd, moved(even, 1), moved(odd, -1)], axis=1).astype(BF16))
    products = {
        (0, 0): tn(mid, sides[0]),
        (0, 1): tn(mid, sides[1]),
        (-1, 0): tn(over, sides[0]),
        (1, 1): tn(under, sides[1]),
    }
    for a, whole in enumerate(
        (
            products[-1, 0] + products[0, 1],
            products[0, 0] + products[0, 1],
            products[0, 0] + products[1, 1],
        )
    ):
        even, odd, even1, odd1 = (whole[:, k * CO : (k + 1) * CO] for k in range(4))
        rest_sum.part[(3 * a) * CH : (3 * a + 1) * CH] = even1 + odd
        rest_sum.part[(3 * a + 1) * CH : (3 * a + 2) * CH] = even + odd
        rest_sum.part[(3 * a + 2) * CH : (3 * a + 3) * CH] = even + odd1
    rest_sum.begin()

    stack_keys(feat[...], 0)
    stack_keys(sib_feat[...], 1)
    dg.last(0)
    dg.last(1)
    sg.last()
    acc_a[...] = jnp.zeros((STACK, CH), F32)
    acc_b[...] = jnp.zeros((STACK, CH), F32)

    def backward(j, unused):
        at_step(
            j,
            {
                1: rest_sum.step_u,
                2: rest_sum.step_v,
                3: rest_sum.step_z,
                4: rest_sum.return_v,
                5: rest_sum.return_u,
                6: rest_sum.return_c,
            },
        )
        t, second = where_is(j)
        block = grads[t, second].reshape(CHUNK, CH)
        asked = scaled_queries(feats[t, second].reshape(CHUNK, CH))
        scores[0] = nt(qm[...], asked)
        gweights[0] = nt(dm[...], block)
        for half in (0, 1):
            for h in range(HEADS):

                def tile(i, unused, h=h, half=half):
                    own_span = pl.ds(pl.multiple_of(h * ROW + i * SUB, SUB), SUB)
                    span = pl.ds(pl.multiple_of((half * HEADS + h) * ROW + i * SUB, SUB), SUB)
                    for b in range(RING):
                        cut = pl.ds(b * 128, 128)
                        w = jnp.exp(scores[0, span, cut] - stats[t, second, b, h : h + 1, :])
                        low_w[own_span, cut] = w.astype(BF16)
                        low_g[own_span, cut] = (
                            w * (gweights[0, span, cut] - stats[t, second, b, HEADS + h : HEADS + h + 1, :])
                        ).astype(BF16)
                    return unused

                lax.fori_loop(0, ROW // SUB, tile, 0, unroll=4)
            into = slice(half * HALF, (half + 1) * HALF)
            acc_a[into] += nn(low_g[...], asked)
            acc_b[into] += nn(low_w[...], block)
        return unused

    lax.fori_loop(0, CHUNKS, backward, 0)
    pair_out[:, :CH] = unstack_heads(acc_a, 1)
    pair_out[:, CH:] = unstack_heads(acc_b, 1)
    pairs.start()
    gk_mine = unstack_heads(acc_a, 0)
    gv_mine = unstack_heads(acc_b, 0)
    pairs.arrived()
    gproj[:, CH : 2 * CH] = (gk_mine + pair_in[:, :CH]).astype(BF16)
    gproj[:, 2 * CH :] = (gv_mine + pair_in[:, CH:]).astype(BF16)
    proj = gproj[...]
    qkv_part = tn(feat[...], proj)
    for k in range(6):
        qkv_sum.part[k * CH : (k + 1) * CH] = qkv_part[:, k * 128 : (k + 1) * 128]
    qkv_sum.begin()
    gf[...] = ghid[...] + nt(proj, wqkv[...])
    coarse = 1.0 / math.sqrt(2 * 64 * ROW)
    fine_scale = 1.0 / math.sqrt(2 * 128 * 256)
    qkv_sum.step_u()
    rest_sum.last()
    gconv[...] = rest_sum.done[:2304].astype(F32) * fine_scale
    gout[:, :128] = rest_sum.done[2304:2560].astype(F32) * coarse
    gout[:, 128:] = rest_sum.done[2560:2816].astype(F32) * coarse
    qkv_sum.step_v()
    qkv_sum.step_z()
    qkv_sum.return_v()
    qkv_sum.return_u()
    qkv_sum.return_c()
    qkv_sum.last()
    for k in range(6):
        gqkv[:, k * 128 : (k + 1) * 128] = qkv_sum.done[k * CH : (k + 1) * CH].astype(F32) * coarse

    for group in (fg, dg, sg, rest_sum, qkv_sum):
        group.finish()
    for message in (sib_f, down_fine, up_fine, sib_g, tri, parts, down_hid, up_hid, pairs):
        message.sent()


def shards(features, qkv_weight, out_weight, conv_weight, grad_output):
    messages = 2 * AG_MSGS + ST_MSGS + 2 * RS_MSGS + 9
    whole = pl.BlockSpec(memory_space=pltpu.VMEM)
    gf, gqkv, gout, gconv = pl.pallas_call(
        kernel,
        out_shape=[
            jax.ShapeDtypeStruct((ROW, CH), F32),
            jax.ShapeDtypeStruct((CH, 3 * CH), F32),
            jax.ShapeDtypeStruct((CH, CH), F32),
            jax.ShapeDtypeStruct((9 * CH, CO), F32),
        ],
        in_specs=[whole] * 5,
        out_specs=[whole] * 4,
        scratch_shapes=[
            pltpu.VMEM((2, RING, RING, ROW, CH), BF16),
            pltpu.VMEM((2, RING, RING, ROW, CH), BF16),
            pltpu.VMEM((2, RING, RING, 2 * HEADS, ROW), F32),
            pltpu.VMEM((ROW, CH), BF16),
            pltpu.VMEM((ROW, CH), BF16),
            pltpu.VMEM((4, ROW, 2 * CO), BF16),
            pltpu.VMEM((2, ROW, CH), BF16),
            pltpu.VMEM((CHUNKS, CHUNK, CH), BF16),
            pltpu.VMEM((CHUNKS, CHUNK, CH), BF16),
            pltpu.VMEM((STACK, CH), BF16),
            pltpu.VMEM((STACK, CH), BF16),
            pltpu.VMEM((CHUNKS, STACK, CHUNK), F32),
            pltpu.VMEM((CHUNKS, STACK, CHUNK), F32),
            pltpu.VMEM((HALF, CHUNK), BF16),
            pltpu.VMEM((HALF, CHUNK), BF16),
            pltpu.VMEM((STACK, CH), F32),
            pltpu.VMEM((STACK, CH), F32),
            pltpu.VMEM((STACK, 128), F32),
            pltpu.VMEM((STACK, 128), F32),
            pltpu.VMEM((STACK, 128), F32),
            pltpu.VMEM((3, ROW, 128), F32),
            pltpu.VMEM((3, ROW, 128), F32),
            pltpu.VMEM((2, ROW, CH), F32),
            pltpu.VMEM((2, ROW, CH), F32),
            pltpu.VMEM((ROW, 2 * CH), F32),
            pltpu.VMEM((ROW, 2 * CH), F32),
            pltpu.VMEM((ROW, CH), F32),
            pltpu.VMEM((ROW, CH), BF16),
            pltpu.VMEM((ROW, 3 * CH), BF16),
            pltpu.VMEM((ROW, CH), BF16),
            *total_scratch(REST_ROWS),
            *total_scratch(QKV_ROWS),
            pltpu.SemaphoreType.DMA((messages,)),
            pltpu.SemaphoreType.DMA((messages,)),
        ],
        compiler_params=pltpu.CompilerParams(
            collective_id=0, has_side_effects=True, vmem_limit_bytes=63 * 1024 * 1024
        ),
    )(
        features.reshape(ROW, CH),
        qkv_weight,
        out_weight,
        conv_weight.reshape(9, CH, CO),
        grad_output.reshape(2, ROW, 2 * CO),
    )
    return (
        gf.reshape(1, 1, ROW, CH),
        gqkv,
        gout,
        gconv.reshape(3, 3, CH, CO),
    )


def solution(mesh):
    in_specs = (P("dp", "space", None, None), P(), P(), P(), P("dp", "space", None, None))
    out_specs = (P("dp", "space", None, None), P(), P(), P())
    return jax.shard_map(shards, mesh=mesh, in_specs=in_specs, out_specs=out_specs, check_vma=False)
```

```python
import math

import jax
import jax.numpy as jnp
from jax import lax
from jax.experimental import pallas as pl
from jax.experimental.pallas import tpu as pltpu
from jax.sharding import PartitionSpec as P

MESH = pl.DeviceIdType.MESH
F32 = jnp.float32
BF16 = jnp.bfloat16
HDIM = 64
HEADS = 4
CH = 256
CO = 128
ROW = 128
RING = 4
CHUNK = RING * ROW
CHUNKS = 8
STACK = 2 * HEADS * ROW
HALF = STACK // 2
SUB = 32
REST_ROWS = 3584
QKV_ROWS = 1024
PLANE = [(k % 4, k // 4) for k in range(1, 16)]
AG_MSGS = 41
ST_MSGS = 31
RS_MSGS = 35


def nt(a, b):
    return lax.dot_general(a, b, (((1,), (1,)), ((), ())), preferred_element_type=F32)


def tn(a, b):
    return lax.dot_general(a, b, (((0,), (0,)), ((), ())), preferred_element_type=F32)


def nn(a, b):
    return jnp.dot(a, b, preferred_element_type=F32)


class Message:
    def __init__(self, src, dst, landing, sems, slot, device):
        send, recv = sems
        self.out = pltpu.make_async_remote_copy(
            src_ref=src, dst_ref=dst, send_sem=send.at[slot], recv_sem=recv.at[slot], device_id=device, device_id_type=MESH
        )
        self.into = pltpu.make_async_remote_copy(
            src_ref=landing, dst_ref=landing, send_sem=send.at[slot], recv_sem=recv.at[slot], device_id=device, device_id_type=MESH
        )

    def start(self):
        self.out.start()

    def arrived(self):
        self.into.wait_recv()

    def sent(self):
        self.out.wait_send()


class Place:
    def __init__(self):
        self.d = lax.axis_index("dp")
        self.s = lax.axis_index("space")
        s = self.s
        self.c = lax.rem(s, 2)
        self.x = lax.rem(s // 2, RING)
        self.zl = lax.rem(s // 8, 2)
        self.y = s // 16
        self.zo = 1 - self.zl

    def at(self, d=None, y=None, z=None, x=None, c=None):
        d = self.d if d is None else d
        y = self.y if y is None else y
        z = self.zl if z is None else z
        x = self.x if x is None else x
        c = self.c if c is None else c
        return (d, ((y * 2 + z) * RING + x) * 2 + c)

    def line(self, step):
        return (self.d, lax.rem(self.s + step + 64, 64))

    def ring_x(self, step):
        return self.at(x=lax.rem(self.x + step + RING, RING))

    def ring_y(self, step):
        return self.at(y=lax.rem(self.y + step + RING, RING))

    def plane(self, dx, dy, z=None):
        return self.at(x=lax.rem(self.x + dx + RING, RING), y=lax.rem(self.y + dy + RING, RING), z=z)

    def back(self, t, dx, dy):
        x, y = lax.rem(self.x + RING - dx, RING), lax.rem(self.y + RING - dy, RING)
        return t, jnp.where(t == 0, y, x), jnp.where(t == 0, x, y)

    def first(self, t, step):
        hit = t == 0
        return self.at(
            x=jnp.where(hit, lax.rem(self.x + step + RING, RING), self.x),
            y=jnp.where(hit, self.y, lax.rem(self.y + step + RING, RING)),
        )

    def second(self, t, step):
        return self.first(1 - t, step)

    def coords(self, t):
        return jnp.where(t == 0, self.y, self.x), jnp.where(t == 0, self.x, self.y)


class Gather:
    def __init__(self, place, buf, sems, base, direct):
        self.place, self.buf, self.sems, self.count, self.base = place, buf, sems, 0, base
        self.direct = direct
        half = ROW // 2
        low, high = pl.ds(0, half), pl.ds(half, half)
        s0, f0 = place.coords(place.zl)
        s1, f1 = place.coords(place.zo)
        m = {"z": self.make((place.zl, s0, f0), (place.zo, s1, f1), place.at(z=place.zo))}
        for r in (0, 1):
            t = place.zl if r == 0 else place.zo
            s, f = (s0, f0) if r == 0 else (s1, f1)
            sm, sp, s2 = (lax.rem(s + k, RING) for k in (3, 1, 2))
            fm, fp, f2 = (lax.rem(f + k, RING) for k in (3, 1, 2))
            up, down = place.first(t, 1), place.first(t, -1)
            m[r, "1+"] = self.make((t, s, f), (t, s, fm), up)
            m[r, "1-"] = self.make((t, s, f), (t, s, fp), down)
            if direct:
                m[r, "12"] = self.make((t, s, f), (t, s, f2), place.first(t, 2))
            else:
                m[r, "1f+"] = self.make((t, s, fm, low), (t, s, f2, low), up)
                m[r, "1f-"] = self.make((t, s, fp, high), (t, s, f2, high), down)
            up, down = place.second(t, 1), place.second(t, -1)
            for q, g in enumerate((f, fm, fp, f2)):
                m[r, q, "2+"] = self.make((t, s, g), (t, sm, g), up)
                m[r, q, "2-"] = self.make((t, s, g), (t, sp, g), down)
                m[r, q, "2f+"] = self.make((t, sm, g, low), (t, s2, g, low), up)
                m[r, q, "2f-"] = self.make((t, sp, g, high), (t, s2, g, high), down)
        self.m = m

    def make(self, src, landing, device):
        slot = self.base + self.count
        self.count += 1
        src = self.buf.at[src]
        return Message(src, src, self.buf.at[landing], self.sems, slot, device)

    def go(self, *keys):
        for key in keys:
            self.m[key].start()

    def ring(self, r):
        self.go((r, "1+"), (r, "1-"), *([(r, "12")] if self.direct else []), (r, 0, "2+"), (r, 0, "2-"))

    def begin(self):
        self.go("z")
        self.ring(0)

    def other(self):
        self.m["z"].arrived()
        self.ring(1)

    def near(self, r):
        self.m[r, "1+"].arrived()
        self.go(*([] if self.direct else [(r, "1f+")]), (r, 1, "2+"), (r, 1, "2-"))
        self.m[r, "1-"].arrived()
        self.go(*([] if self.direct else [(r, "1f-")]), (r, 2, "2+"), (r, 2, "2-"))

    def pass_on(self, r, *blocks):
        for q in blocks:
            self.m[r, q, "2+"].arrived()
            self.go((r, q, "2f+"))
            self.m[r, q, "2-"].arrived()
            self.go((r, q, "2f-"))

    def far(self, r):
        if self.direct:
            self.m[r, "12"].arrived()
        else:
            self.m[r, "1f+"].arrived()
            self.m[r, "1f-"].arrived()
        self.go((r, 3, "2+"), (r, 3, "2-"))

    def last(self, r):
        for q in range(4):
            self.m[r, q, "2f+"].arrived()
            self.m[r, q, "2f-"].arrived()

    def finish(self):
        for message in self.m.values():
            message.sent()


class StatGather:
    def __init__(self, place, buf, sems, base):
        s0, f0 = place.coords(place.zl)
        s1, f1 = place.coords(place.zo)
        src = buf.at[place.zl, s0, f0]
        self.z = Message(src, src, buf.at[place.zo, s1, f1], sems, base, place.at(z=place.zo))
        self.wide = ([], [])
        slot = base + 1
        for r in (0, 1):
            t = place.zl if r == 0 else place.zo
            src = buf.at[place.back(t, 0, 0)]
            for dx, dy in PLANE:
                self.wide[r].append(Message(src, src, buf.at[place.back(t, dx, dy)], sems, slot, place.plane(dx, dy)))
                slot += 1

    def begin(self):
        self.z.start()
        for message in self.wide[0]:
            message.start()

    def other(self):
        self.z.arrived()
        for message in self.wide[1]:
            message.start()

    def last(self):
        for message in (*self.wide[0], *self.wide[1]):
            message.arrived()

    def finish(self):
        for message in (self.z, *self.wide[0], *self.wide[1]):
            message.sent()


class Total:
    def __init__(self, place, rows, part, half_in, mid_out, mid_in, zed, done, sems, base):
        self.place, self.part, self.half_in = place, part, half_in
        self.mid_out, self.mid_in, self.zed, self.done = mid_out, mid_in, zed, done
        self.half, self.piece = rows // 2, rows // 32
        c = place.c
        self.mine = place.y * RING + place.x
        self.z = place.d * 2 + place.zl
        sib = place.at(c=1 - c)
        away = part.at[self.span(1 - c)]
        self.core = Message(away, half_in, half_in, sems, base, sib)
        slot = base + 1
        self.out, self.by_z, self.back = [], [], []
        here = done.at[self.span(c, self.mine)]
        for k, (dx, dy) in enumerate(PLANE):
            x, y = lax.rem(place.x + dx, RING), lax.rem(place.y + dy, RING)
            src = mid_out.at[pl.ds(pl.multiple_of((y * RING + x) * self.piece, 16), self.piece)]
            self.out.append(Message(src, mid_in.at[k], mid_in.at[k], sems, slot, place.plane(dx, dy)))
            x, y = lax.rem(place.x + RING - dx, RING), lax.rem(place.y + RING - dy, RING)
            self.back.append(
                Message(here, here, done.at[self.span(c, y * RING + x)], sems, slot + 1, place.plane(dx, dy))
            )
            slot += 2
        for k in (1, 3, 2):
            to, of = lax.rem(self.z + k, 4), lax.rem(self.z + 4 - k, 4)
            src = zed.at[self.z]
            self.by_z.append(Message(src, src, zed.at[of], sems, slot, place.at(d=to // 2, z=lax.rem(to, 2))))
            slot += 1
        src = done.at[self.span(c)]
        self.across = Message(src, src, done.at[self.span(1 - c)], sems, slot, sib)

    def span(self, c, piece=None):
        if piece is None:
            return pl.ds(pl.multiple_of(c * self.half, 16), self.half)
        return pl.ds(pl.multiple_of(c * self.half + piece * self.piece, 16), self.piece)

    def begin(self):
        self.core.start()

    def scatter(self):
        self.core.arrived()
        mine = self.span(self.place.c)
        both = self.part[mine] + self.half_in[...]
        self.part[mine] = both
        self.mid_out[...] = both.astype(BF16)
        for message in self.out:
            message.start()

    def along_z(self):
        total = self.part[self.span(self.place.c, self.mine)]
        for k, message in enumerate(self.out):
            message.arrived()
            total = total + self.mid_in[k].astype(F32)
        self.zed[self.z] = total
        for message in self.by_z:
            message.start()

    def spread(self):
        for message in self.by_z:
            message.arrived()
        total = (self.zed[0] + self.zed[1]) + (self.zed[2] + self.zed[3])
        self.done[self.span(self.place.c, self.mine)] = total.astype(BF16)
        for message in self.back:
            message.start()

    def swap(self):
        for message in self.back:
            message.arrived()
        self.across.start()

    def last(self):
        self.across.arrived()

    def finish(self):
        for message in (self.core, *self.out, *self.by_z, *self.back, self.across):
            message.sent()


def total_scratch(rows):
    return [
        pltpu.VMEM((rows, 128), F32),
        pltpu.VMEM((rows // 2, 128), F32),
        pltpu.VMEM((rows // 2, 128), BF16),
        pltpu.VMEM((15, rows // 32, 128), BF16),
        pltpu.VMEM((4, rows // 32, 128), F32),
    ]


def head_mask(shape, h):
    lane = lax.broadcasted_iota(jnp.int32, shape, len(shape) - 1)
    return jnp.logical_and(lane >= h * HDIM, lane < (h + 1) * HDIM)


def stack_heads(ref, half, rows):
    for h in range(HEADS):
        start = (half * HEADS + h) * ROW
        ref[start : start + ROW] = jnp.where(head_mask(rows.shape, h), rows, jnp.zeros_like(rows))


def unstack_heads(ref, half):
    out = jnp.zeros((ROW, CH), F32)
    for h in range(HEADS):
        start = (half * HEADS + h) * ROW
        out = jnp.where(head_mask((ROW, CH), h), ref[start : start + ROW], out)
    return out


def moved(rows, step):
    n = rows.shape[0]
    index = lax.broadcasted_iota(jnp.int32, rows.shape, 0)
    if step == 1:
        return jnp.where(index == n - 1, 0.0, pltpu.roll(rows, n - 1, 0))
    return jnp.where(index == 0, 0.0, pltpu.roll(rows, 1, 0))


def kernel(
    feat, wqkv, wout, wconv, go,
    gf, rest_done, qkv_done,
    feats, grads, stats, sib_feat, sib_grad, fine, rim, sides,
    keys, values, qm, dm,
    scores, gweights, low_w, low_g, acc_a, acc_b,
    run_m, run_l, run_d, tri_out, tri_in,
    part_out, part_in, pair_out, pair_in, ghid, glow, gproj, hid,
    wide, *rest,
):
    rest_total, qkv_total, (send, recv) = (*rest[:5], rest_done), (*rest[5:10], qkv_done), rest[10:12]
    greet = rest[12]
    sems = (send, recv)
    place = Place()
    c, s, zl = place.c, place.s, place.zl
    sib = place.at(c=1 - c)
    above, below = place.line(-1), place.line(1)

    base = 0
    fg = Gather(place, feats, sems, base, True)
    base += AG_MSGS
    dg = Gather(place, grads, sems, base, False)
    base += AG_MSGS
    sg = StatGather(place, stats, sems, base)
    base += ST_MSGS
    rest_sum = Total(place, REST_ROWS, *rest_total, sems, base)
    base += RS_MSGS
    qkv_sum = Total(place, QKV_ROWS, *qkv_total, sems, base)
    base += RS_MSGS
    sib_f = Message(feat, sib_feat, sib_feat, sems, base, sib)
    down_fine = Message(go.at[1], fine.at[0], fine.at[0], sems, base + 1, below)
    up_fine = Message(go.at[0], fine.at[1], fine.at[1], sems, base + 2, above)
    s0, f0 = place.coords(zl)
    own = (zl, s0, f0)
    sib_g = Message(grads.at[own], sib_grad, sib_grad, sems, base + 3, sib)
    tri = Message(tri_out, tri_in, tri_in, sems, base + 4, sib)
    parts = Message(part_out, part_in, part_in, sems, base + 5, sib)
    down_hid = Message(hid, rim.at[0], rim.at[0], sems, base + 6, below)
    up_hid = Message(hid, rim.at[1], rim.at[1], sems, base + 7, above)
    pairs = Message(pair_out, pair_in, pair_in, sems, base + 8, sib)

    def scaled_queries(rows):
        whole = nn(rows, wqkv[:, :CH]).astype(BF16)
        return (whole.astype(F32) * (1.0 / math.sqrt(HDIM))).astype(BF16)

    def stack_keys(rows, half):
        whole = nn(rows, wqkv[:, CH:]).astype(BF16)
        stack_heads(qm, half, whole[:, :CH])
        stack_heads(dm, half, whole[:, CH:])

    barrier = pltpu.get_barrier_semaphore()
    peers = [sib, place.at(z=place.zo), above, below]
    peers += [place.ring_x(k) for k in (1, 2, 3)] + [place.ring_y(k) for k in (1, 2, 3)]
    next_z = place.at(d=1 - place.d, z=place.zo)
    peers.append(next_z)
    for peer in peers:
        pl.semaphore_signal(barrier, inc=1, device_id=peer, device_id_type=MESH)
    pl.semaphore_wait(barrier, len(peers))
    pl.semaphore_signal(greet, inc=1, device_id=next_z, device_id_type=MESH)

    feats[own] = feat[...]
    down_fine.start()
    up_fine.start()
    fg.begin()
    sib_f.start()

    def split(rows, shift=False):
        wide[...] = rows.astype(F32)
        return wide[pl.ds(0, ROW, stride=2)], wide[pl.ds(1, ROW, stride=2)]

    def pack(even, odd):
        return jnp.concatenate([even, odd], axis=1).astype(BF16)

    own_lines = []
    for r in (0, 1):
        even, odd = split(go[r])
        sides[r] = jnp.concatenate([even, odd, moved(even, 1), moved(odd, -1)], axis=1).astype(BF16)
        own_lines.append(pack(even, odd))
    stack_heads(qm, 0, scaled_queries(feat[...]))
    down_fine.arrived()
    up_fine.arrived()
    top, bottom = pack(*split(fine[0])), pack(*split(fine[1]))
    top = jnp.where(s > 0, top, jnp.zeros_like(top))
    bottom = jnp.where(s < 63, bottom, jnp.zeros_like(bottom))
    lines = [top, *own_lines, bottom]
    main = jnp.zeros((2 * ROW, CH), F32)
    plus = jnp.zeros((2 * ROW, CH), F32)
    minus = jnp.zeros((2 * ROW, CH), F32)
    for a in range(3):
        both = jnp.concatenate([lines[2 - a], lines[3 - a]], axis=0)
        w0, w1, w2 = wconv[3 * a], wconv[3 * a + 1], wconv[3 * a + 2]
        main = main + nt(both, jnp.concatenate([w1, w0], axis=1)) + nt(both, jnp.concatenate([w2, w1], axis=1))
        plus = plus + nt(both[:, :CO], w0)
        minus = minus + nt(both[:, CO:], w2)
    main, plus, minus = (m[:ROW] + m[ROW:] for m in (main, plus, minus))
    hidden_grad = main + moved(plus, 1) + moved(minus, -1)
    ghid[...] = hidden_grad
    hidden_low = hidden_grad.astype(BF16)
    glow[...] = hidden_low
    own_grad = nt(hidden_low, wout[...]).astype(BF16)
    grads[own] = own_grad
    sib_g.start()
    dg.begin()
    fg.other()
    fg.near(0)
    fg.far(0)
    fg.pass_on(0, 0)

    stack_heads(dm, 0, own_grad)
    sib_f.arrived()
    stack_heads(qm, 1, scaled_queries(sib_feat[...]))
    sib_g.arrived()
    stack_heads(dm, 1, sib_grad[...])

    run_m[...] = jnp.full((STACK, 128), -1e30, F32)
    run_l[...] = jnp.zeros((STACK, 128), F32)
    run_d[...] = jnp.zeros((STACK, 128), F32)

    def where_is(j):
        role = jnp.where((j == 1) | (j == 4) | (j == 5) | (j == 7), 1, 0)
        t = jnp.where(role == 0, zl, place.zo)
        offset = jnp.where(j < 2, 0, jnp.where(j > 5, 2, jnp.where(lax.rem(j, 2) == 0, 3, 1)))
        second, _ = place.coords(t)
        return t, lax.rem(second + offset, RING)

    def at_step(j, steps):
        for when, act in steps.items():
            pl.when(j == when)(act)

    def stat_steps():
        def first(j, unused):
            def act1():
                fg.near(1)
                fg.far(1)
                fg.pass_on(1, 0)

            def act2():
                fg.pass_on(0, 1, 2, 3)

            def act3():
                dg.other()
                dg.near(0)
                dg.pass_on(0, 0)

            def act4():
                fg.pass_on(1, 1, 2, 3)

            def act5():
                dg.near(1)
                dg.pass_on(1, 0)

            def act6():
                fg.last(0)
                dg.far(0)

            def act7():
                fg.last(1)
                dg.far(1)

            at_step(j, {1: act1, 2: act2, 3: act3, 4: act4, 5: act5, 6: act6, 7: act7})
            t, second = where_is(j)
            block = feats[t, second].reshape(CHUNK, CH)
            whole = nn(block, wqkv[:, CH:]).astype(BF16)
            keys[j] = whole[:, :CH]
            values[j] = whole[:, CH:]
            scores[j] = nt(qm[...], keys[j])
            gweights[j] = nt(dm[...], values[j])

            def tile(i, unused):
                span = pl.ds(pl.multiple_of(i * SUB, SUB), SUB)
                cut = [pl.ds(b * 128, 128) for b in range(RING)]
                sc = [scores[j, span, k] for k in cut]
                old = run_m[span]
                new = jnp.maximum(jnp.maximum(jnp.maximum(sc[0], sc[1]), jnp.maximum(sc[2], sc[3])), old)
                shrink = jnp.exp(old - new)
                total, dot = run_l[span] * shrink, run_d[span] * shrink
                for k in range(RING):
                    w = jnp.exp(sc[k] - new)
                    total = total + w
                    dot = dot + w * gweights[j, span, cut[k]]
                run_m[span] = new
                run_l[span] = total
                run_d[span] = dot
                return unused

            lax.fori_loop(0, STACK // SUB, tile, 0, unroll=4)
            return unused

        lax.fori_loop(0, CHUNKS, first, 0)

    stat_steps()

    lane = lax.broadcasted_iota(jnp.int32, (ROW, 128), 1)
    mine = [jnp.zeros((ROW, 128), F32), jnp.ones((ROW, 128), F32), jnp.zeros((ROW, 128), F32)]
    theirs = list(mine)
    for half in (0, 1):
        for h in range(HEADS):
            g = half * HEADS + h
            span = slice(g * ROW, (g + 1) * ROW)
            m = run_m[span]
            top = jnp.max(m, axis=1, keepdims=True)
            e = jnp.exp(m - top)
            cols = [
                top,
                jnp.sum(run_l[span] * e, axis=1, keepdims=True),
                jnp.sum(run_d[span] * e, axis=1, keepdims=True),
            ]
            for k in range(3):
                mine[k] = jnp.where(lane == g, cols[k], mine[k])
                theirs[k] = jnp.where(lane == (1 - half) * HEADS + h, cols[k], theirs[k])
    for k in range(3):
        tri_out[k] = theirs[k]
    tri.start()
    tri.arrived()
    top = jnp.maximum(mine[0], tri_in[0])
    ea, eb = jnp.exp(mine[0] - top), jnp.exp(tri_in[0] - top)
    total = mine[1] * ea + tri_in[1] * eb
    delta = (mine[2] * ea + tri_in[2] * eb) / total
    lse = top + jnp.log(total)
    stats[own] = jnp.concatenate([jnp.transpose(lse)[:HEADS], jnp.transpose(delta)[:HEADS]], axis=0)
    sg.begin()
    for g in range(2 * HEADS):
        span = slice(g * ROW, (g + 1) * ROW)
        run_m[span] = jnp.broadcast_to(lse[:, g : g + 1], (ROW, 128))
        run_l[span] = jnp.broadcast_to(delta[:, g : g + 1], (ROW, 128))

    acc_a[...] = jnp.zeros((STACK, CH), F32)
    acc_b[...] = jnp.zeros((STACK, CH), F32)

    def forward(j, unused):
        def act0():
            dg.pass_on(0, 1, 2)

        def act1():
            sg.other()

        def act2():
            dg.pass_on(1, 1, 2)

        def act3():
            dg.pass_on(0, 3)

        def act4():
            dg.pass_on(1, 3)

        at_step(j, {0: act0, 1: act1, 2: act2, 3: act3, 4: act4})

        for half in (0, 1):

            def tile(i, unused, half=half):
                own_span = pl.ds(pl.multiple_of(i * SUB, SUB), SUB)
                span = pl.ds(pl.multiple_of(half * HALF + i * SUB, SUB), SUB)
                lse_t, delta_t = run_m[span], run_l[span]
                for b in range(RING):
                    cut = pl.ds(b * 128, 128)
                    w = jnp.exp(scores[j, span, cut] - lse_t)
                    low_w[own_span, cut] = w.astype(BF16)
                    low_g[own_span, cut] = (w * (gweights[j, span, cut] - delta_t)).astype(BF16)
                return unused

            lax.fori_loop(0, HALF // SUB, tile, 0, unroll=4)
            into = slice(half * HALF, (half + 1) * HALF)
            acc_a[into] += nn(low_w[...], values[j])
            acc_b[into] += nn(low_g[...], keys[j])
        return unused

    lax.fori_loop(0, CHUNKS, forward, 0)
    part_out[0] = unstack_heads(acc_a, 1)
    part_out[1] = unstack_heads(acc_b, 1)
    parts.start()
    attended_mine = unstack_heads(acc_a, 0)
    gq_mine = unstack_heads(acc_b, 0)
    parts.arrived()
    attended = (attended_mine + part_in[0]).astype(BF16)
    gproj[:, :CH] = ((gq_mine + part_in[1]) * (1.0 / math.sqrt(HDIM))).astype(BF16)
    hid[...] = (feat[...].astype(F32) + nn(attended, wout[...])).astype(BF16)
    down_hid.start()
    up_hid.start()
    out_part = tn(attended, glow[...])
    rest_sum.part[2304:2560] = out_part[:, :128]
    rest_sum.part[2560:2816] = out_part[:, 128:]
    query_part = tn(feat[...], gproj[:, :CH])
    rest_sum.part[2816:3072] = query_part[:, :128]
    rest_sum.part[3072:3328] = query_part[:, 128:]
    rest_sum.part[3328:] = jnp.zeros((REST_ROWS - 3328, 128), F32)

    down_hid.arrived()
    up_hid.arrived()
    mid = hid[...]
    over = jnp.where(s > 0, rim[0], jnp.zeros_like(mid))
    under = jnp.where(s < 63, rim[1], jnp.zeros_like(mid))
    products = {
        (0, 0): tn(mid, sides[0]),
        (0, 1): tn(mid, sides[1]),
        (-1, 0): tn(over, sides[0]),
        (1, 1): tn(under, sides[1]),
    }
    for a, whole in enumerate(
        (
            products[-1, 0] + products[0, 1],
            products[0, 0] + products[0, 1],
            products[0, 0] + products[1, 1],
        )
    ):
        even, odd, even1, odd1 = (whole[:, k * CO : (k + 1) * CO] for k in range(4))
        rest_sum.part[(3 * a) * CH : (3 * a + 1) * CH] = even1 + odd
        rest_sum.part[(3 * a + 1) * CH : (3 * a + 2) * CH] = even + odd
        rest_sum.part[(3 * a + 2) * CH : (3 * a + 3) * CH] = even + odd1
    rest_sum.begin()

    stack_keys(feat[...], 0)
    stack_keys(sib_feat[...], 1)
    pl.semaphore_wait(greet, 1)
    dg.last(0)
    dg.last(1)
    sg.last()
    acc_a[...] = jnp.zeros((STACK, CH), F32)
    acc_b[...] = jnp.zeros((STACK, CH), F32)

    def backward(j, unused):
        at_step(
            j,
            {
                1: rest_sum.scatter,
                5: rest_sum.along_z,
            },
        )
        t, second = where_is(j)
        block = grads[t, second].reshape(CHUNK, CH)
        asked = scaled_queries(feats[t, second].reshape(CHUNK, CH))
        scores[0] = nt(qm[...], asked)
        gweights[0] = nt(dm[...], block)
        for half in (0, 1):
            for h in range(HEADS):

                def tile(i, unused, h=h, half=half):
                    own_span = pl.ds(pl.multiple_of(h * ROW + i * SUB, SUB), SUB)
                    span = pl.ds(pl.multiple_of((half * HEADS + h) * ROW + i * SUB, SUB), SUB)
                    for b in range(RING):
                        cut = pl.ds(b * 128, 128)
                        w = jnp.exp(scores[0, span, cut] - stats[t, second, b, h : h + 1, :])
                        low_w[own_span, cut] = w.astype(BF16)
                        low_g[own_span, cut] = (
                            w * (gweights[0, span, cut] - stats[t, second, b, HEADS + h : HEADS + h + 1, :])
                        ).astype(BF16)
                    return unused

                lax.fori_loop(0, ROW // SUB, tile, 0, unroll=4)
            into = slice(half * HALF, (half + 1) * HALF)
            acc_a[into] += nn(low_g[...], asked)
            acc_b[into] += nn(low_w[...], block)
        return unused

    lax.fori_loop(0, CHUNKS, backward, 0)
    pair_out[:, :CH] = unstack_heads(acc_a, 1)
    pair_out[:, CH:] = unstack_heads(acc_b, 1)
    pairs.start()
    gk_mine = unstack_heads(acc_a, 0)
    gv_mine = unstack_heads(acc_b, 0)
    pairs.arrived()
    gproj[:, CH : 2 * CH] = (gk_mine + pair_in[:, :CH]).astype(BF16)
    gproj[:, 2 * CH :] = (gv_mine + pair_in[:, CH:]).astype(BF16)
    proj = gproj[...]
    qkv_part = tn(feat[...], proj[:, CH:])
    for k in range(4):
        qkv_sum.part[k * CH : (k + 1) * CH] = qkv_part[:, k * 128 : (k + 1) * 128]
    qkv_sum.begin()
    rest_sum.spread()
    qkv_sum.scatter()
    gf[...] = ghid[...] + nt(proj, wqkv[...])
    qkv_sum.along_z()
    rest_sum.swap()
    qkv_sum.spread()
    rest_sum.last()
    qkv_sum.swap()
    qkv_sum.last()

    for group in (fg, dg, sg, rest_sum, qkv_sum):
        group.finish()
    for message in (sib_f, down_fine, up_fine, sib_g, tri, parts, down_hid, up_hid, pairs):
        message.sent()


def scale_out(gf_in, rest, qkv, gf, gqkv, gout, gconv):
    coarse = 1.0 / math.sqrt(2 * 64 * ROW)
    fine_scale = 1.0 / math.sqrt(2 * 128 * 256)
    gf[...] = gf_in[...]
    gconv[...] = rest[:2304].astype(F32) * fine_scale
    for k in range(2):
        gout[:, k * 128 : (k + 1) * 128] = rest[2304 + k * CH : 2304 + (k + 1) * CH].astype(F32) * coarse
        gqkv[:, k * 128 : (k + 1) * 128] = rest[2816 + k * CH : 2816 + (k + 1) * CH].astype(F32) * coarse
    for k in range(4):
        gqkv[:, CH + k * 128 : CH + (k + 1) * 128] = qkv[k * CH : (k + 1) * CH].astype(F32) * coarse


def shards(features, qkv_weight, out_weight, conv_weight, grad_output):
    messages = 2 * AG_MSGS + ST_MSGS + 2 * RS_MSGS + 9
    whole = pl.BlockSpec(memory_space=pltpu.VMEM)
    sums = pl.pallas_call(
        kernel,
        out_shape=[
            jax.ShapeDtypeStruct((ROW, CH), F32),
            jax.ShapeDtypeStruct((REST_ROWS, 128), BF16),
            jax.ShapeDtypeStruct((QKV_ROWS, 128), BF16),
        ],
        in_specs=[whole] * 5,
        out_specs=[whole] * 3,
        scratch_shapes=[
            pltpu.VMEM((2, RING, RING, ROW, CH), BF16),
            pltpu.VMEM((2, RING, RING, ROW, CH), BF16),
            pltpu.VMEM((2, RING, RING, 2 * HEADS, ROW), F32),
            pltpu.VMEM((ROW, CH), BF16),
            pltpu.VMEM((ROW, CH), BF16),
            pltpu.VMEM((2, 2 * ROW, CO), BF16),
            pltpu.VMEM((2, ROW, CH), BF16),
            pltpu.VMEM((2, ROW, 4 * CO), BF16),
            pltpu.VMEM((CHUNKS, CHUNK, CH), BF16),
            pltpu.VMEM((CHUNKS, CHUNK, CH), BF16),
            pltpu.VMEM((STACK, CH), BF16),
            pltpu.VMEM((STACK, CH), BF16),
            pltpu.VMEM((CHUNKS, STACK, CHUNK), F32),
            pltpu.VMEM((CHUNKS, STACK, CHUNK), F32),
            pltpu.VMEM((HALF, CHUNK), BF16),
            pltpu.VMEM((HALF, CHUNK), BF16),
            pltpu.VMEM((STACK, CH), F32),
            pltpu.VMEM((STACK, CH), F32),
            pltpu.VMEM((STACK, 128), F32),
            pltpu.VMEM((STACK, 128), F32),
            pltpu.VMEM((STACK, 128), F32),
            pltpu.VMEM((3, ROW, 128), F32),
            pltpu.VMEM((3, ROW, 128), F32),
            pltpu.VMEM((2, ROW, CH), F32),
            pltpu.VMEM((2, ROW, CH), F32),
            pltpu.VMEM((ROW, 2 * CH), F32),
            pltpu.VMEM((ROW, 2 * CH), F32),
            pltpu.VMEM((ROW, CH), F32),
            pltpu.VMEM((ROW, CH), BF16),
            pltpu.VMEM((ROW, 3 * CH), BF16),
            pltpu.VMEM((ROW, CH), BF16),
            pltpu.VMEM((2 * ROW, CO), F32),
            *total_scratch(REST_ROWS),
            *total_scratch(QKV_ROWS),
            pltpu.SemaphoreType.DMA((messages,)),
            pltpu.SemaphoreType.DMA((messages,)),
            pltpu.SemaphoreType.REGULAR,
        ],
        compiler_params=pltpu.CompilerParams(
            collective_id=0, has_side_effects=True, vmem_limit_bytes=63 * 1024 * 1024
        ),
    )(
        features.reshape(ROW, CH),
        qkv_weight,
        out_weight,
        conv_weight.reshape(9, CH, CO),
        grad_output.reshape(2, 2 * ROW, CO),
    )
    gf, gqkv, gout, gconv = pl.pallas_call(
        scale_out,
        out_shape=[
            jax.ShapeDtypeStruct((ROW, CH), F32),
            jax.ShapeDtypeStruct((CH, 3 * CH), F32),
            jax.ShapeDtypeStruct((CH, CH), F32),
            jax.ShapeDtypeStruct((9 * CH, CO), F32),
        ],
        in_specs=[whole] * 3,
        out_specs=[whole] * 4,
        compiler_params=pltpu.CompilerParams(vmem_limit_bytes=16 * 1024 * 1024),
    )(*sums)
    return (
        gf.reshape(1, 1, ROW, CH),
        gqkv,
        gout,
        gconv.reshape(3, 3, CH, CO),
    )


def solution(mesh):
    in_specs = (P("dp", "space", None, None), P(), P(), P(), P("dp", "space", None, None))
    out_specs = (P("dp", "space", None, None), P(), P(), P())
    return jax.shard_map(shards, mesh=mesh, in_specs=in_specs, out_specs=out_specs, check_vma=False)
```

```python
import math

import jax
import jax.numpy as jnp
from jax import lax
from jax.experimental import pallas as pl
from jax.experimental.pallas import tpu as pltpu
from jax.sharding import PartitionSpec as P

MESH = pl.DeviceIdType.MESH
F32 = jnp.float32
BF16 = jnp.bfloat16
HDIM = 64
HEADS = 4
CH = 256
CO = 128
ROW = 128
RING = 4
CHUNK = RING * ROW
CHUNKS = 8
STACK = 2 * HEADS * ROW
PAIR = STACK // 2
SUB = 32
SLOT = RING * STACK
REST_ROWS = 3584
QKV_ROWS = 1024
PLANE = [(k % 4, k // 4) for k in range(1, 16)]
AG_MSGS = 41
ST_MSGS = 31
RS_MSGS = 35


def nt(a, b):
    return lax.dot_general(a, b, (((1,), (1,)), ((), ())), preferred_element_type=F32)


def tn(a, b):
    return lax.dot_general(a, b, (((0,), (0,)), ((), ())), preferred_element_type=F32)


def nn(a, b):
    return jnp.dot(a, b, preferred_element_type=F32)


class Message:
    def __init__(self, src, dst, landing, sems, slot, device):
        send, recv = sems
        self.out = pltpu.make_async_remote_copy(
            src_ref=src, dst_ref=dst, send_sem=send.at[slot], recv_sem=recv.at[slot], device_id=device, device_id_type=MESH
        )
        self.into = pltpu.make_async_remote_copy(
            src_ref=landing, dst_ref=landing, send_sem=send.at[slot], recv_sem=recv.at[slot], device_id=device, device_id_type=MESH
        )

    def start(self):
        self.out.start()

    def arrived(self):
        self.into.wait_recv()

    def sent(self):
        self.out.wait_send()


class Place:
    def __init__(self):
        self.d = lax.axis_index("dp")
        self.s = lax.axis_index("space")
        s = self.s
        self.c = lax.rem(s, 2)
        self.x = lax.rem(s // 2, RING)
        self.zl = lax.rem(s // 8, 2)
        self.y = s // 16
        self.zo = 1 - self.zl

    def at(self, d=None, y=None, z=None, x=None, c=None):
        d = self.d if d is None else d
        y = self.y if y is None else y
        z = self.zl if z is None else z
        x = self.x if x is None else x
        c = self.c if c is None else c
        return (d, ((y * 2 + z) * RING + x) * 2 + c)

    def line(self, step):
        return (self.d, lax.rem(self.s + step + 64, 64))

    def ring_x(self, step):
        return self.at(x=lax.rem(self.x + step + RING, RING))

    def ring_y(self, step):
        return self.at(y=lax.rem(self.y + step + RING, RING))

    def plane(self, dx, dy, z=None):
        return self.at(x=lax.rem(self.x + dx + RING, RING), y=lax.rem(self.y + dy + RING, RING), z=z)

    def back(self, t, dx, dy):
        x, y = lax.rem(self.x + RING - dx, RING), lax.rem(self.y + RING - dy, RING)
        return t, jnp.where(t == 0, y, x), jnp.where(t == 0, x, y)

    def first(self, t, step):
        hit = t == 0
        return self.at(
            x=jnp.where(hit, lax.rem(self.x + step + RING, RING), self.x),
            y=jnp.where(hit, self.y, lax.rem(self.y + step + RING, RING)),
        )

    def second(self, t, step):
        return self.first(1 - t, step)

    def coords(self, t):
        return jnp.where(t == 0, self.y, self.x), jnp.where(t == 0, self.x, self.y)


class Gather:
    def __init__(self, place, buf, sems, base, direct):
        self.place, self.buf, self.sems, self.count, self.base = place, buf, sems, 0, base
        self.direct = direct
        half = ROW // 2
        low, high = pl.ds(0, half), pl.ds(half, half)
        s0, f0 = place.coords(place.zl)
        s1, f1 = place.coords(place.zo)
        m = {"z": self.make((place.zl, s0, f0), (place.zo, s1, f1), place.at(z=place.zo))}
        for r in (0, 1):
            t = place.zl if r == 0 else place.zo
            s, f = (s0, f0) if r == 0 else (s1, f1)
            sm, sp, s2 = (lax.rem(s + k, RING) for k in (3, 1, 2))
            fm, fp, f2 = (lax.rem(f + k, RING) for k in (3, 1, 2))
            up, down = place.first(t, 1), place.first(t, -1)
            m[r, "1+"] = self.make((t, s, f), (t, s, fm), up)
            m[r, "1-"] = self.make((t, s, f), (t, s, fp), down)
            if direct:
                m[r, "12"] = self.make((t, s, f), (t, s, f2), place.first(t, 2))
            else:
                m[r, "1f+"] = self.make((t, s, fm, low), (t, s, f2, low), up)
                m[r, "1f-"] = self.make((t, s, fp, high), (t, s, f2, high), down)
            up, down = place.second(t, 1), place.second(t, -1)
            for q, g in enumerate((f, fm, fp, f2)):
                m[r, q, "2+"] = self.make((t, s, g), (t, sm, g), up)
                m[r, q, "2-"] = self.make((t, s, g), (t, sp, g), down)
                m[r, q, "2f+"] = self.make((t, sm, g, low), (t, s2, g, low), up)
                m[r, q, "2f-"] = self.make((t, sp, g, high), (t, s2, g, high), down)
        self.m = m

    def make(self, src, landing, device):
        slot = self.base + self.count
        self.count += 1
        src = self.buf.at[src]
        return Message(src, src, self.buf.at[landing], self.sems, slot, device)

    def go(self, *keys):
        for key in keys:
            self.m[key].start()

    def ring(self, r):
        self.go((r, "1+"), (r, "1-"), *([(r, "12")] if self.direct else []), (r, 0, "2+"), (r, 0, "2-"))

    def begin(self):
        self.go("z")
        self.ring(0)

    def other(self):
        self.m["z"].arrived()
        self.ring(1)

    def near(self, r):
        self.m[r, "1+"].arrived()
        self.go(*([] if self.direct else [(r, "1f+")]), (r, 1, "2+"), (r, 1, "2-"))
        self.m[r, "1-"].arrived()
        self.go(*([] if self.direct else [(r, "1f-")]), (r, 2, "2+"), (r, 2, "2-"))

    def pass_on(self, r, *blocks):
        for q in blocks:
            self.m[r, q, "2+"].arrived()
            self.go((r, q, "2f+"))
            self.m[r, q, "2-"].arrived()
            self.go((r, q, "2f-"))

    def far(self, r):
        if self.direct:
            self.m[r, "12"].arrived()
        else:
            self.m[r, "1f+"].arrived()
            self.m[r, "1f-"].arrived()
        self.go((r, 3, "2+"), (r, 3, "2-"))

    def last(self, r):
        for q in range(4):
            self.m[r, q, "2f+"].arrived()
            self.m[r, q, "2f-"].arrived()

    def finish(self):
        for message in self.m.values():
            message.sent()


class StatGather:
    def __init__(self, place, buf, sems, base):
        s0, f0 = place.coords(place.zl)
        s1, f1 = place.coords(place.zo)
        src = buf.at[place.zl, s0, f0]
        self.z = Message(src, src, buf.at[place.zo, s1, f1], sems, base, place.at(z=place.zo))
        self.wide = ([], [])
        slot = base + 1
        for r in (0, 1):
            t = place.zl if r == 0 else place.zo
            src = buf.at[place.back(t, 0, 0)]
            for dx, dy in PLANE:
                self.wide[r].append(Message(src, src, buf.at[place.back(t, dx, dy)], sems, slot, place.plane(dx, dy)))
                slot += 1

    def begin(self):
        self.z.start()
        for message in self.wide[0]:
            message.start()

    def other(self):
        self.z.arrived()
        for message in self.wide[1]:
            message.start()

    def last(self):
        for message in (*self.wide[0], *self.wide[1]):
            message.arrived()

    def finish(self):
        for message in (self.z, *self.wide[0], *self.wide[1]):
            message.sent()


class Total:
    def __init__(self, place, rows, part, half_in, mid_out, mid_in, zed, done, sems, base):
        self.place, self.part, self.half_in = place, part, half_in
        self.mid_out, self.mid_in, self.zed, self.done = mid_out, mid_in, zed, done
        self.half, self.piece = rows // 2, rows // 32
        c = place.c
        self.mine = place.y * RING + place.x
        self.z = place.d * 2 + place.zl
        sib = place.at(c=1 - c)
        away = part.at[self.span(1 - c)]
        self.core = Message(away, half_in, half_in, sems, base, sib)
        slot = base + 1
        self.out, self.by_z, self.back = [], [], []
        here = done.at[self.span(c, self.mine)]
        for k, (dx, dy) in enumerate(PLANE):
            x, y = lax.rem(place.x + dx, RING), lax.rem(place.y + dy, RING)
            src = mid_out.at[pl.ds(pl.multiple_of((y * RING + x) * self.piece, 16), self.piece)]
            self.out.append(Message(src, mid_in.at[k], mid_in.at[k], sems, slot, place.plane(dx, dy)))
            x, y = lax.rem(place.x + RING - dx, RING), lax.rem(place.y + RING - dy, RING)
            self.back.append(
                Message(here, here, done.at[self.span(c, y * RING + x)], sems, slot + 1, place.plane(dx, dy))
            )
            slot += 2
        for k in (1, 3, 2):
            to, of = lax.rem(self.z + k, 4), lax.rem(self.z + 4 - k, 4)
            src = zed.at[self.z]
            self.by_z.append(Message(src, src, zed.at[of], sems, slot, place.at(d=to // 2, z=lax.rem(to, 2))))
            slot += 1
        src = done.at[self.span(c)]
        self.across = Message(src, src, done.at[self.span(1 - c)], sems, slot, sib)

    def span(self, c, piece=None):
        if piece is None:
            return pl.ds(pl.multiple_of(c * self.half, 16), self.half)
        return pl.ds(pl.multiple_of(c * self.half + piece * self.piece, 16), self.piece)

    def begin(self):
        self.core.start()

    def scatter(self):
        self.core.arrived()
        mine = self.span(self.place.c)
        both = self.part[mine] + self.half_in[...]
        self.part[mine] = both
        self.mid_out[...] = both.astype(BF16)
        for message in self.out:
            message.start()

    def along_z(self):
        total = self.part[self.span(self.place.c, self.mine)]
        for k, message in enumerate(self.out):
            message.arrived()
            total = total + self.mid_in[k].astype(F32)
        self.zed[self.z] = total
        for message in self.by_z:
            message.start()

    def spread(self):
        for message in self.by_z:
            message.arrived()
        total = (self.zed[0] + self.zed[1]) + (self.zed[2] + self.zed[3])
        self.done[self.span(self.place.c, self.mine)] = total.astype(BF16)
        for message in self.back:
            message.start()

    def swap(self):
        for message in self.back:
            message.arrived()
        self.across.start()

    def last(self):
        self.across.arrived()

    def finish(self):
        for message in (self.core, *self.out, *self.by_z, *self.back, self.across):
            message.sent()


def total_scratch(rows):
    return [
        pltpu.VMEM((rows // 2, 128), F32),
        pltpu.VMEM((rows // 2, 128), BF16),
        pltpu.VMEM((15, rows // 32, 128), BF16),
        pltpu.VMEM((4, rows // 32, 128), F32),
    ]


def head_mask(shape, h):
    lane = lax.broadcasted_iota(jnp.int32, shape, len(shape) - 1)
    return jnp.logical_and(lane >= h * HDIM, lane < (h + 1) * HDIM)


def stack_heads(ref, half, rows):
    for h in range(HEADS):
        start = ((h // 2) * 4 + half * 2 + h % 2) * ROW
        ref[start : start + ROW] = jnp.where(head_mask(rows.shape, h), rows, jnp.zeros_like(rows))


def unstack_heads(ref, half):
    out = []
    for pair in range(2):
        start = (pair * 4 + half * 2) * ROW
        first, second = ref[start : start + ROW], ref[start + ROW : start + 2 * ROW]
        out.append(jnp.where(head_mask((ROW, 128), 0), first, second))
    return jnp.concatenate(out, axis=1)


def moved(rows, step):
    n = rows.shape[0]
    index = lax.broadcasted_iota(jnp.int32, rows.shape, 0)
    if step == 1:
        return jnp.where(index == n - 1, 0.0, pltpu.roll(rows, n - 1, 0))
    return jnp.where(index == 0, 0.0, pltpu.roll(rows, 1, 0))


def kernel(
    feat, wqkv, wout, wconv, go,
    gf, rest_done, qkv_done,
    feats, grads, stats, sib_feat, sib_grad, fine, rim, sides,
    keys, values, queries, qm, dm,
    even, odd, low_w0, low_g0, low_w1, low_g1, acc_a, acc_b,
    run_m, run_l, run_d, tri_out, tri_in,
    part_out, part_in, kept, pair_out, pair_in, ghid, glow, gproj, hid,
    wide, *rest,
):
    rest_total = (odd.at[pl.ds(4 * SLOT, REST_ROWS)], *rest[:4], rest_done)
    qkv_total = (odd.at[pl.ds(5 * SLOT, QKV_ROWS)], *rest[4:8], qkv_done)
    send, recv, greet = rest[8:]
    sems = (send, recv)
    place = Place()
    c, s, zl = place.c, place.s, place.zl
    sib = place.at(c=1 - c)
    above, below = place.line(-1), place.line(1)

    base = 0
    fg = Gather(place, feats, sems, base, True)
    base += AG_MSGS
    dg = Gather(place, grads, sems, base, False)
    base += AG_MSGS
    sg = StatGather(place, stats, sems, base)
    base += ST_MSGS
    rest_sum = Total(place, REST_ROWS, *rest_total, sems, base)
    base += RS_MSGS
    qkv_sum = Total(place, QKV_ROWS, *qkv_total, sems, base)
    base += RS_MSGS
    sib_f = Message(feat, sib_feat, sib_feat, sems, base, sib)
    down_fine = Message(go.at[1], fine.at[0], fine.at[0], sems, base + 1, below)
    up_fine = Message(go.at[0], fine.at[1], fine.at[1], sems, base + 2, above)
    s0, f0 = place.coords(zl)
    own = (zl, s0, f0)
    sib_g = Message(grads.at[own], sib_grad, sib_grad, sems, base + 3, sib)
    tri = Message(tri_out, tri_in, tri_in, sems, base + 4, sib)
    parts = Message(part_out, part_in, part_in, sems, base + 5, sib)
    down_hid = Message(hid, rim.at[0], rim.at[0], sems, base + 6, below)
    up_hid = Message(hid, rim.at[1], rim.at[1], sems, base + 7, above)
    pairs = Message(pair_out, pair_in, pair_in, sems, base + 8, sib)

    def scaled_queries(rows):
        whole = nn(rows, wqkv[:, :CH]).astype(BF16)
        return (whole.astype(F32) * (1.0 / math.sqrt(HDIM))).astype(BF16)

    def stack_keys(rows, half):
        whole = nn(rows, wqkv[:, CH:]).astype(BF16)
        stack_heads(qm, half, whole[:, :CH])
        stack_heads(dm, half, whole[:, CH:])

    barrier = pltpu.get_barrier_semaphore()
    peers = [sib, place.at(z=place.zo), above, below]
    peers += [place.ring_x(k) for k in (1, 2, 3)] + [place.ring_y(k) for k in (1, 2, 3)]
    next_z = place.at(d=1 - place.d, z=place.zo)
    peers.append(next_z)
    for peer in peers:
        pl.semaphore_signal(barrier, inc=1, device_id=peer, device_id_type=MESH)

    def split(rows):
        wide[...] = rows.astype(F32)
        return wide[pl.ds(0, ROW, stride=2)], wide[pl.ds(1, ROW, stride=2)]

    def pack(*cells):
        return jnp.concatenate(cells, axis=1).astype(BF16)

    def taps(lines, a):
        w0, w1, w2 = wconv[3 * a], wconv[3 * a + 1], wconv[3 * a + 2]
        main = nt(lines, jnp.concatenate([w1, w0], axis=1)) + nt(lines, jnp.concatenate([w2, w1], axis=1))
        return main, nt(lines[:, :CO], w0), nt(lines[:, CO:], w2)

    feats[own] = feat[...]
    stack_heads(qm, 0, scaled_queries(feat[...]))
    own_lines = []
    for r in (0, 1):
        even_cells, odd_cells = split(go[r])
        sides[r] = pack(even_cells, odd_cells, moved(even_cells, 1), moved(odd_cells, -1))
        own_lines.append(pack(even_cells, odd_cells))
    middle = taps(jnp.concatenate(own_lines, axis=0), 1)
    local = [
        m[:ROW] + m[ROW:] + f + l for m, f, l in zip(middle, taps(own_lines[1], 0), taps(own_lines[0], 2), strict=True)
    ]
    run_m[...] = jnp.full((STACK, 128), -1e30, F32)
    run_l[...] = jnp.zeros((STACK, 128), F32)
    run_d[...] = jnp.zeros((STACK, 128), F32)
    odd[:SLOT] = jnp.full((SLOT, 128), -1e30, F32)
    odd[SLOT : 2 * SLOT] = jnp.zeros((SLOT, 128), F32)

    def clear():
        for ref in (acc_a, acc_b):
            ref[...] = jnp.zeros((STACK, 128), F32)
        for ref in (low_w1, low_g1):
            ref[...] = jnp.zeros((PAIR, CHUNK), BF16)

    clear()

    pl.semaphore_wait(barrier, len(peers))
    pl.semaphore_signal(greet, inc=1, device_id=next_z, device_id_type=MESH)
    down_fine.start()
    up_fine.start()
    fg.begin()
    sib_f.start()

    down_fine.arrived()
    up_fine.arrived()
    top, bottom = pack(*split(fine[0])), pack(*split(fine[1]))
    top = jnp.where(s > 0, top, jnp.zeros_like(top))
    bottom = jnp.where(s < 63, bottom, jnp.zeros_like(bottom))
    main, plus, minus = (m + f + l for m, f, l in zip(local, taps(bottom, 0), taps(top, 2), strict=True))
    hidden_grad = main + moved(plus, 1) + moved(minus, -1)
    ghid[...] = hidden_grad
    hidden_low = hidden_grad.astype(BF16)
    glow[...] = hidden_low
    own_grad = nt(hidden_low, wout[...]).astype(BF16)
    grads[own] = own_grad
    sib_g.start()
    dg.begin()
    fg.other()
    fg.near(0)
    fg.far(0)
    fg.pass_on(0, 0)

    stack_heads(dm, 0, own_grad)
    sib_f.arrived()
    stack_heads(qm, 1, scaled_queries(sib_feat[...]))
    sib_g.arrived()
    stack_heads(dm, 1, sib_grad[...])

    def where_is(j):
        role = jnp.where((j == 1) | (j == 4) | (j == 5) | (j == 7), 1, 0)
        t = jnp.where(role == 0, zl, place.zo)
        offset = jnp.where(j < 2, 0, jnp.where(j > 5, 2, jnp.where(lax.rem(j, 2) == 0, 3, 1)))
        second, _ = place.coords(t)
        return t, lax.rem(second + offset, RING)

    def steps(jj, p, acts):
        for when, act in acts.items():
            if when % 2 == p:
                pl.when(jj == when // 2)(act)

    holds = (even, odd)
    lows = ((low_w0, low_g0), (low_w1, low_g1))

    def tile_at(slot, b, first, count):
        return pl.ds(pl.multiple_of(slot * SLOT + b * STACK + first, SUB), count)

    def put(ref, slot, pair, product):
        for b in range(RING):
            ref[tile_at(slot, b, pair * PAIR, PAIR)] = product[:, b * 128 : (b + 1) * 128]

    def statistics(ref, slot, pair):
        for i in range(PAIR // SUB):
            first = pair * PAIR + i * SUB
            span = slice(first, first + SUB)
            sc = [ref[tile_at(slot, b, first, SUB)] for b in range(RING)]
            old = run_m[span]
            new = jnp.maximum(jnp.maximum(jnp.maximum(sc[0], sc[1]), jnp.maximum(sc[2], sc[3])), old)
            shrink = jnp.exp(old - new)
            total, dot = run_l[span] * shrink, run_d[span] * shrink
            for b in range(RING):
                w = jnp.exp(sc[b] - new)
                total = total + w
                dot = dot + w * ref[tile_at(slot + 1, b, first, SUB)]
            run_m[span] = new
            run_l[span] = total
            run_d[span] = dot

    def f1():
        fg.near(1)
        fg.far(1)
        fg.pass_on(1, 0)

    def f2():
        fg.pass_on(0, 1, 2, 3)

    def f3():
        dg.other()
        dg.near(0)
        dg.pass_on(0, 0)

    def f4():
        fg.pass_on(1, 1, 2, 3)

    def f5():
        dg.near(1)
        dg.pass_on(1, 0)

    def f6():
        fg.last(0)
        dg.far(0)

    def f7():
        fg.last(1)
        dg.far(1)

    def first_pass(jj, skip):
        for p in (0, 1):
            j = 2 * jj + p
            steps(jj, p, {1: f1, 2: f2, 3: f3, 4: f4, 5: f5, 6: f6, 7: f7})
            t, second = where_is(j)
            block = feats[t, second].reshape(CHUNK, CH)
            whole = nn(block, wqkv[...]).astype(BF16)
            queries[j] = (whole[:, :CH].astype(F32) * (1.0 / math.sqrt(HDIM))).astype(BF16)
            keys[j] = whole[:, CH : 2 * CH]
            values[j] = whole[:, 2 * CH :]
            for pair in range(2):
                rows = slice(pair * PAIR, (pair + 1) * PAIR)
                put(holds[p], 2 * jj, pair, nt(qm[rows], whole[:, CH : 2 * CH]))
                put(holds[p], 2 * jj + 1, pair, nt(dm[rows], whole[:, 2 * CH :]))
                if p == 1:
                    statistics(even, 2 * jj, pair)
                else:
                    statistics(odd, jnp.maximum(2 * jj - 2, 0), pair)
        return skip

    lax.fori_loop(0, CHUNKS // 2, first_pass, 0)
    for pair in range(2):
        statistics(odd, CHUNKS - 2, pair)

    lane = lax.broadcasted_iota(jnp.int32, (ROW, 128), 1)
    mine = [jnp.zeros((ROW, 128), F32), jnp.ones((ROW, 128), F32), jnp.zeros((ROW, 128), F32)]
    theirs = list(mine)
    for half in (0, 1):
        for h in range(HEADS):
            g = half * HEADS + h
            start = ((h // 2) * 4 + half * 2 + h % 2) * ROW
            span = slice(start, start + ROW)
            m = run_m[span]
            top = jnp.max(m, axis=1, keepdims=True)
            e = jnp.exp(m - top)
            cols = [
                top,
                jnp.sum(run_l[span] * e, axis=1, keepdims=True),
                jnp.sum(run_d[span] * e, axis=1, keepdims=True),
            ]
            for k in range(3):
                mine[k] = jnp.where(lane == g, cols[k], mine[k])
                theirs[k] = jnp.where(lane == (1 - half) * HEADS + h, cols[k], theirs[k])
    for k in range(3):
        tri_out[k] = theirs[k]
    tri.start()
    stack_keys(feat[...], 0)
    stack_keys(sib_feat[...], 1)
    tri.arrived()
    top = jnp.maximum(mine[0], tri_in[0])
    ea, eb = jnp.exp(mine[0] - top), jnp.exp(tri_in[0] - top)
    total = mine[1] * ea + tri_in[1] * eb
    delta = (mine[2] * ea + tri_in[2] * eb) / total
    lse = top + jnp.log(total)
    stats[own] = jnp.concatenate([jnp.transpose(lse)[:HEADS], jnp.transpose(delta)[:HEADS]], axis=0)
    sg.begin()
    for g in range(2 * HEADS):
        half, h = g // HEADS, g % HEADS
        start = ((h // 2) * 4 + half * 2 + h % 2) * ROW
        span = slice(start, start + ROW)
        run_m[span] = jnp.broadcast_to(lse[:, g : g + 1], (ROW, 128))
        run_l[span] = jnp.broadcast_to(delta[:, g : g + 1], (ROW, 128))

    def weights_of(ref, p_slot, pair):
        low_w, low_g = lows[pair]
        for i in range(PAIR // SUB):
            first = pair * PAIR + i * SUB
            to = slice(i * SUB, (i + 1) * SUB)
            lse_t, delta_t = run_m[first : first + SUB], run_l[first : first + SUB]
            for b in range(RING):
                w = jnp.exp(ref[tile_at(p_slot, b, first, SUB)] - lse_t)
                low_w[to, b * 128 : (b + 1) * 128] = w.astype(BF16)
                low_g[to, b * 128 : (b + 1) * 128] = (
                    w * (ref[tile_at(p_slot + 1, b, first, SUB)] - delta_t)
                ).astype(BF16)

    def add_products(pair, with_w, with_g):
        low_w, low_g = lows[pair]
        rows = slice(pair * PAIR, (pair + 1) * PAIR)
        acc_a[rows] += nn(low_w[...], with_w)
        acc_b[rows] += nn(low_g[...], with_g)

    def columns(pair):
        return slice(pair * 128, (pair + 1) * 128)

    def p0():
        dg.pass_on(0, 1, 2)

    def p1():
        sg.other()

    def p2():
        dg.pass_on(1, 1, 2)

    def p3():
        dg.pass_on(0, 3)

    def p4():
        dg.pass_on(1, 3)

    def forward(jj, skip):
        for p in (0, 1):
            j = 2 * jj + p
            steps(jj, p, {0: p0, 1: p1, 2: p2, 3: p3, 4: p4})
            before = jnp.maximum(j - 1, 0)
            add_products(1, values[before, :, columns(1)], keys[before, :, columns(1)])
            weights_of(holds[p], 2 * jj, 0)
            add_products(0, values[j, :, columns(0)], keys[j, :, columns(0)])
            weights_of(holds[p], 2 * jj, 1)
        return skip

    lax.fori_loop(0, CHUNKS // 2, forward, 0)
    add_products(1, values[CHUNKS - 1, :, columns(1)], keys[CHUNKS - 1, :, columns(1)])
    part_out[0] = unstack_heads(acc_a, 1)
    part_out[1] = unstack_heads(acc_b, 1)
    parts.start()
    kept[0] = unstack_heads(acc_a, 0)
    kept[1] = unstack_heads(acc_b, 0)
    clear()

    def attended_rows():
        parts.arrived()
        attended = (kept[0] + part_in[0]).astype(BF16)
        gproj[:, :CH] = ((kept[1] + part_in[1]) * (1.0 / math.sqrt(HDIM))).astype(BF16)
        hid[...] = (feat[...].astype(F32) + nn(attended, wout[...])).astype(BF16)
        down_hid.start()
        up_hid.start()
        out_part = tn(attended, glow[...])
        part = rest_sum.part
        part[2304:2560] = out_part[:, :128]
        part[2560:2816] = out_part[:, 128:]
        query_part = tn(feat[...], gproj[:, :CH])
        part[2816:3072] = query_part[:, :128]
        part[3072:3328] = query_part[:, 128:]
        part[3328:] = jnp.zeros((REST_ROWS - 3328, 128), F32)

    def conv_rows():
        down_hid.arrived()
        up_hid.arrived()
        mid = hid[...]
        over = jnp.where(s > 0, rim[0], jnp.zeros_like(mid))
        under = jnp.where(s < 63, rim[1], jnp.zeros_like(mid))
        same, other = tn(mid, sides[0]), tn(mid, sides[1])
        part = rest_sum.part
        for a, whole in enumerate((tn(over, sides[0]) + other, same + other, same + tn(under, sides[1]))):
            even_c, odd_c, even1, odd1 = (whole[:, k * CO : (k + 1) * CO] for k in range(4))
            part[(3 * a) * CH : (3 * a + 1) * CH] = even1 + odd_c
            part[(3 * a + 1) * CH : (3 * a + 2) * CH] = even_c + odd_c
            part[(3 * a + 2) * CH : (3 * a + 3) * CH] = even_c + odd1
        rest_sum.begin()

    def block_of(j):
        t, second = where_is(j)
        return grads[t, second].reshape(CHUNK, CH)

    def transposed_scores(j, p, pair):
        rows = slice(pair * PAIR, (pair + 1) * PAIR)
        put(holds[p], 0, pair, nt(qm[rows], queries[j]))
        put(holds[p], 1, pair, nt(dm[rows], block_of(j)))

    def transposed_weights(j, p, pair):
        low_w, low_g = lows[pair]
        t, second = where_is(j)
        for part in range(4):
            h = 2 * pair + part % 2
            for i in range(ROW // SUB):
                first = part * ROW + i * SUB
                to = slice(first, first + SUB)
                for b in range(RING):
                    w = jnp.exp(holds[p][tile_at(0, b, pair * PAIR + first, SUB)] - stats[t, second, b, h : h + 1, :])
                    low_w[to, b * 128 : (b + 1) * 128] = w.astype(BF16)
                    low_g[to, b * 128 : (b + 1) * 128] = (
                        w * (holds[p][tile_at(1, b, pair * PAIR + first, SUB)] - stats[t, second, b, HEADS + h : HEADS + h + 1, :])
                    ).astype(BF16)

    def backward(jj, skip, final=False):
        for p in (0, 1):
            j = 2 * jj + p
            if final and p == 0:
                rest_sum.scatter()
                dg.last(1)
            if not final:
                steps(jj, p, {2: attended_rows, 4: conv_rows, 5: lambda: dg.last(0)})
            before = jnp.maximum(j - 1, 0)
            more = not (final and p == 1)
            if more:
                transposed_scores(j + 1, 1 - p, 0)
            add_products(1, block_of(before)[:, columns(1)], queries[before, :, columns(1)])
            transposed_weights(j, p, 0)
            if more:
                transposed_scores(j + 1, 1 - p, 1)
            add_products(0, block_of(j)[:, columns(0)], queries[j, :, columns(0)])
            transposed_weights(j, p, 1)
        return skip

    pl.semaphore_wait(greet, 1)
    transposed_scores(0, 0, 0)
    transposed_scores(0, 0, 1)
    sg.last()
    lax.fori_loop(0, CHUNKS // 2 - 1, backward, 0)
    backward(CHUNKS // 2 - 1, 0, True)
    add_products(1, block_of(CHUNKS - 1)[:, columns(1)], queries[CHUNKS - 1, :, columns(1)])
    pair_out[:, :CH] = unstack_heads(acc_b, 1)
    pair_out[:, CH:] = unstack_heads(acc_a, 1)
    pairs.start()
    gk_mine = unstack_heads(acc_b, 0)
    gv_mine = unstack_heads(acc_a, 0)
    pairs.arrived()
    gproj[:, CH : 2 * CH] = (gk_mine + pair_in[:, :CH]).astype(BF16)
    gproj[:, 2 * CH :] = (gv_mine + pair_in[:, CH:]).astype(BF16)
    proj = gproj[...]
    qkv_part = tn(feat[...], proj[:, CH:])
    for k in range(4):
        qkv_sum.part[k * CH : (k + 1) * CH] = qkv_part[:, k * 128 : (k + 1) * 128]
    qkv_sum.begin()
    gf[...] = ghid[...] + nt(proj, wqkv[...])
    qkv_sum.scatter()
    rest_sum.along_z()
    qkv_sum.along_z()
    rest_sum.spread()
    qkv_sum.spread()
    rest_sum.swap()
    qkv_sum.swap()
    rest_sum.last()
    qkv_sum.last()

    for group in (fg, dg, sg, rest_sum, qkv_sum):
        group.finish()
    for message in (sib_f, down_fine, up_fine, sib_g, tri, parts, down_hid, up_hid, pairs):
        message.sent()


def scale_out(gf_in, rest, qkv, gf, gqkv, gout, gconv):
    coarse = 1.0 / math.sqrt(2 * 64 * ROW)
    fine_scale = 1.0 / math.sqrt(2 * 128 * 256)
    gf[...] = gf_in[...]
    gconv[...] = rest[:2304].astype(F32) * fine_scale
    for k in range(2):
        gout[:, k * 128 : (k + 1) * 128] = rest[2304 + k * CH : 2304 + (k + 1) * CH].astype(F32) * coarse
        gqkv[:, k * 128 : (k + 1) * 128] = rest[2816 + k * CH : 2816 + (k + 1) * CH].astype(F32) * coarse
    for k in range(4):
        gqkv[:, CH + k * 128 : CH + (k + 1) * 128] = qkv[k * CH : (k + 1) * CH].astype(F32) * coarse


def shards(features, qkv_weight, out_weight, conv_weight, grad_output):
    messages = 2 * AG_MSGS + ST_MSGS + 2 * RS_MSGS + 9
    whole = pl.BlockSpec(memory_space=pltpu.VMEM)
    sums = pl.pallas_call(
        kernel,
        out_shape=[
            jax.ShapeDtypeStruct((ROW, CH), F32),
            jax.ShapeDtypeStruct((REST_ROWS, 128), BF16),
            jax.ShapeDtypeStruct((QKV_ROWS, 128), BF16),
        ],
        in_specs=[whole] * 5,
        out_specs=[whole] * 3,
        scratch_shapes=[
            pltpu.VMEM((2, RING, RING, ROW, CH), BF16),
            pltpu.VMEM((2, RING, RING, ROW, CH), BF16),
            pltpu.VMEM((2, RING, RING, 2 * HEADS, ROW), F32),
            pltpu.VMEM((ROW, CH), BF16),
            pltpu.VMEM((ROW, CH), BF16),
            pltpu.VMEM((2, 2 * ROW, CO), BF16),
            pltpu.VMEM((2, ROW, CH), BF16),
            pltpu.VMEM((2, ROW, 4 * CO), BF16),
            pltpu.VMEM((CHUNKS, CHUNK, CH), BF16),
            pltpu.VMEM((CHUNKS, CHUNK, CH), BF16),
            pltpu.VMEM((CHUNKS, CHUNK, CH), BF16),
            pltpu.VMEM((STACK, CH), BF16),
            pltpu.VMEM((STACK, CH), BF16),
            pltpu.VMEM((CHUNKS * SLOT, 128), F32),
            pltpu.VMEM((CHUNKS * SLOT, 128), F32),
            pltpu.VMEM((PAIR, CHUNK), BF16),
            pltpu.VMEM((PAIR, CHUNK), BF16),
            pltpu.VMEM((PAIR, CHUNK), BF16),
            pltpu.VMEM((PAIR, CHUNK), BF16),
            pltpu.VMEM((STACK, 128), F32),
            pltpu.VMEM((STACK, 128), F32),
            pltpu.VMEM((STACK, 128), F32),
            pltpu.VMEM((STACK, 128), F32),
            pltpu.VMEM((STACK, 128), F32),
            pltpu.VMEM((3, ROW, 128), F32),
            pltpu.VMEM((3, ROW, 128), F32),
            pltpu.VMEM((2, ROW, CH), F32),
            pltpu.VMEM((2, ROW, CH), F32),
            pltpu.VMEM((2, ROW, CH), F32),
            pltpu.VMEM((ROW, 2 * CH), F32),
            pltpu.VMEM((ROW, 2 * CH), F32),
            pltpu.VMEM((ROW, CH), F32),
            pltpu.VMEM((ROW, CH), BF16),
            pltpu.VMEM((ROW, 3 * CH), BF16),
            pltpu.VMEM((ROW, CH), BF16),
            pltpu.VMEM((2 * ROW, CO), F32),
            *total_scratch(REST_ROWS),
            *total_scratch(QKV_ROWS),
            pltpu.SemaphoreType.DMA((messages,)),
            pltpu.SemaphoreType.DMA((messages,)),
            pltpu.SemaphoreType.REGULAR,
        ],
        compiler_params=pltpu.CompilerParams(
            collective_id=0, has_side_effects=True, vmem_limit_bytes=63 * 1024 * 1024
        ),
    )(
        features.reshape(ROW, CH),
        qkv_weight,
        out_weight,
        conv_weight.reshape(9, CH, CO),
        grad_output.reshape(2, 2 * ROW, CO),
    )
    gf, gqkv, gout, gconv = pl.pallas_call(
        scale_out,
        out_shape=[
            jax.ShapeDtypeStruct((ROW, CH), F32),
            jax.ShapeDtypeStruct((CH, 3 * CH), F32),
            jax.ShapeDtypeStruct((CH, CH), F32),
            jax.ShapeDtypeStruct((9 * CH, CO), F32),
        ],
        in_specs=[whole] * 3,
        out_specs=[whole] * 4,
        compiler_params=pltpu.CompilerParams(vmem_limit_bytes=62 * 1024 * 1024),
    )(*sums)
    return (
        gf.reshape(1, 1, ROW, CH),
        gqkv,
        gout,
        gconv.reshape(3, 3, CH, CO),
    )


def solution(mesh):
    in_specs = (P("dp", "space", None, None), P(), P(), P(), P("dp", "space", None, None))
    out_specs = (P("dp", "space", None, None), P(), P(), P())
    return jax.shard_map(shards, mesh=mesh, in_specs=in_specs, out_specs=out_specs, check_vma=False)
```

```python
import math

import jax
import jax.numpy as jnp
from jax import lax
from jax.experimental import pallas as pl
from jax.experimental.pallas import tpu as pltpu
from jax.sharding import PartitionSpec as P

MESH = pl.DeviceIdType.MESH
F32 = jnp.float32
BF16 = jnp.bfloat16
HDIM = 64
HEADS = 4
CH = 256
CO = 128
ROW = 128
RING = 4
CHUNK = RING * ROW
CHUNKS = 8
STACK = 2 * HEADS * ROW
PAIR = STACK // 2
SUB = 32
SLOT = RING * STACK
REST_ROWS = 3584
QKV_ROWS = 1024
PLANE = [(k % 4, k // 4) for k in range(1, 16)]
AG_MSGS = 41
ST_MSGS = 31
RS_MSGS = 35
WIDE_MSGS = 49


def nt(a, b):
    return lax.dot_general(a, b, (((1,), (1,)), ((), ())), preferred_element_type=F32)


def tn(a, b):
    return lax.dot_general(a, b, (((0,), (0,)), ((), ())), preferred_element_type=F32)


def nn(a, b):
    return jnp.dot(a, b, preferred_element_type=F32)


class Message:
    def __init__(self, src, dst, landing, sems, slot, device):
        send, recv = sems
        self.out = pltpu.make_async_remote_copy(
            src_ref=src, dst_ref=dst, send_sem=send.at[slot], recv_sem=recv.at[slot], device_id=device, device_id_type=MESH
        )
        self.into = pltpu.make_async_remote_copy(
            src_ref=landing, dst_ref=landing, send_sem=send.at[slot], recv_sem=recv.at[slot], device_id=device, device_id_type=MESH
        )

    def start(self):
        self.out.start()

    def arrived(self):
        self.into.wait_recv()

    def sent(self):
        self.out.wait_send()


class Place:
    def __init__(self):
        self.d = lax.axis_index("dp")
        self.s = lax.axis_index("space")
        s = self.s
        self.c = lax.rem(s, 2)
        self.x = lax.rem(s // 2, RING)
        self.zl = lax.rem(s // 8, 2)
        self.y = s // 16
        self.zo = 1 - self.zl

    def at(self, d=None, y=None, z=None, x=None, c=None):
        d = self.d if d is None else d
        y = self.y if y is None else y
        z = self.zl if z is None else z
        x = self.x if x is None else x
        c = self.c if c is None else c
        return (d, ((y * 2 + z) * RING + x) * 2 + c)

    def line(self, step):
        return (self.d, lax.rem(self.s + step + 64, 64))

    def ring_x(self, step):
        return self.at(x=lax.rem(self.x + step + RING, RING))

    def ring_y(self, step):
        return self.at(y=lax.rem(self.y + step + RING, RING))

    def plane(self, dx, dy, c=None):
        return self.at(x=lax.rem(self.x + dx + RING, RING), y=lax.rem(self.y + dy + RING, RING), c=c)

    def back(self, t, dx, dy):
        x, y = lax.rem(self.x + RING - dx, RING), lax.rem(self.y + RING - dy, RING)
        return t, jnp.where(t == 0, y, x), jnp.where(t == 0, x, y)

    def first(self, t, step):
        hit = t == 0
        return self.at(
            x=jnp.where(hit, lax.rem(self.x + step + RING, RING), self.x),
            y=jnp.where(hit, self.y, lax.rem(self.y + step + RING, RING)),
        )

    def second(self, t, step):
        return self.first(1 - t, step)

    def coords(self, t):
        return jnp.where(t == 0, self.y, self.x), jnp.where(t == 0, self.x, self.y)


class Gather:
    def __init__(self, place, buf, sems, base, direct):
        self.place, self.buf, self.sems, self.count, self.base = place, buf, sems, 0, base
        self.direct = direct
        half = ROW // 2
        low, high = pl.ds(0, half), pl.ds(half, half)
        s0, f0 = place.coords(place.zl)
        s1, f1 = place.coords(place.zo)
        m = {"z": self.make((place.zl, s0, f0), (place.zo, s1, f1), place.at(z=place.zo))}
        for r in (0, 1):
            t = place.zl if r == 0 else place.zo
            s, f = (s0, f0) if r == 0 else (s1, f1)
            sm, sp, s2 = (lax.rem(s + k, RING) for k in (3, 1, 2))
            fm, fp, f2 = (lax.rem(f + k, RING) for k in (3, 1, 2))
            up, down = place.first(t, 1), place.first(t, -1)
            m[r, "1+"] = self.make((t, s, f), (t, s, fm), up)
            m[r, "1-"] = self.make((t, s, f), (t, s, fp), down)
            if direct:
                m[r, "12"] = self.make((t, s, f), (t, s, f2), place.first(t, 2))
            else:
                m[r, "1f+"] = self.make((t, s, fm, low), (t, s, f2, low), up)
                m[r, "1f-"] = self.make((t, s, fp, high), (t, s, f2, high), down)
            up, down = place.second(t, 1), place.second(t, -1)
            for q, g in enumerate((f, fm, fp, f2)):
                m[r, q, "2+"] = self.make((t, s, g), (t, sm, g), up)
                m[r, q, "2-"] = self.make((t, s, g), (t, sp, g), down)
                m[r, q, "2f+"] = self.make((t, sm, g, low), (t, s2, g, low), up)
                m[r, q, "2f-"] = self.make((t, sp, g, high), (t, s2, g, high), down)
        self.m = m

    def make(self, src, landing, device):
        slot = self.base + self.count
        self.count += 1
        src = self.buf.at[src]
        return Message(src, src, self.buf.at[landing], self.sems, slot, device)

    def go(self, *keys):
        for key in keys:
            self.m[key].start()

    def ring(self, r):
        self.go((r, "1+"), (r, "1-"), *([(r, "12")] if self.direct else []), (r, 0, "2+"), (r, 0, "2-"))

    def begin(self):
        self.go("z")
        self.ring(0)

    def other(self):
        self.m["z"].arrived()
        self.ring(1)

    def near(self, r):
        self.m[r, "1+"].arrived()
        self.go(*([] if self.direct else [(r, "1f+")]), (r, 1, "2+"), (r, 1, "2-"))
        self.m[r, "1-"].arrived()
        self.go(*([] if self.direct else [(r, "1f-")]), (r, 2, "2+"), (r, 2, "2-"))

    def pass_on(self, r, *blocks):
        for q in blocks:
            self.m[r, q, "2+"].arrived()
            self.go((r, q, "2f+"))
            self.m[r, q, "2-"].arrived()
            self.go((r, q, "2f-"))

    def far(self, r):
        if self.direct:
            self.m[r, "12"].arrived()
        else:
            self.m[r, "1f+"].arrived()
            self.m[r, "1f-"].arrived()
        self.go((r, 3, "2+"), (r, 3, "2-"))

    def last(self, r):
        for q in range(4):
            self.m[r, q, "2f+"].arrived()
            self.m[r, q, "2f-"].arrived()

    def finish(self):
        for message in self.m.values():
            message.sent()


class StatGather:
    def __init__(self, place, buf, sems, base):
        s0, f0 = place.coords(place.zl)
        s1, f1 = place.coords(place.zo)
        src = buf.at[place.zl, s0, f0]
        self.z = Message(src, src, buf.at[place.zo, s1, f1], sems, base, place.at(z=place.zo))
        self.wide = ([], [])
        slot = base + 1
        for r in (0, 1):
            t = place.zl if r == 0 else place.zo
            src = buf.at[place.back(t, 0, 0)]
            for dx, dy in PLANE:
                self.wide[r].append(Message(src, src, buf.at[place.back(t, dx, dy)], sems, slot, place.plane(dx, dy)))
                slot += 1

    def begin(self):
        self.z.start()
        for message in self.wide[0]:
            message.start()

    def other(self):
        self.z.arrived()
        for message in self.wide[1]:
            message.start()

    def last(self):
        for message in (*self.wide[0], *self.wide[1]):
            message.arrived()

    def finish(self):
        for message in (self.z, *self.wide[0], *self.wide[1]):
            message.sent()


class Total:
    def __init__(self, place, rows, part, half_in, mid_out, mid_in, zed, done, sems, base, wide):
        self.place, self.part, self.half_in = place, part, half_in
        self.mid_out, self.mid_in, self.zed, self.done = mid_out, mid_in, zed, done
        self.half, self.piece = rows // 2, rows // 32
        c = place.c
        self.mine = place.y * RING + place.x
        self.z = place.d * 2 + place.zl
        sib = place.at(c=1 - c)
        slot = base
        self.core = []
        if not wide:
            away = part.at[self.span(1 - c)]
            self.core.append(Message(away, half_in, half_in, sems, slot, sib))
            slot += 1
        self.out, self.by_z, self.back = [], [], []
        here = done.at[self.span(c, self.mine)]
        for k, (dx, dy) in enumerate(PLANE):
            x, y = lax.rem(place.x + dx, RING), lax.rem(place.y + dy, RING)
            src = mid_out.at[pl.ds(pl.multiple_of((y * RING + x) * self.piece, 16), self.piece)]
            self.out.append(Message(src, mid_in.at[k], mid_in.at[k], sems, slot, place.plane(dx, dy)))
            x, y = lax.rem(place.x + RING - dx, RING), lax.rem(place.y + RING - dy, RING)
            landing = done.at[self.span(c, y * RING + x)]
            self.back.append(Message(here, here, landing, sems, slot + 1, place.plane(dx, dy)))
            slot += 2
            if wide:
                landing = done.at[self.span(1 - c, y * RING + x)]
                self.back.append(Message(here, here, landing, sems, slot, place.plane(dx, dy, 1 - c)))
                slot += 1
        for k in (1, 3, 2):
            to, of = lax.rem(self.z + k, 4), lax.rem(self.z + 4 - k, 4)
            src = zed.at[self.z]
            self.by_z.append(Message(src, src, zed.at[of], sems, slot, place.at(d=to // 2, z=lax.rem(to, 2))))
            slot += 1
        self.across = []
        if wide:
            self.back.append(Message(here, here, done.at[self.span(1 - c, self.mine)], sems, slot, sib))
        else:
            src = done.at[self.span(c)]
            self.across.append(Message(src, src, done.at[self.span(1 - c)], sems, slot, sib))

    def span(self, c, piece=None):
        if piece is None:
            return pl.ds(pl.multiple_of(c * self.half, 16), self.half)
        return pl.ds(pl.multiple_of(c * self.half + piece * self.piece, 16), self.piece)

    def begin(self):
        self.core[0].start()

    def scatter(self, both=None):
        mine = self.span(self.place.c)
        if both is None:
            self.core[0].arrived()
            both = self.part[mine] + self.half_in[...]
        self.part[mine] = both
        self.mid_out[...] = both.astype(BF16)
        for message in self.out:
            message.start()

    def along_z(self):
        total = self.part[self.span(self.place.c, self.mine)]
        for k, message in enumerate(self.out):
            message.arrived()
            total = total + self.mid_in[k].astype(F32)
        self.zed[self.z] = total
        for message in self.by_z:
            message.start()

    def spread(self):
        for message in self.by_z:
            message.arrived()
        total = (self.zed[0] + self.zed[1]) + (self.zed[2] + self.zed[3])
        self.done[self.span(self.place.c, self.mine)] = total.astype(BF16)
        for message in self.back:
            message.start()

    def swap(self):
        for message in self.back:
            message.arrived()
        for message in self.across:
            message.start()

    def last(self):
        for message in self.across:
            message.arrived()

    def finish(self):
        for message in (*self.core, *self.out, *self.by_z, *self.back, *self.across):
            message.sent()


def total_scratch(rows):
    return [
        pltpu.VMEM((rows // 2, 128), F32),
        pltpu.VMEM((rows // 2, 128), BF16),
        pltpu.VMEM((15, rows // 32, 128), BF16),
        pltpu.VMEM((4, rows // 32, 128), F32),
    ]


def head_mask(shape, h):
    lane = lax.broadcasted_iota(jnp.int32, shape, len(shape) - 1)
    return jnp.logical_and(lane >= h * HDIM, lane < (h + 1) * HDIM)


def stack_heads(ref, half, rows):
    for pair in range(2):
        cols = rows[:, pair * 128 : (pair + 1) * 128]
        for h in range(2):
            start = (pair * 4 + half * 2 + h) * ROW
            ref[start : start + ROW] = jnp.where(head_mask(cols.shape, h), cols, jnp.zeros_like(cols))


def unstack_heads(ref, half):
    out = []
    for pair in range(2):
        start = (pair * 4 + half * 2) * ROW
        first, second = ref[start : start + ROW], ref[start + ROW : start + 2 * ROW]
        out.append(jnp.where(head_mask((ROW, 128), 0), first, second))
    return jnp.concatenate(out, axis=1)


def moved(rows, step):
    n = rows.shape[0]
    index = lax.broadcasted_iota(jnp.int32, rows.shape, 0)
    if step == 1:
        return jnp.where(index == n - 1, 0.0, pltpu.roll(rows, n - 1, 0))
    return jnp.where(index == 0, 0.0, pltpu.roll(rows, 1, 0))


def kernel(
    feat, wqkv, wout, wconv, go,
    gf, rest_done, qkv_done,
    feats, grads, stats, sib_feat, sib_grad, fine, sides,
    keys, values, queries, qm, dm,
    even, odd, low_w0, low_g0, low_w1, low_g1, acc_a, acc_b,
    run_m, run_l, run_d, tri_out, tri_in,
    part_out, part_in, kept, pair_out, pair_in, gone_out, gone_in, ghid, glow, gproj, hid,
    wide, *rest,
):
    rest_total = (odd.at[pl.ds(4 * SLOT, REST_ROWS)], *rest[:4], rest_done)
    qkv_total = (odd.at[pl.ds(5 * SLOT, QKV_ROWS)], *rest[4:8], qkv_done)
    send, recv, greet = rest[8:]
    sems = (send, recv)
    place = Place()
    c, s, zl = place.c, place.s, place.zl
    sib = place.at(c=1 - c)
    above, below = place.line(-1), place.line(1)

    base = 0
    fg = Gather(place, feats, sems, base, True)
    base += AG_MSGS
    dg = Gather(place, grads, sems, base, False)
    base += AG_MSGS
    sg = StatGather(place, stats, sems, base)
    base += ST_MSGS
    rest_sum = Total(place, REST_ROWS, *rest_total, sems, base, False)
    base += RS_MSGS
    qkv_sum = Total(place, QKV_ROWS, *qkv_total, sems, base, True)
    base += WIDE_MSGS
    sib_f = Message(feat, sib_feat, sib_feat, sems, base, sib)
    down_fine = Message(go.at[1], fine.at[0], fine.at[0], sems, base + 1, below)
    up_fine = Message(go.at[0], fine.at[1], fine.at[1], sems, base + 2, above)
    s0, f0 = place.coords(zl)
    own = (zl, s0, f0)
    sib_g = Message(grads.at[own], sib_grad, sib_grad, sems, base + 3, sib)
    tri = Message(tri_out, tri_in, tri_in, sems, base + 4, sib)
    parts = Message(part_out, part_in, part_in, sems, base + 5, sib)
    pairs = Message(pair_out, pair_in, pair_in, sems, base + 8, sib)
    final_rows = Message(gone_out, gone_in, gone_in, sems, base + 9, sib)

    def scaled_queries(rows):
        whole = nn(rows, wqkv[:, :CH]).astype(BF16)
        return (whole.astype(F32) * (1.0 / math.sqrt(HDIM))).astype(BF16)

    def stack_keys(rows, half):
        whole = nn(rows, wqkv[:, CH:]).astype(BF16)
        stack_heads(qm, half, whole[:, :CH])
        stack_heads(dm, half, whole[:, CH:])

    barrier = pltpu.get_barrier_semaphore()
    peers = [sib, place.at(z=place.zo), above, below]
    peers += [place.ring_x(k) for k in (1, 2, 3)] + [place.ring_y(k) for k in (1, 2, 3)]
    next_z = place.at(d=1 - place.d, z=place.zo)
    peers.append(next_z)
    for peer in peers:
        pl.semaphore_signal(barrier, inc=1, device_id=peer, device_id_type=MESH)

    def split(rows):
        wide[...] = rows.astype(F32)
        return wide[pl.ds(0, ROW, stride=2)], wide[pl.ds(1, ROW, stride=2)]

    def pack(*cells):
        return jnp.concatenate(cells, axis=1).astype(BF16)

    def taps(lines, a):
        w0, w1, w2 = wconv[3 * a], wconv[3 * a + 1], wconv[3 * a + 2]
        main = nt(lines, jnp.concatenate([w1, w0], axis=1)) + nt(lines, jnp.concatenate([w2, w1], axis=1))
        return main, nt(lines[:, :CO], w0), nt(lines[:, CO:], w2)

    feats[own] = feat[...]
    pl.semaphore_wait(barrier, len(peers))
    pl.semaphore_signal(greet, inc=1, device_id=next_z, device_id_type=MESH)
    down_fine.start()
    up_fine.start()
    fg.begin()
    sib_f.start()

    stack_heads(qm, 0, scaled_queries(feat[...]))
    own_lines = []
    for r in (0, 1):
        even_cells, odd_cells = split(go[r])
        sides[1 + r] = pack(even_cells, odd_cells, moved(even_cells, 1), moved(odd_cells, -1))
        own_lines.append(pack(even_cells, odd_cells))
    middle = taps(jnp.concatenate(own_lines, axis=0), 1)
    local = [
        m[:ROW] + m[ROW:] + f + l for m, f, l in zip(middle, taps(own_lines[1], 0), taps(own_lines[0], 2), strict=True)
    ]
    run_m[...] = jnp.full((STACK, 128), -1e30, F32)
    run_l[...] = jnp.zeros((STACK, 128), F32)
    run_d[...] = jnp.zeros((STACK, 128), F32)
    odd[:SLOT] = jnp.full((SLOT, 128), -1e30, F32)
    odd[SLOT : 2 * SLOT] = jnp.zeros((SLOT, 128), F32)

    def clear():
        for ref in (acc_a, acc_b):
            ref[...] = jnp.zeros((STACK, 128), F32)
        for ref in (low_w1, low_g1):
            ref[...] = jnp.zeros((PAIR, CHUNK), BF16)

    clear()

    fg.other()
    fg.near(0)
    fg.far(0)
    fg.pass_on(0, 0)

    down_fine.arrived()
    up_fine.arrived()
    outer = []
    for r, inside in ((0, s > 0), (1, s < 63)):
        even_cells, odd_cells = (jnp.where(inside, cells, 0.0) for cells in split(fine[r]))
        sides[3 * r] = pack(even_cells, odd_cells, moved(even_cells, 1), moved(odd_cells, -1))
        outer.append(pack(even_cells, odd_cells))
    top, bottom = outer
    main, plus, minus = (m + f + l for m, f, l in zip(local, taps(bottom, 0), taps(top, 2), strict=True))
    hidden_grad = main + moved(plus, 1) + moved(minus, -1)
    ghid[...] = hidden_grad
    hidden_low = hidden_grad.astype(BF16)
    glow[...] = hidden_low
    own_grad = nt(hidden_low, wout[...]).astype(BF16)
    grads[own] = own_grad
    sib_g.start()
    dg.begin()

    stack_heads(dm, 0, own_grad)
    sib_f.arrived()
    stack_heads(qm, 1, scaled_queries(sib_feat[...]))
    sib_g.arrived()
    stack_heads(dm, 1, sib_grad[...])

    def where_is(j):
        t = jnp.where((j == 1) | (j > 4), place.zo, zl)
        far = (j == 4) | (j == 7)
        offset = jnp.where(j < 2, 0, jnp.where(far, 2, jnp.where((j == 2) | (j == 5), 3, 1)))
        second, _ = place.coords(t)
        return t, lax.rem(second + offset, RING)

    def steps(jj, p, acts):
        for when, act in acts.items():
            if when % 2 == p:
                pl.when(jj == when // 2)(act)

    holds = (even, odd)
    lows = ((low_w0, low_g0), (low_w1, low_g1))

    def tile_at(slot, b, first, count):
        return pl.ds(pl.multiple_of(slot * SLOT + b * STACK + first, SUB), count)

    def put(ref, slot, pair, product):
        for b in range(RING):
            ref[tile_at(slot, b, pair * PAIR, PAIR)] = product[:, b * 128 : (b + 1) * 128]

    def statistics(ref, slot, pair):
        for i in range(PAIR // SUB):
            first = pair * PAIR + i * SUB
            span = slice(first, first + SUB)
            sc = [ref[tile_at(slot, b, first, SUB)] for b in range(RING)]
            old = run_m[span]
            new = jnp.maximum(jnp.maximum(jnp.maximum(sc[0], sc[1]), jnp.maximum(sc[2], sc[3])), old)
            shrink = jnp.exp(old - new)
            total, dot = run_l[span] * shrink, run_d[span] * shrink
            for b in range(RING):
                w = jnp.exp(sc[b] - new)
                total = total + w
                dot = dot + w * ref[tile_at(slot + 1, b, first, SUB)]
            run_m[span] = new
            run_l[span] = total
            run_d[span] = dot

    def f1():
        fg.near(1)
        fg.far(1)
        fg.pass_on(1, 0)

    def f2():
        fg.pass_on(0, 1, 2, 3)
        dg.other()

    def f3():
        dg.near(0)
        dg.pass_on(0, 0)

    def f4():
        fg.pass_on(1, 1, 2)
        fg.last(0)

    def f5():
        fg.pass_on(1, 3)
        dg.near(1)
        dg.pass_on(1, 0)

    def f6():
        dg.far(0)
        dg.pass_on(0, 1, 2)

    def f7():
        fg.last(1)
        dg.far(1)

    def first_pass(jj, skip):
        for p in (0, 1):
            j = 2 * jj + p
            steps(jj, p, {1: f1, 2: f2, 3: f3, 4: f4, 5: f5, 6: f6, 7: f7})
            t, second = where_is(j)
            block = feats[t, second].reshape(CHUNK, CH)
            whole = nn(block, wqkv[...]).astype(BF16)
            queries[j] = (whole[:, :CH].astype(F32) * (1.0 / math.sqrt(HDIM))).astype(BF16)
            keys[j] = whole[:, CH : 2 * CH]
            values[j] = whole[:, 2 * CH :]
            for pair in range(2):
                rows = slice(pair * PAIR, (pair + 1) * PAIR)
                first = CH + pair * 128
                put(holds[p], 2 * jj, pair, nt(qm[rows], whole[:, first : first + 128]))
                put(holds[p], 2 * jj + 1, pair, nt(dm[rows], whole[:, first + CH : first + CH + 128]))
                if p == 1:
                    statistics(even, 2 * jj, pair)
                else:
                    statistics(odd, jnp.maximum(2 * jj - 2, 0), pair)
        return skip

    lax.fori_loop(0, CHUNKS // 2, first_pass, 0)
    for pair in range(2):
        statistics(odd, CHUNKS - 2, pair)

    lane = lax.broadcasted_iota(jnp.int32, (ROW, 128), 1)
    mine = [jnp.zeros((ROW, 128), F32), jnp.ones((ROW, 128), F32), jnp.zeros((ROW, 128), F32)]
    theirs = list(mine)
    for half in (0, 1):
        for h in range(HEADS):
            g = half * HEADS + h
            start = ((h // 2) * 4 + half * 2 + h % 2) * ROW
            span = slice(start, start + ROW)
            m = run_m[span]
            top = jnp.max(m, axis=1, keepdims=True)
            e = jnp.exp(m - top)
            cols = [
                top,
                jnp.sum(run_l[span] * e, axis=1, keepdims=True),
                jnp.sum(run_d[span] * e, axis=1, keepdims=True),
            ]
            for k in range(3):
                mine[k] = jnp.where(lane == g, cols[k], mine[k])
                theirs[k] = jnp.where(lane == (1 - half) * HEADS + h, cols[k], theirs[k])
    for k in range(3):
        tri_out[k] = theirs[k]
    tri.start()
    stack_keys(feat[...], 0)
    stack_keys(sib_feat[...], 1)
    tri.arrived()
    top = jnp.maximum(mine[0], tri_in[0])
    ea, eb = jnp.exp(mine[0] - top), jnp.exp(tri_in[0] - top)
    total = mine[1] * ea + tri_in[1] * eb
    delta = (mine[2] * ea + tri_in[2] * eb) / total
    lse = top + jnp.log(total)
    stats[own] = jnp.concatenate([jnp.transpose(lse)[:HEADS], jnp.transpose(delta)[:HEADS]], axis=0)
    sg.begin()
    for g in range(2 * HEADS):
        half, h = g // HEADS, g % HEADS
        start = ((h // 2) * 4 + half * 2 + h % 2) * ROW
        span = slice(start, start + ROW)
        run_m[span] = jnp.broadcast_to(lse[:, g : g + 1], (ROW, 128))
        run_l[span] = jnp.broadcast_to(delta[:, g : g + 1], (ROW, 128))

    def weights_of(ref, p_slot, pair):
        low_w, low_g = lows[pair]
        for i in range(PAIR // SUB):
            first = pair * PAIR + i * SUB
            to = slice(i * SUB, (i + 1) * SUB)
            lse_t, delta_t = run_m[first : first + SUB], run_l[first : first + SUB]
            for b in range(RING):
                w = jnp.exp(ref[tile_at(p_slot, b, first, SUB)] - lse_t)
                low_w[to, b * 128 : (b + 1) * 128] = w.astype(BF16)
                low_g[to, b * 128 : (b + 1) * 128] = (
                    w * (ref[tile_at(p_slot + 1, b, first, SUB)] - delta_t)
                ).astype(BF16)

    def add_products(pair, with_w, with_g):
        low_w, low_g = lows[pair]
        rows = slice(pair * PAIR, (pair + 1) * PAIR)
        acc_a[rows] += nn(low_w[...], with_w)
        acc_b[rows] += nn(low_g[...], with_g)

    def columns(pair):
        return slice(pair * 128, (pair + 1) * 128)

    def p0():
        dg.pass_on(1, 1, 2)

    def p1():
        dg.pass_on(0, 3)

    def p2():
        sg.other()

    def p3():
        dg.pass_on(1, 3)

    def forward(jj, skip):
        for p in (0, 1):
            j = 2 * jj + p
            steps(jj, p, {0: p0, 1: p1, 2: p2, 3: p3})
            before = jnp.maximum(j - 1, 0)
            add_products(1, values[before, :, columns(1)], keys[before, :, columns(1)])
            weights_of(holds[p], 2 * jj, 0)
            add_products(0, values[j, :, columns(0)], keys[j, :, columns(0)])
            weights_of(holds[p], 2 * jj, 1)
        return skip

    lax.fori_loop(0, CHUNKS // 2, forward, 0)
    add_products(1, values[CHUNKS - 1, :, columns(1)], keys[CHUNKS - 1, :, columns(1)])
    part_out[0] = unstack_heads(acc_a, 1)
    part_out[1] = unstack_heads(acc_b, 1)
    parts.start()
    kept[0] = unstack_heads(acc_a, 0)
    kept[1] = unstack_heads(acc_b, 0)
    clear()

    def attended_rows():
        parts.arrived()
        attended = (kept[0] + part_in[0]).astype(BF16)
        gproj[:, :CH] = ((kept[1] + part_in[1]) * (1.0 / math.sqrt(HDIM))).astype(BF16)
        hid[...] = (feat[...].astype(F32) + nn(attended, wout[...])).astype(BF16)
        out_part = tn(attended, glow[...])
        part = rest_sum.part
        part[2304:2560] = out_part[:, :128]
        part[2560:2816] = out_part[:, 128:]
        query_part = tn(feat[...], gproj[:, :CH])
        part[2816:3072] = query_part[:, :128]
        part[3072:3328] = query_part[:, 128:]
        part[3328:] = jnp.zeros((REST_ROWS - 3328, 128), F32)

    def conv_rows():
        mid = hid[...]
        met = [tn(mid, sides[r]) for r in range(4)]
        part = rest_sum.part
        for a, whole in enumerate((met[2] + met[3], met[1] + met[2], met[0] + met[1])):
            even_c, odd_c, even1, odd1 = (whole[:, k * CO : (k + 1) * CO] for k in range(4))
            part[(3 * a) * CH : (3 * a + 1) * CH] = even1 + odd_c
            part[(3 * a + 1) * CH : (3 * a + 2) * CH] = even_c + odd_c
            part[(3 * a + 2) * CH : (3 * a + 3) * CH] = even_c + odd1
        rest_sum.begin()

    def block_of(j):
        t, second = where_is(j)
        return grads[t, second].reshape(CHUNK, CH)

    def transposed_scores(j, p, pair):
        rows = slice(pair * PAIR, (pair + 1) * PAIR)
        put(holds[p], 0, pair, nt(qm[rows], queries[j, :, columns(pair)]))
        put(holds[p], 1, pair, nt(dm[rows], block_of(j)[:, columns(pair)]))

    def transposed_weights(j, p, pair):
        low_w, low_g = lows[pair]
        t, second = where_is(j)
        for part in range(4):
            h = 2 * pair + part % 2
            for i in range(ROW // SUB):
                first = part * ROW + i * SUB
                to = slice(first, first + SUB)
                for b in range(RING):
                    w = jnp.exp(holds[p][tile_at(0, b, pair * PAIR + first, SUB)] - stats[t, second, b, h : h + 1, :])
                    low_w[to, b * 128 : (b + 1) * 128] = w.astype(BF16)
                    low_g[to, b * 128 : (b + 1) * 128] = (
                        w * (holds[p][tile_at(1, b, pair * PAIR + first, SUB)] - stats[t, second, b, HEADS + h : HEADS + h + 1, :])
                    ).astype(BF16)

    def first_sums():
        attended_rows()
        conv_rows()

    def before_four():
        dg.last(0)

    def backward(jj, skip, final=False):
        for p in (0, 1):
            j = 2 * jj + p
            if final and p == 0:
                dg.last(1)
            if final and p == 1:
                rest_sum.along_z()
            if not final:
                steps(jj, p, {0: first_sums, 2: rest_sum.scatter, 3: before_four})
            before = jnp.maximum(j - 1, 0)
            more = not (final and p == 1)
            if more:
                transposed_scores(j + 1, 1 - p, 0)
            add_products(1, block_of(before)[:, columns(1)], queries[before, :, columns(1)])
            transposed_weights(j, p, 0)
            if more:
                transposed_scores(j + 1, 1 - p, 1)
            add_products(0, block_of(j)[:, columns(0)], queries[j, :, columns(0)])
            transposed_weights(j, p, 1)
        return skip

    pl.semaphore_wait(greet, 1)
    transposed_scores(0, 0, 0)
    transposed_scores(0, 0, 1)
    sg.last()
    lax.fori_loop(0, CHUNKS // 2 - 1, backward, 0)
    backward(CHUNKS // 2 - 1, 0, True)
    add_products(1, block_of(CHUNKS - 1)[:, columns(1)], queries[CHUNKS - 1, :, columns(1)])
    first_core = c == 0
    own_part = []
    for half in (0, 1):
        gk, gv = unstack_heads(acc_b, half), unstack_heads(acc_a, half)
        pair_out[1 - half] = jnp.where(first_core, gv, gk)
        own_part.append(jnp.where(first_core, gk, gv))
    pairs.start()
    pairs.arrived()
    done_rows = [(own_part[half] + pair_in[half]).astype(BF16) for half in (0, 1)]
    gone_out[...] = done_rows[1]
    final_rows.start()
    qkv_part = tn(jnp.concatenate([feat[...], sib_feat[...]], axis=0), jnp.concatenate(done_rows, axis=0))
    qkv_sum.scatter(jnp.concatenate([qkv_part[:, :128], qkv_part[:, 128:]], axis=0))
    final_rows.arrived()
    gproj[:, CH : 2 * CH] = jnp.where(first_core, done_rows[0], gone_in[...])
    gproj[:, 2 * CH :] = jnp.where(first_core, gone_in[...], done_rows[0])
    gf[...] = ghid[...] + nt(gproj[...], wqkv[...])
    rest_sum.spread()
    qkv_sum.along_z()
    qkv_sum.spread()
    rest_sum.swap()
    qkv_sum.swap()
    rest_sum.last()

    for group in (fg, dg, sg, rest_sum, qkv_sum):
        group.finish()
    for message in (sib_f, down_fine, up_fine, sib_g, tri, parts, pairs, final_rows):
        message.sent()


def scale_out(gf_in, rest, qkv, gf, gqkv, gout, gconv):
    coarse = 1.0 / math.sqrt(2 * 64 * ROW)
    fine_scale = 1.0 / math.sqrt(2 * 128 * 256)
    gf[...] = gf_in[...]
    gconv[...] = rest[:2304].astype(F32) * fine_scale
    for k in range(2):
        gout[:, k * 128 : (k + 1) * 128] = rest[2304 + k * CH : 2304 + (k + 1) * CH].astype(F32) * coarse
        gqkv[:, k * 128 : (k + 1) * 128] = rest[2816 + k * CH : 2816 + (k + 1) * CH].astype(F32) * coarse
    for k in range(4):
        gqkv[:, CH + k * 128 : CH + (k + 1) * 128] = qkv[k * CH : (k + 1) * CH].astype(F32) * coarse


def shards(features, qkv_weight, out_weight, conv_weight, grad_output):
    messages = 2 * AG_MSGS + ST_MSGS + RS_MSGS + WIDE_MSGS + 10
    whole = pl.BlockSpec(memory_space=pltpu.VMEM)
    sums = pl.pallas_call(
        kernel,
        out_shape=[
            jax.ShapeDtypeStruct((ROW, CH), F32),
            jax.ShapeDtypeStruct((REST_ROWS, 128), BF16),
            jax.ShapeDtypeStruct((QKV_ROWS, 128), BF16),
        ],
        in_specs=[whole] * 5,
        out_specs=[whole] * 3,
        scratch_shapes=[
            pltpu.VMEM((2, RING, RING, ROW, CH), BF16),
            pltpu.VMEM((2, RING, RING, ROW, CH), BF16),
            pltpu.VMEM((2, RING, RING, 2 * HEADS, ROW), F32),
            pltpu.VMEM((ROW, CH), BF16),
            pltpu.VMEM((ROW, CH), BF16),
            pltpu.VMEM((2, 2 * ROW, CO), BF16),
            pltpu.VMEM((4, ROW, 4 * CO), BF16),
            pltpu.VMEM((CHUNKS, CHUNK, CH), BF16),
            pltpu.VMEM((CHUNKS, CHUNK, CH), BF16),
            pltpu.VMEM((CHUNKS, CHUNK, CH), BF16),
            pltpu.VMEM((STACK, 128), BF16),
            pltpu.VMEM((STACK, 128), BF16),
            pltpu.VMEM((CHUNKS * SLOT, 128), F32),
            pltpu.VMEM((CHUNKS * SLOT, 128), F32),
            pltpu.VMEM((PAIR, CHUNK), BF16),
            pltpu.VMEM((PAIR, CHUNK), BF16),
            pltpu.VMEM((PAIR, CHUNK), BF16),
            pltpu.VMEM((PAIR, CHUNK), BF16),
            pltpu.VMEM((STACK, 128), F32),
            pltpu.VMEM((STACK, 128), F32),
            pltpu.VMEM((STACK, 128), F32),
            pltpu.VMEM((STACK, 128), F32),
            pltpu.VMEM((STACK, 128), F32),
            pltpu.VMEM((3, ROW, 128), F32),
            pltpu.VMEM((3, ROW, 128), F32),
            pltpu.VMEM((2, ROW, CH), F32),
            pltpu.VMEM((2, ROW, CH), F32),
            pltpu.VMEM((2, ROW, CH), F32),
            pltpu.VMEM((2, ROW, CH), F32),
            pltpu.VMEM((2, ROW, CH), F32),
            pltpu.VMEM((ROW, CH), BF16),
            pltpu.VMEM((ROW, CH), BF16),
            pltpu.VMEM((ROW, CH), F32),
            pltpu.VMEM((ROW, CH), BF16),
            pltpu.VMEM((ROW, 3 * CH), BF16),
            pltpu.VMEM((ROW, CH), BF16),
            pltpu.VMEM((2 * ROW, CO), F32),
            *total_scratch(REST_ROWS),
            *total_scratch(QKV_ROWS),
            pltpu.SemaphoreType.DMA((messages,)),
            pltpu.SemaphoreType.DMA((messages,)),
            pltpu.SemaphoreType.REGULAR,
        ],
        compiler_params=pltpu.CompilerParams(
            collective_id=0, has_side_effects=True, vmem_limit_bytes=63 * 1024 * 1024
        ),
    )(
        features.reshape(ROW, CH),
        qkv_weight,
        out_weight,
        conv_weight.reshape(9, CH, CO),
        grad_output.reshape(2, 2 * ROW, CO),
    )
    gf, gqkv, gout, gconv = pl.pallas_call(
        scale_out,
        out_shape=[
            jax.ShapeDtypeStruct((ROW, CH), F32),
            jax.ShapeDtypeStruct((CH, 3 * CH), F32),
            jax.ShapeDtypeStruct((CH, CH), F32),
            jax.ShapeDtypeStruct((9 * CH, CO), F32),
        ],
        in_specs=[whole] * 3,
        out_specs=[whole] * 4,
        compiler_params=pltpu.CompilerParams(vmem_limit_bytes=62 * 1024 * 1024),
    )(*sums)
    return (
        gf.reshape(1, 1, ROW, CH),
        gqkv,
        gout,
        gconv.reshape(3, 3, CH, CO),
    )


def solution(mesh):
    in_specs = (P("dp", "space", None, None), P(), P(), P(), P("dp", "space", None, None))
    out_specs = (P("dp", "space", None, None), P(), P(), P())
    return jax.shard_map(shards, mesh=mesh, in_specs=in_specs, out_specs=out_specs, check_vma=False)
```

```python
import math

import jax
import jax.numpy as jnp
from jax import lax
from jax.experimental import pallas as pl
from jax.experimental.pallas import tpu as pltpu
from jax.sharding import PartitionSpec as P

MESH = pl.DeviceIdType.MESH
F32 = jnp.float32
BF16 = jnp.bfloat16
HDIM = 64
HEADS = 4
CH = 256
CO = 128
ROW = 128
RING = 4
CHUNK = RING * ROW
CHUNKS = 8
STACK = 2 * HEADS * ROW
PAIR = STACK // 2
SUB = 32
SLOT = RING * STACK
REST_ROWS = 3584
QKV_ROWS = 1024
PLANE = sorted([(k % 4, k // 4) for k in range(1, 16)], key=lambda step: -sum(min(d, 4 - d) for d in step))
AG_MSGS = 41
ST_MSGS = 31
RS_MSGS = 35
WIDE_MSGS = 49


def nt(a, b):
    return lax.dot_general(a, b, (((1,), (1,)), ((), ())), preferred_element_type=F32)


def tn(a, b):
    return lax.dot_general(a, b, (((0,), (0,)), ((), ())), preferred_element_type=F32)


def nn(a, b):
    return jnp.dot(a, b, preferred_element_type=F32)


class Message:
    def __init__(self, src, dst, landing, sems, slot, device):
        send, recv = sems
        self.out = pltpu.make_async_remote_copy(
            src_ref=src, dst_ref=dst, send_sem=send.at[slot], recv_sem=recv.at[slot], device_id=device, device_id_type=MESH
        )
        self.into = pltpu.make_async_remote_copy(
            src_ref=landing, dst_ref=landing, send_sem=send.at[slot], recv_sem=recv.at[slot], device_id=device, device_id_type=MESH
        )

    def start(self):
        self.out.start()

    def arrived(self):
        self.into.wait_recv()

    def sent(self):
        self.out.wait_send()


class Place:
    def __init__(self):
        self.d = lax.axis_index("dp")
        self.s = lax.axis_index("space")
        s = self.s
        self.c = lax.rem(s, 2)
        self.x = lax.rem(s // 2, RING)
        self.zl = lax.rem(s // 8, 2)
        self.y = s // 16
        self.zo = 1 - self.zl

    def at(self, d=None, y=None, z=None, x=None, c=None):
        d = self.d if d is None else d
        y = self.y if y is None else y
        z = self.zl if z is None else z
        x = self.x if x is None else x
        c = self.c if c is None else c
        return (d, ((y * 2 + z) * RING + x) * 2 + c)

    def line(self, step):
        return (self.d, lax.rem(self.s + step + 64, 64))

    def ring_x(self, step):
        return self.at(x=lax.rem(self.x + step + RING, RING))

    def ring_y(self, step):
        return self.at(y=lax.rem(self.y + step + RING, RING))

    def plane(self, dx, dy, c=None):
        return self.at(x=lax.rem(self.x + dx + RING, RING), y=lax.rem(self.y + dy + RING, RING), c=c)

    def back(self, t, dx, dy):
        x, y = lax.rem(self.x + RING - dx, RING), lax.rem(self.y + RING - dy, RING)
        return t, jnp.where(t == 0, y, x), jnp.where(t == 0, x, y)

    def first(self, t, step):
        hit = t == 0
        return self.at(
            x=jnp.where(hit, lax.rem(self.x + step + RING, RING), self.x),
            y=jnp.where(hit, self.y, lax.rem(self.y + step + RING, RING)),
        )

    def second(self, t, step):
        return self.first(1 - t, step)

    def coords(self, t):
        return jnp.where(t == 0, self.y, self.x), jnp.where(t == 0, self.x, self.y)


class Gather:
    def __init__(self, place, buf, sems, base, direct):
        self.place, self.buf, self.sems, self.count, self.base = place, buf, sems, 0, base
        self.direct = direct
        half = ROW // 2
        low, high = pl.ds(0, half), pl.ds(half, half)
        s0, f0 = place.coords(place.zl)
        s1, f1 = place.coords(place.zo)
        m = {"z": self.make((place.zl, s0, f0), (place.zo, s1, f1), place.at(z=place.zo))}
        for r in (0, 1):
            t = place.zl if r == 0 else place.zo
            s, f = (s0, f0) if r == 0 else (s1, f1)
            sm, sp, s2 = (lax.rem(s + k, RING) for k in (3, 1, 2))
            fm, fp, f2 = (lax.rem(f + k, RING) for k in (3, 1, 2))
            up, down = place.first(t, 1), place.first(t, -1)
            m[r, "1+"] = self.make((t, s, f), (t, s, fm), up)
            m[r, "1-"] = self.make((t, s, f), (t, s, fp), down)
            if direct:
                m[r, "12"] = self.make((t, s, f), (t, s, f2), place.first(t, 2))
            else:
                m[r, "1f+"] = self.make((t, s, fm, low), (t, s, f2, low), up)
                m[r, "1f-"] = self.make((t, s, fp, high), (t, s, f2, high), down)
            up, down = place.second(t, 1), place.second(t, -1)
            for q, g in enumerate((f, fm, fp, f2)):
                m[r, q, "2+"] = self.make((t, s, g), (t, sm, g), up)
                m[r, q, "2-"] = self.make((t, s, g), (t, sp, g), down)
                m[r, q, "2f+"] = self.make((t, sm, g, low), (t, s2, g, low), up)
                m[r, q, "2f-"] = self.make((t, sp, g, high), (t, s2, g, high), down)
        self.m = m

    def make(self, src, landing, device):
        slot = self.base + self.count
        self.count += 1
        src = self.buf.at[src]
        return Message(src, src, self.buf.at[landing], self.sems, slot, device)

    def go(self, *keys):
        for key in keys:
            self.m[key].start()

    def ring(self, r):
        self.go((r, "1+"), (r, "1-"), *([(r, "12")] if self.direct else []), (r, 0, "2+"), (r, 0, "2-"))

    def begin(self):
        self.go("z")
        self.ring(0)

    def other(self):
        self.m["z"].arrived()
        self.ring(1)

    def near(self, r):
        self.m[r, "1+"].arrived()
        self.go(*([] if self.direct else [(r, "1f+")]), (r, 1, "2+"), (r, 1, "2-"))
        self.m[r, "1-"].arrived()
        self.go(*([] if self.direct else [(r, "1f-")]), (r, 2, "2+"), (r, 2, "2-"))

    def pass_on(self, r, *blocks):
        for q in blocks:
            self.m[r, q, "2+"].arrived()
            self.go((r, q, "2f+"))
            self.m[r, q, "2-"].arrived()
            self.go((r, q, "2f-"))

    def far(self, r):
        if self.direct:
            self.m[r, "12"].arrived()
        else:
            self.m[r, "1f+"].arrived()
            self.m[r, "1f-"].arrived()
        self.go((r, 3, "2+"), (r, 3, "2-"))

    def last(self, r):
        for q in range(4):
            self.m[r, q, "2f+"].arrived()
            self.m[r, q, "2f-"].arrived()

    def finish(self):
        for message in self.m.values():
            message.sent()


class StatGather:
    def __init__(self, place, buf, sems, base):
        s0, f0 = place.coords(place.zl)
        s1, f1 = place.coords(place.zo)
        src = buf.at[place.zl, s0, f0]
        self.z = Message(src, src, buf.at[place.zo, s1, f1], sems, base, place.at(z=place.zo))
        self.wide = ([], [])
        slot = base + 1
        for r in (0, 1):
            t = place.zl if r == 0 else place.zo
            src = buf.at[place.back(t, 0, 0)]
            for dx, dy in PLANE:
                self.wide[r].append(Message(src, src, buf.at[place.back(t, dx, dy)], sems, slot, place.plane(dx, dy)))
                slot += 1

    def begin(self):
        self.z.start()
        for message in self.wide[0]:
            message.start()

    def other(self):
        self.z.arrived()
        for message in self.wide[1]:
            message.start()

    def last(self):
        for message in (*self.wide[0], *self.wide[1]):
            message.arrived()

    def finish(self):
        for message in (self.z, *self.wide[0], *self.wide[1]):
            message.sent()


class Total:
    def __init__(self, place, rows, part, half_in, mid_out, mid_in, zed, done, sems, base, wide):
        self.place, self.part, self.half_in = place, part, half_in
        self.mid_out, self.mid_in, self.zed, self.done = mid_out, mid_in, zed, done
        self.half, self.piece = rows // 2, rows // 32
        c = place.c
        self.mine = place.y * RING + place.x
        self.z = place.d * 2 + place.zl
        sib = place.at(c=1 - c)
        slot = base
        self.core = []
        if not wide:
            away = part.at[self.span(1 - c)]
            self.core.append(Message(away, half_in, half_in, sems, slot, sib))
            slot += 1
        self.out, self.by_z, self.back = [], [], []
        here = done.at[self.span(c, self.mine)]
        for k, (dx, dy) in enumerate(PLANE):
            x, y = lax.rem(place.x + dx, RING), lax.rem(place.y + dy, RING)
            src = mid_out.at[pl.ds(pl.multiple_of((y * RING + x) * self.piece, 16), self.piece)]
            self.out.append(Message(src, mid_in.at[k], mid_in.at[k], sems, slot, place.plane(dx, dy)))
            x, y = lax.rem(place.x + RING - dx, RING), lax.rem(place.y + RING - dy, RING)
            landing = done.at[self.span(c, y * RING + x)]
            self.back.append(Message(here, here, landing, sems, slot + 1, place.plane(dx, dy)))
            slot += 2
            if wide:
                landing = done.at[self.span(1 - c, y * RING + x)]
                self.back.append(Message(here, here, landing, sems, slot, place.plane(dx, dy, 1 - c)))
                slot += 1
        for k in (1, 3, 2):
            to, of = lax.rem(self.z + k, 4), lax.rem(self.z + 4 - k, 4)
            src = zed.at[self.z]
            self.by_z.append(Message(src, src, zed.at[of], sems, slot, place.at(d=to // 2, z=lax.rem(to, 2))))
            slot += 1
        self.across = []
        if wide:
            self.back.append(Message(here, here, done.at[self.span(1 - c, self.mine)], sems, slot, sib))
        else:
            src = done.at[self.span(c)]
            self.across.append(Message(src, src, done.at[self.span(1 - c)], sems, slot, sib))

    def span(self, c, piece=None):
        if piece is None:
            return pl.ds(pl.multiple_of(c * self.half, 16), self.half)
        return pl.ds(pl.multiple_of(c * self.half + piece * self.piece, 16), self.piece)

    def begin(self):
        self.core[0].start()

    def scatter(self, both=None):
        mine = self.span(self.place.c)
        if both is None:
            self.core[0].arrived()
            both = self.part[mine] + self.half_in[...]
        self.part[mine] = both
        self.mid_out[...] = both.astype(BF16)
        for message in self.out:
            message.start()

    def along_z(self):
        total = self.part[self.span(self.place.c, self.mine)]
        for k, message in enumerate(self.out):
            message.arrived()
            total = total + self.mid_in[k].astype(F32)
        self.zed[self.z] = total
        for message in self.by_z:
            message.start()

    def spread(self):
        for message in self.by_z:
            message.arrived()
        total = (self.zed[0] + self.zed[1]) + (self.zed[2] + self.zed[3])
        self.done[self.span(self.place.c, self.mine)] = total.astype(BF16)
        for message in self.back:
            message.start()

    def swap(self):
        for message in self.back:
            message.arrived()
        for message in self.across:
            message.start()

    def last(self):
        for message in self.across:
            message.arrived()

    def finish(self):
        for message in (*self.core, *self.out, *self.by_z, *self.back, *self.across):
            message.sent()


def total_scratch(rows):
    return [
        pltpu.VMEM((rows // 2, 128), F32),
        pltpu.VMEM((rows // 2, 128), BF16),
        pltpu.VMEM((15, rows // 32, 128), BF16),
        pltpu.VMEM((4, rows // 32, 128), F32),
    ]


def head_mask(shape, h):
    lane = lax.broadcasted_iota(jnp.int32, shape, len(shape) - 1)
    return jnp.logical_and(lane >= h * HDIM, lane < (h + 1) * HDIM)


def stack_heads(ref, half, rows):
    for pair in range(2):
        cols = rows[:, pair * 128 : (pair + 1) * 128]
        for h in range(2):
            start = (pair * 4 + half * 2 + h) * ROW
            ref[start : start + ROW] = jnp.where(head_mask(cols.shape, h), cols, jnp.zeros_like(cols))


def unstack_heads(ref, half):
    out = []
    for pair in range(2):
        start = (pair * 4 + half * 2) * ROW
        first, second = ref[start : start + ROW], ref[start + ROW : start + 2 * ROW]
        out.append(jnp.where(head_mask((ROW, 128), 0), first, second))
    return jnp.concatenate(out, axis=1)


def moved(rows, step):
    n = rows.shape[0]
    index = lax.broadcasted_iota(jnp.int32, rows.shape, 0)
    if step == 1:
        return jnp.where(index == n - 1, 0.0, pltpu.roll(rows, n - 1, 0))
    return jnp.where(index == 0, 0.0, pltpu.roll(rows, 1, 0))


def kernel(
    feat, wqkv, wout, wconv, go,
    gf, rest_done, qkv_done,
    feats, grads, stats, sib_feat, sib_grad, fine, sides,
    keys, values, queries, qm, dm,
    even, odd, low_w0, low_g0, low_w1, low_g1, acc_a, acc_b,
    run_m, run_l, run_d, tri_out, tri_in,
    part_out, part_in, kept, pair_out, pair_in, gone_out, gone_in, ghid, glow, gproj, hid,
    wide, *rest,
):
    rest_total = (odd.at[pl.ds(4 * SLOT, REST_ROWS)], *rest[:4], rest_done)
    qkv_total = (odd.at[pl.ds(5 * SLOT, QKV_ROWS)], *rest[4:8], qkv_done)
    send, recv, greet = rest[8:]
    sems = (send, recv)
    place = Place()
    c, s, zl = place.c, place.s, place.zl
    sib = place.at(c=1 - c)
    above, below = place.line(-1), place.line(1)

    base = 0
    fg = Gather(place, feats, sems, base, True)
    base += AG_MSGS
    dg = Gather(place, grads, sems, base, False)
    base += AG_MSGS
    sg = StatGather(place, stats, sems, base)
    base += ST_MSGS
    rest_sum = Total(place, REST_ROWS, *rest_total, sems, base, False)
    base += RS_MSGS
    qkv_sum = Total(place, QKV_ROWS, *qkv_total, sems, base, True)
    base += WIDE_MSGS
    sib_f = Message(feat, sib_feat, sib_feat, sems, base, sib)
    down_fine = Message(go.at[1], fine.at[0], fine.at[0], sems, base + 1, below)
    up_fine = Message(go.at[0], fine.at[1], fine.at[1], sems, base + 2, above)
    s0, f0 = place.coords(zl)
    own = (zl, s0, f0)
    sib_g = Message(grads.at[own], sib_grad, sib_grad, sems, base + 3, sib)
    tri = Message(tri_out, tri_in, tri_in, sems, base + 4, sib)
    parts = Message(part_out, part_in, part_in, sems, base + 5, sib)
    pairs = Message(pair_out, pair_in, pair_in, sems, base + 8, sib)
    final_rows = Message(gone_out, gone_in, gone_in, sems, base + 9, sib)

    def scaled_queries(rows):
        whole = nn(rows, wqkv[:, :CH]).astype(BF16)
        return (whole.astype(F32) * (1.0 / math.sqrt(HDIM))).astype(BF16)

    def stack_keys(rows, half):
        whole = nn(rows, wqkv[:, CH:]).astype(BF16)
        stack_heads(qm, half, whole[:, :CH])
        stack_heads(dm, half, whole[:, CH:])

    barrier = pltpu.get_barrier_semaphore()
    peers = [sib, place.at(z=place.zo), above, below]
    peers += [place.ring_x(k) for k in (1, 2, 3)] + [place.ring_y(k) for k in (1, 2, 3)]
    next_z = place.at(d=1 - place.d, z=place.zo)
    peers.append(next_z)
    for peer in peers:
        pl.semaphore_signal(barrier, inc=1, device_id=peer, device_id_type=MESH)

    def split(rows):
        wide[...] = rows.astype(F32)
        return wide[pl.ds(0, ROW, stride=2)], wide[pl.ds(1, ROW, stride=2)]

    def pack(*cells):
        return jnp.concatenate(cells, axis=1).astype(BF16)

    def side(r):
        return slice(r * 4 * CO, (r + 1) * 4 * CO)

    def taps(lines, a):
        w0, w1, w2 = wconv[3 * a], wconv[3 * a + 1], wconv[3 * a + 2]
        main = nt(lines, jnp.concatenate([w1, w0], axis=1)) + nt(lines, jnp.concatenate([w2, w1], axis=1))
        return main, nt(lines[:, :CO], w0), nt(lines[:, CO:], w2)

    feats[own] = feat[...]
    pl.semaphore_wait(barrier, len(peers))
    pl.semaphore_signal(greet, inc=1, device_id=next_z, device_id_type=MESH)
    down_fine.start()
    up_fine.start()
    fg.begin()
    sib_f.start()

    stack_heads(qm, 0, scaled_queries(feat[...]))
    own_lines = []
    for r in (0, 1):
        even_cells, odd_cells = split(go[r])
        sides[:, side(1 + r)] = pack(even_cells, odd_cells, moved(even_cells, 1), moved(odd_cells, -1))
        own_lines.append(pack(even_cells, odd_cells))
    middle = taps(jnp.concatenate(own_lines, axis=0), 1)
    local = [
        m[:ROW] + m[ROW:] + f + l for m, f, l in zip(middle, taps(own_lines[1], 0), taps(own_lines[0], 2), strict=True)
    ]
    run_m[...] = jnp.full((STACK, 128), -1e30, F32)
    run_l[...] = jnp.zeros((STACK, 128), F32)
    run_d[...] = jnp.zeros((STACK, 128), F32)
    odd[:SLOT] = jnp.full((SLOT, 128), -1e30, F32)
    odd[SLOT : 2 * SLOT] = jnp.zeros((SLOT, 128), F32)

    def clear():
        for ref in (acc_a, acc_b):
            ref[...] = jnp.zeros((STACK, 128), F32)
        for ref in (low_w1, low_g1):
            ref[...] = jnp.zeros((PAIR, CHUNK), BF16)

    clear()

    fg.other()
    fg.near(0)
    fg.far(0)
    fg.pass_on(0, 0)

    down_fine.arrived()
    up_fine.arrived()
    outer = []
    for r, inside in ((0, s > 0), (1, s < 63)):
        even_cells, odd_cells = (jnp.where(inside, cells, 0.0) for cells in split(fine[r]))
        sides[:, side(3 * r)] = pack(even_cells, odd_cells, moved(even_cells, 1), moved(odd_cells, -1))
        outer.append(pack(even_cells, odd_cells))
    top, bottom = outer
    main, plus, minus = (m + f + l for m, f, l in zip(local, taps(bottom, 0), taps(top, 2), strict=True))
    hidden_grad = main + moved(plus, 1) + moved(minus, -1)
    ghid[...] = hidden_grad
    hidden_low = hidden_grad.astype(BF16)
    glow[...] = hidden_low
    own_grad = nt(hidden_low, wout[...]).astype(BF16)
    grads[own] = own_grad
    sib_g.start()
    dg.begin()

    stack_heads(dm, 0, own_grad)
    sib_f.arrived()
    stack_heads(qm, 1, scaled_queries(sib_feat[...]))
    sib_g.arrived()
    stack_heads(dm, 1, sib_grad[...])

    def where_is(j):
        t = jnp.where((j == 1) | (j > 4), place.zo, zl)
        far = (j == 4) | (j == 7)
        offset = jnp.where(j < 2, 0, jnp.where(far, 2, jnp.where((j == 2) | (j == 5), 3, 1)))
        second, _ = place.coords(t)
        return t, lax.rem(second + offset, RING)

    def steps(jj, p, acts):
        for when, act in acts.items():
            if when % 2 == p:
                pl.when(jj == when // 2)(act)

    holds = (even, odd)
    lows = ((low_w0, low_g0), (low_w1, low_g1))

    def tile_at(slot, b, first, count):
        return pl.ds(pl.multiple_of(slot * SLOT + b * STACK + first, SUB), count)

    def put(ref, slot, pair, product):
        for b in range(RING):
            ref[tile_at(slot, b, pair * PAIR, PAIR)] = product[:, b * 128 : (b + 1) * 128]

    def statistics(ref, slot, pair):
        for i in range(PAIR // SUB):
            first = pair * PAIR + i * SUB
            span = slice(first, first + SUB)
            sc = [ref[tile_at(slot, b, first, SUB)] for b in range(RING)]
            old = run_m[span]
            new = jnp.maximum(jnp.maximum(jnp.maximum(sc[0], sc[1]), jnp.maximum(sc[2], sc[3])), old)
            shrink = jnp.exp(old - new)
            total, dot = run_l[span] * shrink, run_d[span] * shrink
            for b in range(RING):
                w = jnp.exp(sc[b] - new)
                total = total + w
                dot = dot + w * ref[tile_at(slot + 1, b, first, SUB)]
            run_m[span] = new
            run_l[span] = total
            run_d[span] = dot

    def f1():
        fg.near(1)
        fg.far(1)
        fg.pass_on(1, 0)

    def f2():
        fg.pass_on(0, 1, 2, 3)
        dg.other()

    def f3():
        dg.near(0)
        dg.pass_on(0, 0)

    def f4():
        fg.pass_on(1, 1, 2)
        fg.last(0)

    def f5():
        fg.pass_on(1, 3)
        dg.near(1)
        dg.pass_on(1, 0)

    def f6():
        dg.far(0)
        dg.pass_on(0, 1, 2)

    def f7():
        fg.last(1)
        dg.far(1)

    def first_pass(jj, skip):
        for p in (0, 1):
            j = 2 * jj + p
            steps(jj, p, {1: f1, 2: f2, 3: f3, 4: f4, 5: f5, 6: f6, 7: f7})
            t, second = where_is(j)
            block = feats[t, second].reshape(CHUNK, CH)
            whole = nn(block, wqkv[...]).astype(BF16)
            queries[j] = (whole[:, :CH].astype(F32) * (1.0 / math.sqrt(HDIM))).astype(BF16)
            keys[j] = whole[:, CH : 2 * CH]
            values[j] = whole[:, 2 * CH :]
            for pair in range(2):
                rows = slice(pair * PAIR, (pair + 1) * PAIR)
                first = CH + pair * 128
                put(holds[p], 2 * jj, pair, nt(qm[rows], whole[:, first : first + 128]))
                put(holds[p], 2 * jj + 1, pair, nt(dm[rows], whole[:, first + CH : first + CH + 128]))
                if p == 1:
                    statistics(even, 2 * jj, pair)
                else:
                    statistics(odd, jnp.maximum(2 * jj - 2, 0), pair)
        return skip

    lax.fori_loop(0, CHUNKS // 2, first_pass, 0)
    for pair in range(2):
        statistics(odd, CHUNKS - 2, pair)

    lane = lax.broadcasted_iota(jnp.int32, (ROW, 128), 1)
    mine = [jnp.zeros((ROW, 128), F32), jnp.ones((ROW, 128), F32), jnp.zeros((ROW, 128), F32)]
    theirs = list(mine)
    for half in (0, 1):
        for h in range(HEADS):
            g = half * HEADS + h
            start = ((h // 2) * 4 + half * 2 + h % 2) * ROW
            span = slice(start, start + ROW)
            m = run_m[span]
            top = jnp.max(m, axis=1, keepdims=True)
            e = jnp.exp(m - top)
            cols = [
                top,
                jnp.sum(run_l[span] * e, axis=1, keepdims=True),
                jnp.sum(run_d[span] * e, axis=1, keepdims=True),
            ]
            for k in range(3):
                mine[k] = jnp.where(lane == g, cols[k], mine[k])
                theirs[k] = jnp.where(lane == (1 - half) * HEADS + h, cols[k], theirs[k])
    for k in range(3):
        tri_out[k] = theirs[k]
    tri.start()
    stack_keys(feat[...], 0)
    stack_keys(sib_feat[...], 1)
    tri.arrived()
    top = jnp.maximum(mine[0], tri_in[0])
    ea, eb = jnp.exp(mine[0] - top), jnp.exp(tri_in[0] - top)
    total = mine[1] * ea + tri_in[1] * eb
    delta = (mine[2] * ea + tri_in[2] * eb) / total
    lse = top + jnp.log(total)
    stats[own] = jnp.concatenate([jnp.transpose(lse)[:HEADS], jnp.transpose(delta)[:HEADS]], axis=0)
    sg.begin()
    for g in range(2 * HEADS):
        half, h = g // HEADS, g % HEADS
        start = ((h // 2) * 4 + half * 2 + h % 2) * ROW
        span = slice(start, start + ROW)
        run_m[span] = jnp.broadcast_to(lse[:, g : g + 1], (ROW, 128))
        run_l[span] = jnp.broadcast_to(delta[:, g : g + 1], (ROW, 128))

    def weights_of(ref, p_slot, pair):
        low_w, low_g = lows[pair]
        for i in range(PAIR // SUB):
            first = pair * PAIR + i * SUB
            to = slice(i * SUB, (i + 1) * SUB)
            lse_t, delta_t = run_m[first : first + SUB], run_l[first : first + SUB]
            for b in range(RING):
                w = jnp.exp(ref[tile_at(p_slot, b, first, SUB)] - lse_t)
                low_w[to, b * 128 : (b + 1) * 128] = w.astype(BF16)
                low_g[to, b * 128 : (b + 1) * 128] = (
                    w * (ref[tile_at(p_slot + 1, b, first, SUB)] - delta_t)
                ).astype(BF16)

    def add_products(pair, with_w, with_g):
        low_w, low_g = lows[pair]
        rows = slice(pair * PAIR, (pair + 1) * PAIR)
        acc_a[rows] += nn(low_w[...], with_w)
        acc_b[rows] += nn(low_g[...], with_g)

    def columns(pair):
        return slice(pair * 128, (pair + 1) * 128)

    def p0():
        dg.pass_on(1, 1, 2)

    def p1():
        dg.pass_on(0, 3)

    def p2():
        sg.other()

    def p3():
        dg.pass_on(1, 3)

    def forward(jj, skip):
        for p in (0, 1):
            j = 2 * jj + p
            steps(jj, p, {0: p0, 1: p1, 2: p2, 3: p3})
            before = jnp.maximum(j - 1, 0)
            add_products(1, values[before, :, columns(1)], keys[before, :, columns(1)])
            weights_of(holds[p], 2 * jj, 0)
            add_products(0, values[j, :, columns(0)], keys[j, :, columns(0)])
            weights_of(holds[p], 2 * jj, 1)
        return skip

    lax.fori_loop(0, CHUNKS // 2, forward, 0)
    add_products(1, values[CHUNKS - 1, :, columns(1)], keys[CHUNKS - 1, :, columns(1)])
    part_out[0] = unstack_heads(acc_a, 1)
    part_out[1] = unstack_heads(acc_b, 1)
    parts.start()
    kept[0] = unstack_heads(acc_a, 0)
    kept[1] = unstack_heads(acc_b, 0)
    clear()

    def attended_rows():
        parts.arrived()
        attended = (kept[0] + part_in[0]).astype(BF16)
        gproj[:, :CH] = ((kept[1] + part_in[1]) * (1.0 / math.sqrt(HDIM))).astype(BF16)
        hid[...] = (feat[...].astype(F32) + nn(attended, wout[...])).astype(BF16)
        out_part = tn(attended, glow[...])
        part = rest_sum.part
        part[2304:2560] = out_part[:, :128]
        part[2560:2816] = out_part[:, 128:]
        query_part = tn(feat[...], gproj[:, :CH])
        part[2816:3072] = query_part[:, :128]
        part[3072:3328] = query_part[:, 128:]
        part[3328:] = jnp.zeros((REST_ROWS - 3328, 128), F32)

    def conv_rows():
        mid = hid[...]
        every = tn(mid, sides[...])
        met = [every[:, side(r)] for r in range(4)]
        part = rest_sum.part
        for a, whole in enumerate((met[2] + met[3], met[1] + met[2], met[0] + met[1])):
            even_c, odd_c, even1, odd1 = (whole[:, k * CO : (k + 1) * CO] for k in range(4))
            part[(3 * a) * CH : (3 * a + 1) * CH] = even1 + odd_c
            part[(3 * a + 1) * CH : (3 * a + 2) * CH] = even_c + odd_c
            part[(3 * a + 2) * CH : (3 * a + 3) * CH] = even_c + odd1
        rest_sum.begin()

    def block_of(j):
        t, second = where_is(j)
        return grads[t, second].reshape(CHUNK, CH)

    def transposed_scores(j, p, pair):
        rows = slice(pair * PAIR, (pair + 1) * PAIR)
        put(holds[p], 0, pair, nt(qm[rows], queries[j, :, columns(pair)]))
        put(holds[p], 1, pair, nt(dm[rows], block_of(j)[:, columns(pair)]))

    def transposed_weights(j, p, pair):
        low_w, low_g = lows[pair]
        t, second = where_is(j)
        for part in range(4):
            h = 2 * pair + part % 2
            for i in range(ROW // SUB):
                first = part * ROW + i * SUB
                to = slice(first, first + SUB)
                for b in range(RING):
                    w = jnp.exp(holds[p][tile_at(0, b, pair * PAIR + first, SUB)] - stats[t, second, b, h : h + 1, :])
                    low_w[to, b * 128 : (b + 1) * 128] = w.astype(BF16)
                    low_g[to, b * 128 : (b + 1) * 128] = (
                        w * (holds[p][tile_at(1, b, pair * PAIR + first, SUB)] - stats[t, second, b, HEADS + h : HEADS + h + 1, :])
                    ).astype(BF16)

    def first_sums():
        attended_rows()
        conv_rows()

    def before_four():
        dg.last(0)

    def backward(jj, skip, final=False):
        for p in (0, 1):
            j = 2 * jj + p
            if final and p == 0:
                dg.last(1)
            if not final:
                steps(jj, p, {0: first_sums, 2: rest_sum.scatter, 3: before_four})
            before = jnp.maximum(j - 1, 0)
            more = not (final and p == 1)
            if more:
                transposed_scores(j + 1, 1 - p, 0)
            add_products(1, block_of(before)[:, columns(1)], queries[before, :, columns(1)])
            transposed_weights(j, p, 0)
            if more:
                transposed_scores(j + 1, 1 - p, 1)
            add_products(0, block_of(j)[:, columns(0)], queries[j, :, columns(0)])
            transposed_weights(j, p, 1)
        return skip

    pl.semaphore_wait(greet, 1)
    transposed_scores(0, 0, 0)
    transposed_scores(0, 0, 1)
    sg.last()
    lax.fori_loop(0, CHUNKS // 2 - 1, backward, 0)
    backward(CHUNKS // 2 - 1, 0, True)
    add_products(1, block_of(CHUNKS - 1)[:, columns(1)], queries[CHUNKS - 1, :, columns(1)])
    first_core = c == 0
    own_part = []
    for half in (0, 1):
        gk, gv = unstack_heads(acc_b, half), unstack_heads(acc_a, half)
        pair_out[1 - half] = jnp.where(first_core, gv, gk)
        own_part.append(jnp.where(first_core, gk, gv))
    pairs.start()
    rest_sum.along_z()
    pairs.arrived()
    done_rows = [(own_part[half] + pair_in[half]).astype(BF16) for half in (0, 1)]
    gone_out[...] = done_rows[1]
    final_rows.start()
    qkv_part = tn(jnp.concatenate([feat[...], sib_feat[...]], axis=0), jnp.concatenate(done_rows, axis=0))
    qkv_sum.scatter(jnp.concatenate([qkv_part[:, :128], qkv_part[:, 128:]], axis=0))
    final_rows.arrived()
    gproj[:, CH : 2 * CH] = jnp.where(first_core, done_rows[0], gone_in[...])
    gproj[:, 2 * CH :] = jnp.where(first_core, gone_in[...], done_rows[0])
    gf[...] = ghid[...] + nt(gproj[...], wqkv[...])
    rest_sum.spread()
    qkv_sum.along_z()
    qkv_sum.spread()
    rest_sum.swap()
    qkv_sum.swap()
    rest_sum.last()

    for group in (fg, dg, sg, rest_sum, qkv_sum):
        group.finish()
    for message in (sib_f, down_fine, up_fine, sib_g, tri, parts, pairs, final_rows):
        message.sent()


def scale_out(gf_in, rest, qkv, gf, gqkv, gout, gconv):
    coarse = 1.0 / math.sqrt(2 * 64 * ROW)
    fine_scale = 1.0 / math.sqrt(2 * 128 * 256)
    gf[...] = gf_in[...]
    gconv[...] = rest[:2304].astype(F32) * fine_scale
    for k in range(2):
        gout[:, k * 128 : (k + 1) * 128] = rest[2304 + k * CH : 2304 + (k + 1) * CH].astype(F32) * coarse
        gqkv[:, k * 128 : (k + 1) * 128] = rest[2816 + k * CH : 2816 + (k + 1) * CH].astype(F32) * coarse
    for k in range(4):
        gqkv[:, CH + k * 128 : CH + (k + 1) * 128] = qkv[k * CH : (k + 1) * CH].astype(F32) * coarse


def shards(features, qkv_weight, out_weight, conv_weight, grad_output):
    messages = 2 * AG_MSGS + ST_MSGS + RS_MSGS + WIDE_MSGS + 10
    whole = pl.BlockSpec(memory_space=pltpu.VMEM)
    sums = pl.pallas_call(
        kernel,
        out_shape=[
            jax.ShapeDtypeStruct((ROW, CH), F32),
            jax.ShapeDtypeStruct((REST_ROWS, 128), BF16),
            jax.ShapeDtypeStruct((QKV_ROWS, 128), BF16),
        ],
        in_specs=[whole] * 5,
        out_specs=[whole] * 3,
        scratch_shapes=[
            pltpu.VMEM((2, RING, RING, ROW, CH), BF16),
            pltpu.VMEM((2, RING, RING, ROW, CH), BF16),
            pltpu.VMEM((2, RING, RING, 2 * HEADS, ROW), F32),
            pltpu.VMEM((ROW, CH), BF16),
            pltpu.VMEM((ROW, CH), BF16),
            pltpu.VMEM((2, 2 * ROW, CO), BF16),
            pltpu.VMEM((ROW, 16 * CO), BF16),
            pltpu.VMEM((CHUNKS, CHUNK, CH), BF16),
            pltpu.VMEM((CHUNKS, CHUNK, CH), BF16),
            pltpu.VMEM((CHUNKS, CHUNK, CH), BF16),
            pltpu.VMEM((STACK, 128), BF16),
            pltpu.VMEM((STACK, 128), BF16),
            pltpu.VMEM((CHUNKS * SLOT, 128), F32),
            pltpu.VMEM((CHUNKS * SLOT, 128), F32),
            pltpu.VMEM((PAIR, CHUNK), BF16),
            pltpu.VMEM((PAIR, CHUNK), BF16),
            pltpu.VMEM((PAIR, CHUNK), BF16),
            pltpu.VMEM((PAIR, CHUNK), BF16),
            pltpu.VMEM((STACK, 128), F32),
            pltpu.VMEM((STACK, 128), F32),
            pltpu.VMEM((STACK, 128), F32),
            pltpu.VMEM((STACK, 128), F32),
            pltpu.VMEM((STACK, 128), F32),
            pltpu.VMEM((3, ROW, 128), F32),
            pltpu.VMEM((3, ROW, 128), F32),
            pltpu.VMEM((2, ROW, CH), F32),
            pltpu.VMEM((2, ROW, CH), F32),
            pltpu.VMEM((2, ROW, CH), F32),
            pltpu.VMEM((2, ROW, CH), F32),
            pltpu.VMEM((2, ROW, CH), F32),
            pltpu.VMEM((ROW, CH), BF16),
            pltpu.VMEM((ROW, CH), BF16),
            pltpu.VMEM((ROW, CH), F32),
            pltpu.VMEM((ROW, CH), BF16),
            pltpu.VMEM((ROW, 3 * CH), BF16),
            pltpu.VMEM((ROW, CH), BF16),
            pltpu.VMEM((2 * ROW, CO), F32),
            *total_scratch(REST_ROWS),
            *total_scratch(QKV_ROWS),
            pltpu.SemaphoreType.DMA((messages,)),
            pltpu.SemaphoreType.DMA((messages,)),
            pltpu.SemaphoreType.REGULAR,
        ],
        compiler_params=pltpu.CompilerParams(
            collective_id=0, has_side_effects=True, vmem_limit_bytes=63 * 1024 * 1024
        ),
    )(
        features.reshape(ROW, CH),
        qkv_weight,
        out_weight,
        conv_weight.reshape(9, CH, CO),
        grad_output.reshape(2, 2 * ROW, CO),
    )
    gf, gqkv, gout, gconv = pl.pallas_call(
        scale_out,
        out_shape=[
            jax.ShapeDtypeStruct((ROW, CH), F32),
            jax.ShapeDtypeStruct((CH, 3 * CH), F32),
            jax.ShapeDtypeStruct((CH, CH), F32),
            jax.ShapeDtypeStruct((9 * CH, CO), F32),
        ],
        in_specs=[whole] * 3,
        out_specs=[whole] * 4,
        compiler_params=pltpu.CompilerParams(vmem_limit_bytes=62 * 1024 * 1024),
    )(*sums)
    return (
        gf.reshape(1, 1, ROW, CH),
        gqkv,
        gout,
        gconv.reshape(3, 3, CH, CO),
    )


def solution(mesh):
    in_specs = (P("dp", "space", None, None), P(), P(), P(), P("dp", "space", None, None))
    out_specs = (P("dp", "space", None, None), P(), P(), P())
    return jax.shard_map(shards, mesh=mesh, in_specs=in_specs, out_specs=out_specs, check_vma=False)
```

```python
import math

import jax
import jax.numpy as jnp
from jax import lax
from jax.experimental import pallas as pl
from jax.experimental.pallas import tpu as pltpu
from jax.sharding import PartitionSpec as P

MESH = pl.DeviceIdType.MESH
F32 = jnp.float32
BF16 = jnp.bfloat16
HDIM = 64
HEADS = 4
CH = 256
CO = 128
ROW = 128
RING = 4
CHUNK = RING * ROW
CHUNKS = 8
STACK = 2 * HEADS * ROW
PAIR = STACK // 2
SUB = 32
SLOT = RING * STACK
REST_ROWS = 3584
QKV_ROWS = 1024
PLANE = sorted([(k % 4, k // 4) for k in range(1, 16)], key=lambda step: -sum(min(d, 4 - d) for d in step))
AG_MSGS = 41
ST_MSGS = 31
RS_MSGS = 35
WIDE_MSGS = 49


def nt(a, b):
    return lax.dot_general(a, b, (((1,), (1,)), ((), ())), preferred_element_type=F32)


def tn(a, b):
    return lax.dot_general(a, b, (((0,), (0,)), ((), ())), preferred_element_type=F32)


def nn(a, b):
    return jnp.dot(a, b, preferred_element_type=F32)


class Message:
    def __init__(self, src, dst, landing, sems, slot, device):
        send, recv = sems
        self.out = pltpu.make_async_remote_copy(
            src_ref=src, dst_ref=dst, send_sem=send.at[slot], recv_sem=recv.at[slot], device_id=device, device_id_type=MESH
        )
        self.into = pltpu.make_async_remote_copy(
            src_ref=landing, dst_ref=landing, send_sem=send.at[slot], recv_sem=recv.at[slot], device_id=device, device_id_type=MESH
        )

    def start(self):
        self.out.start()

    def arrived(self):
        self.into.wait_recv()

    def sent(self):
        self.out.wait_send()


class Place:
    def __init__(self):
        self.d = lax.axis_index("dp")
        self.s = lax.axis_index("space")
        s = self.s
        self.c = lax.rem(s, 2)
        self.x = lax.rem(s // 2, RING)
        self.zl = lax.rem(s // 8, 2)
        self.y = s // 16
        self.zo = 1 - self.zl

    def at(self, d=None, y=None, z=None, x=None, c=None):
        d = self.d if d is None else d
        y = self.y if y is None else y
        z = self.zl if z is None else z
        x = self.x if x is None else x
        c = self.c if c is None else c
        return (d, ((y * 2 + z) * RING + x) * 2 + c)

    def line(self, step):
        return (self.d, lax.rem(self.s + step + 64, 64))

    def ring_x(self, step):
        return self.at(x=lax.rem(self.x + step + RING, RING))

    def ring_y(self, step):
        return self.at(y=lax.rem(self.y + step + RING, RING))

    def plane(self, dx, dy, c=None):
        return self.at(x=lax.rem(self.x + dx + RING, RING), y=lax.rem(self.y + dy + RING, RING), c=c)

    def back(self, t, dx, dy):
        x, y = lax.rem(self.x + RING - dx, RING), lax.rem(self.y + RING - dy, RING)
        return t, jnp.where(t == 0, y, x), jnp.where(t == 0, x, y)

    def first(self, t, step):
        hit = t == 0
        return self.at(
            x=jnp.where(hit, lax.rem(self.x + step + RING, RING), self.x),
            y=jnp.where(hit, self.y, lax.rem(self.y + step + RING, RING)),
        )

    def second(self, t, step):
        return self.first(1 - t, step)

    def coords(self, t):
        return jnp.where(t == 0, self.y, self.x), jnp.where(t == 0, self.x, self.y)


class Gather:
    def __init__(self, place, buf, sems, base, direct):
        self.place, self.buf, self.sems, self.count, self.base = place, buf, sems, 0, base
        self.direct = direct
        half = ROW // 2
        low, high = pl.ds(0, half), pl.ds(half, half)
        s0, f0 = place.coords(place.zl)
        s1, f1 = place.coords(place.zo)
        m = {"z": self.make((place.zl, s0, f0), (place.zo, s1, f1), place.at(z=place.zo))}
        for r in (0, 1):
            t = place.zl if r == 0 else place.zo
            s, f = (s0, f0) if r == 0 else (s1, f1)
            sm, sp, s2 = (lax.rem(s + k, RING) for k in (3, 1, 2))
            fm, fp, f2 = (lax.rem(f + k, RING) for k in (3, 1, 2))
            up, down = place.first(t, 1), place.first(t, -1)
            m[r, "1+"] = self.make((t, s, f), (t, s, fm), up)
            m[r, "1-"] = self.make((t, s, f), (t, s, fp), down)
            if direct:
                m[r, "12"] = self.make((t, s, f), (t, s, f2), place.first(t, 2))
            else:
                m[r, "1f+"] = self.make((t, s, fm, low), (t, s, f2, low), up)
                m[r, "1f-"] = self.make((t, s, fp, high), (t, s, f2, high), down)
            up, down = place.second(t, 1), place.second(t, -1)
            for q, g in enumerate((f, fm, fp, f2)):
                m[r, q, "2+"] = self.make((t, s, g), (t, sm, g), up)
                m[r, q, "2-"] = self.make((t, s, g), (t, sp, g), down)
                m[r, q, "2f+"] = self.make((t, sm, g, low), (t, s2, g, low), up)
                m[r, q, "2f-"] = self.make((t, sp, g, high), (t, s2, g, high), down)
        self.m = m

    def make(self, src, landing, device):
        slot = self.base + self.count
        self.count += 1
        src = self.buf.at[src]
        return Message(src, src, self.buf.at[landing], self.sems, slot, device)

    def go(self, *keys):
        for key in keys:
            self.m[key].start()

    def ring(self, r):
        self.go((r, "1+"), (r, "1-"), *([(r, "12")] if self.direct else []), (r, 0, "2+"), (r, 0, "2-"))

    def begin(self):
        self.go("z")
        self.ring(0)

    def other(self):
        self.m["z"].arrived()
        self.ring(1)

    def near(self, r):
        self.m[r, "1+"].arrived()
        self.go(*([] if self.direct else [(r, "1f+")]), (r, 1, "2+"), (r, 1, "2-"))
        self.m[r, "1-"].arrived()
        self.go(*([] if self.direct else [(r, "1f-")]), (r, 2, "2+"), (r, 2, "2-"))

    def pass_on(self, r, *blocks):
        for q in blocks:
            self.m[r, q, "2+"].arrived()
            self.go((r, q, "2f+"))
            self.m[r, q, "2-"].arrived()
            self.go((r, q, "2f-"))

    def far(self, r):
        if self.direct:
            self.m[r, "12"].arrived()
        else:
            self.m[r, "1f+"].arrived()
            self.m[r, "1f-"].arrived()
        self.go((r, 3, "2+"), (r, 3, "2-"))

    def last(self, r):
        for q in range(4):
            self.m[r, q, "2f+"].arrived()
            self.m[r, q, "2f-"].arrived()

    def finish(self):
        for message in self.m.values():
            message.sent()


class StatGather:
    def __init__(self, place, buf, sems, base):
        s0, f0 = place.coords(place.zl)
        s1, f1 = place.coords(place.zo)
        src = buf.at[place.zl, s0, f0]
        self.z = Message(src, src, buf.at[place.zo, s1, f1], sems, base, place.at(z=place.zo))
        self.wide = ([], [])
        slot = base + 1
        for r in (0, 1):
            t = place.zl if r == 0 else place.zo
            src = buf.at[place.back(t, 0, 0)]
            for dx, dy in PLANE:
                self.wide[r].append(Message(src, src, buf.at[place.back(t, dx, dy)], sems, slot, place.plane(dx, dy)))
                slot += 1

    def begin(self):
        self.z.start()
        for message in self.wide[0]:
            message.start()

    def other(self):
        self.z.arrived()
        for message in self.wide[1]:
            message.start()

    def last(self):
        for message in (*self.wide[0], *self.wide[1]):
            message.arrived()

    def finish(self):
        for message in (self.z, *self.wide[0], *self.wide[1]):
            message.sent()


class Total:
    def __init__(self, place, rows, part, half_in, mid_out, mid_in, zed, done, sems, base, wide):
        self.place, self.part, self.half_in = place, part, half_in
        self.mid_out, self.mid_in, self.zed, self.done = mid_out, mid_in, zed, done
        self.half, self.piece = rows // 2, rows // 32
        c = place.c
        self.mine = place.y * RING + place.x
        self.z = place.d * 2 + place.zl
        sib = place.at(c=1 - c)
        slot = base
        self.core = []
        if not wide:
            away = part.at[self.span(1 - c)]
            self.core.append(Message(away, half_in, half_in, sems, slot, sib))
            slot += 1
        self.out, self.by_z, self.back = [], [], []
        here = done.at[self.span(c, self.mine)]
        for k, (dx, dy) in enumerate(PLANE):
            x, y = lax.rem(place.x + dx, RING), lax.rem(place.y + dy, RING)
            src = mid_out.at[pl.ds(pl.multiple_of((y * RING + x) * self.piece, 16), self.piece)]
            self.out.append(Message(src, mid_in.at[k], mid_in.at[k], sems, slot, place.plane(dx, dy)))
            x, y = lax.rem(place.x + RING - dx, RING), lax.rem(place.y + RING - dy, RING)
            landing = done.at[self.span(c, y * RING + x)]
            self.back.append(Message(here, here, landing, sems, slot + 1, place.plane(dx, dy)))
            slot += 2
            if wide:
                landing = done.at[self.span(1 - c, y * RING + x)]
                self.back.append(Message(here, here, landing, sems, slot, place.plane(dx, dy, 1 - c)))
                slot += 1
        for k in (1, 3, 2):
            to, of = lax.rem(self.z + k, 4), lax.rem(self.z + 4 - k, 4)
            src = zed.at[self.z]
            self.by_z.append(Message(src, src, zed.at[of], sems, slot, place.at(d=to // 2, z=lax.rem(to, 2))))
            slot += 1
        self.across = []
        if wide:
            self.back.append(Message(here, here, done.at[self.span(1 - c, self.mine)], sems, slot, sib))
        else:
            src = done.at[self.span(c)]
            self.across.append(Message(src, src, done.at[self.span(1 - c)], sems, slot, sib))

    def span(self, c, piece=None):
        if piece is None:
            return pl.ds(pl.multiple_of(c * self.half, 16), self.half)
        return pl.ds(pl.multiple_of(c * self.half + piece * self.piece, 16), self.piece)

    def begin(self):
        self.core[0].start()

    def scatter(self, both=None):
        mine = self.span(self.place.c)
        if both is None:
            self.core[0].arrived()
            both = self.part[mine] + self.half_in[...]
        self.part[mine] = both
        self.mid_out[...] = both.astype(BF16)
        for message in self.out:
            message.start()

    def along_z(self):
        total = self.part[self.span(self.place.c, self.mine)]
        for k, message in enumerate(self.out):
            message.arrived()
            total = total + self.mid_in[k].astype(F32)
        self.zed[self.z] = total
        for message in self.by_z:
            message.start()

    def spread(self):
        for message in self.by_z:
            message.arrived()
        total = (self.zed[0] + self.zed[1]) + (self.zed[2] + self.zed[3])
        self.done[self.span(self.place.c, self.mine)] = total.astype(BF16)
        for message in self.back:
            message.start()

    def swap(self):
        for message in self.back:
            message.arrived()
        for message in self.across:
            message.start()

    def last(self):
        for message in self.across:
            message.arrived()

    def finish(self):
        for message in (*self.core, *self.out, *self.by_z, *self.back, *self.across):
            message.sent()


def total_scratch(rows):
    return [
        pltpu.VMEM((rows // 2, 128), F32),
        pltpu.VMEM((rows // 2, 128), BF16),
        pltpu.VMEM((15, rows // 32, 128), BF16),
        pltpu.VMEM((4, rows // 32, 128), F32),
    ]


def head_mask(shape, h):
    lane = lax.broadcasted_iota(jnp.int32, shape, len(shape) - 1)
    return jnp.logical_and(lane >= h * HDIM, lane < (h + 1) * HDIM)


def stack_heads(ref, half, rows):
    for pair in range(2):
        cols = rows[:, pair * 128 : (pair + 1) * 128]
        for h in range(2):
            start = (pair * 4 + half * 2 + h) * ROW
            ref[start : start + ROW] = jnp.where(head_mask(cols.shape, h), cols, jnp.zeros_like(cols))


def unstack_heads(ref, half):
    out = []
    for pair in range(2):
        start = (pair * 4 + half * 2) * ROW
        first, second = ref[start : start + ROW], ref[start + ROW : start + 2 * ROW]
        out.append(jnp.where(head_mask((ROW, 128), 0), first, second))
    return jnp.concatenate(out, axis=1)


def moved(rows, step):
    n = rows.shape[0]
    index = lax.broadcasted_iota(jnp.int32, rows.shape, 0)
    if step == 1:
        return jnp.where(index == n - 1, 0.0, pltpu.roll(rows, n - 1, 0))
    return jnp.where(index == 0, 0.0, pltpu.roll(rows, 1, 0))


def kernel(
    feat, wqkv, wout, wconv, go,
    gf, rest_done, qkv_done,
    feats, grads, stats, sib_feat, sib_grad, fine, sides,
    keys, values, queries, qm, dm,
    even, odd, low_w0, low_g0, low_w1, low_g1, acc_a, acc_b,
    run_m, run_l, run_d, tri_out, tri_in,
    part_out, part_in, kept, pair_out, pair_in, gone_out, gone_in, ghid, glow, gproj, hid,
    wide, *rest,
):
    rest_total = (odd.at[pl.ds(4 * SLOT, REST_ROWS)], *rest[:4], rest_done)
    qkv_total = (odd.at[pl.ds(5 * SLOT, QKV_ROWS)], *rest[4:8], qkv_done)
    send, recv, greet = rest[8:]
    sems = (send, recv)
    place = Place()
    c, s, zl = place.c, place.s, place.zl
    sib = place.at(c=1 - c)
    above, below = place.line(-1), place.line(1)

    base = 0
    fg = Gather(place, feats, sems, base, True)
    base += AG_MSGS
    dg = Gather(place, grads, sems, base, False)
    base += AG_MSGS
    sg = StatGather(place, stats, sems, base)
    base += ST_MSGS
    rest_sum = Total(place, REST_ROWS, *rest_total, sems, base, False)
    base += RS_MSGS
    qkv_sum = Total(place, QKV_ROWS, *qkv_total, sems, base, True)
    base += WIDE_MSGS
    sib_f = Message(feat, sib_feat, sib_feat, sems, base, sib)
    down_fine = Message(go.at[1], fine.at[0], fine.at[0], sems, base + 1, below)
    up_fine = Message(go.at[0], fine.at[1], fine.at[1], sems, base + 2, above)
    s0, f0 = place.coords(zl)
    own = (zl, s0, f0)
    sib_g = Message(grads.at[own], sib_grad, sib_grad, sems, base + 3, sib)
    tri = Message(tri_out, tri_in, tri_in, sems, base + 4, sib)
    parts = Message(part_out, part_in, part_in, sems, base + 5, sib)
    pairs = Message(pair_out, pair_in, pair_in, sems, base + 8, sib)
    final_rows = Message(gone_out, gone_in, gone_in, sems, base + 9, sib)

    def scaled_queries(rows):
        whole = nn(rows, wqkv[:, :CH]).astype(BF16)
        return (whole.astype(F32) * (1.0 / math.sqrt(HDIM))).astype(BF16)

    def stack_keys(rows, half):
        whole = nn(rows, wqkv[:, CH:]).astype(BF16)
        stack_heads(qm, half, whole[:, :CH])
        stack_heads(dm, half, whole[:, CH:])

    barrier = pltpu.get_barrier_semaphore()
    peers = [sib, place.at(z=place.zo), above, below]
    peers += [place.ring_x(k) for k in (1, 2, 3)] + [place.ring_y(k) for k in (1, 2, 3)]
    next_z = place.at(d=1 - place.d, z=place.zo)
    peers.append(next_z)
    for peer in peers:
        pl.semaphore_signal(barrier, inc=1, device_id=peer, device_id_type=MESH)

    def split(rows):
        wide[: 2 * ROW] = rows.astype(F32)
        return wide[pl.ds(0, ROW, stride=2)], wide[pl.ds(1, ROW, stride=2)]

    def pack(*cells):
        return jnp.concatenate(cells, axis=1).astype(BF16)

    def side(r):
        return slice(r * 4 * CO, (r + 1) * 4 * CO)

    def taps(lines, a):
        w0, w1, w2 = wconv[3 * a], wconv[3 * a + 1], wconv[3 * a + 2]
        main = nt(lines, jnp.concatenate([w1, w0], axis=1)) + nt(lines, jnp.concatenate([w2, w1], axis=1))
        return main, nt(lines[:, :CO], w0), nt(lines[:, CO:], w2)

    feats[own] = feat[...]
    pl.semaphore_wait(barrier, len(peers))
    pl.semaphore_signal(greet, inc=1, device_id=next_z, device_id_type=MESH)
    down_fine.start()
    up_fine.start()
    fg.begin()
    sib_f.start()

    stack_heads(qm, 0, scaled_queries(feat[...]))
    own_lines = []
    for r in (0, 1):
        even_cells, odd_cells = split(go[r])
        sides[:, side(1 + r)] = pack(even_cells, odd_cells, moved(even_cells, 1), moved(odd_cells, -1))
        own_lines.append(pack(even_cells, odd_cells))
    middle = taps(jnp.concatenate(own_lines, axis=0), 1)
    local = [
        m[:ROW] + m[ROW:] + f + l for m, f, l in zip(middle, taps(own_lines[1], 0), taps(own_lines[0], 2), strict=True)
    ]
    run_m[...] = jnp.full((STACK, 128), -1e30, F32)
    run_l[...] = jnp.zeros((STACK, 128), F32)
    run_d[...] = jnp.zeros((STACK, 128), F32)
    odd[:SLOT] = jnp.full((SLOT, 128), -1e30, F32)
    odd[SLOT : 2 * SLOT] = jnp.zeros((SLOT, 128), F32)

    def clear():
        for ref in (acc_a, acc_b):
            ref[...] = jnp.zeros((STACK, 128), F32)
        for ref in (low_w1, low_g1):
            ref[...] = jnp.zeros((PAIR, CHUNK), BF16)

    clear()

    fg.other()
    fg.near(0)
    fg.far(0)
    fg.pass_on(0, 0)

    down_fine.arrived()
    up_fine.arrived()
    outer = []
    for r, inside in ((0, s > 0), (1, s < 63)):
        even_cells, odd_cells = (jnp.where(inside, cells, 0.0) for cells in split(fine[r]))
        sides[:, side(3 * r)] = pack(even_cells, odd_cells, moved(even_cells, 1), moved(odd_cells, -1))
        outer.append(pack(even_cells, odd_cells))
    top, bottom = outer
    main, plus, minus = (m + f + l for m, f, l in zip(local, taps(bottom, 0), taps(top, 2), strict=True))
    hidden_grad = main + moved(plus, 1) + moved(minus, -1)
    ghid[...] = hidden_grad
    hidden_low = hidden_grad.astype(BF16)
    glow[...] = hidden_low
    own_grad = nt(hidden_low, wout[...]).astype(BF16)
    grads[own] = own_grad
    sib_g.start()
    dg.begin()

    stack_heads(dm, 0, own_grad)
    sib_f.arrived()
    stack_heads(qm, 1, scaled_queries(sib_feat[...]))
    sib_g.arrived()
    stack_heads(dm, 1, sib_grad[...])

    def where_is(j):
        t = jnp.where((j == 1) | (j > 4), place.zo, zl)
        far = (j == 4) | (j == 7)
        offset = jnp.where(j < 2, 0, jnp.where(far, 2, jnp.where((j == 2) | (j == 5), 3, 1)))
        second, _ = place.coords(t)
        return t, lax.rem(second + offset, RING)

    def steps(jj, p, acts):
        for when, act in acts.items():
            if when % 2 == p:
                pl.when(jj == when // 2)(act)

    holds = (even, odd)
    lows = ((low_w0, low_g0), (low_w1, low_g1))

    def tile_at(slot, b, first, count):
        return pl.ds(pl.multiple_of(slot * SLOT + b * STACK + first, SUB), count)

    def put(ref, slot, pair, product):
        for b in range(RING):
            ref[tile_at(slot, b, pair * PAIR, PAIR)] = product[:, b * 128 : (b + 1) * 128]

    def statistics(ref, slot, pair):
        for i in range(PAIR // SUB):
            first = pair * PAIR + i * SUB
            span = slice(first, first + SUB)
            sc = [ref[tile_at(slot, b, first, SUB)] for b in range(RING)]
            old = run_m[span]
            new = jnp.maximum(jnp.maximum(jnp.maximum(sc[0], sc[1]), jnp.maximum(sc[2], sc[3])), old)
            shrink = jnp.exp(old - new)
            total, dot = run_l[span] * shrink, run_d[span] * shrink
            for b in range(RING):
                w = jnp.exp(sc[b] - new)
                total = total + w
                dot = dot + w * ref[tile_at(slot + 1, b, first, SUB)]
            run_m[span] = new
            run_l[span] = total
            run_d[span] = dot

    def f1():
        fg.near(1)
        fg.far(1)
        fg.pass_on(1, 0)

    def f2():
        fg.pass_on(0, 1, 2, 3)
        dg.other()

    def f3():
        dg.near(0)
        dg.pass_on(0, 0)

    def f4():
        fg.pass_on(1, 1, 2)
        fg.last(0)

    def f5():
        fg.pass_on(1, 3)
        dg.near(1)
        dg.pass_on(1, 0)

    def f6():
        dg.far(0)
        dg.pass_on(0, 1, 2)

    def f7():
        fg.last(1)
        dg.far(1)

    def first_pass(jj, skip):
        for p in (0, 1):
            j = 2 * jj + p
            steps(jj, p, {1: f1, 2: f2, 3: f3, 4: f4, 5: f5, 6: f6, 7: f7})
            t, second = where_is(j)
            block = feats[t, second].reshape(CHUNK, CH)
            whole = nn(block, wqkv[...]).astype(BF16)
            queries[j] = (whole[:, :CH].astype(F32) * (1.0 / math.sqrt(HDIM))).astype(BF16)
            keys[j] = whole[:, CH : 2 * CH]
            values[j] = whole[:, 2 * CH :]
            for pair in range(2):
                rows = slice(pair * PAIR, (pair + 1) * PAIR)
                first = CH + pair * 128
                put(holds[p], 2 * jj, pair, nt(qm[rows], whole[:, first : first + 128]))
                put(holds[p], 2 * jj + 1, pair, nt(dm[rows], whole[:, first + CH : first + CH + 128]))
                if p == 1:
                    statistics(even, 2 * jj, pair)
                else:
                    statistics(odd, jnp.maximum(2 * jj - 2, 0), pair)
        return skip

    lax.fori_loop(0, CHUNKS // 2, first_pass, 0)
    for pair in range(2):
        statistics(odd, CHUNKS - 2, pair)

    lane = lax.broadcasted_iota(jnp.int32, (ROW, 128), 1)
    mine = [jnp.zeros((ROW, 128), F32), jnp.ones((ROW, 128), F32), jnp.zeros((ROW, 128), F32)]
    theirs = list(mine)
    for half in (0, 1):
        for h in range(HEADS):
            g = half * HEADS + h
            start = ((h // 2) * 4 + half * 2 + h % 2) * ROW
            span = slice(start, start + ROW)
            m = run_m[span]
            top = jnp.max(m, axis=1, keepdims=True)
            e = jnp.exp(m - top)
            cols = [
                top,
                jnp.sum(run_l[span] * e, axis=1, keepdims=True),
                jnp.sum(run_d[span] * e, axis=1, keepdims=True),
            ]
            for k in range(3):
                mine[k] = jnp.where(lane == g, cols[k], mine[k])
                theirs[k] = jnp.where(lane == (1 - half) * HEADS + h, cols[k], theirs[k])
    for k in range(3):
        tri_out[k] = theirs[k]
    tri.start()
    stack_keys(feat[...], 0)
    stack_keys(sib_feat[...], 1)
    tri.arrived()
    top = jnp.maximum(mine[0], tri_in[0])
    ea, eb = jnp.exp(mine[0] - top), jnp.exp(tri_in[0] - top)
    total = mine[1] * ea + tri_in[1] * eb
    delta = (mine[2] * ea + tri_in[2] * eb) / total
    lse = top + jnp.log(total)
    stats[own] = jnp.concatenate([jnp.transpose(lse)[:HEADS], jnp.transpose(delta)[:HEADS]], axis=0)
    sg.begin()
    for g in range(2 * HEADS):
        half, h = g // HEADS, g % HEADS
        start = ((h // 2) * 4 + half * 2 + h % 2) * ROW
        span = slice(start, start + ROW)
        run_m[span] = jnp.broadcast_to(lse[:, g : g + 1], (ROW, 128))
        run_l[span] = jnp.broadcast_to(delta[:, g : g + 1], (ROW, 128))

    def weights_of(ref, p_slot, pair):
        low_w, low_g = lows[pair]
        for i in range(PAIR // SUB):
            first = pair * PAIR + i * SUB
            to = slice(i * SUB, (i + 1) * SUB)
            lse_t, delta_t = run_m[first : first + SUB], run_l[first : first + SUB]
            for b in range(RING):
                w = jnp.exp(ref[tile_at(p_slot, b, first, SUB)] - lse_t)
                low_w[to, b * 128 : (b + 1) * 128] = w.astype(BF16)
                low_g[to, b * 128 : (b + 1) * 128] = (
                    w * (ref[tile_at(p_slot + 1, b, first, SUB)] - delta_t)
                ).astype(BF16)

    def add_products(pair, with_w, with_g):
        low_w, low_g = lows[pair]
        rows = slice(pair * PAIR, (pair + 1) * PAIR)
        acc_a[rows] += nn(low_w[...], with_w)
        acc_b[rows] += nn(low_g[...], with_g)

    def columns(pair):
        return slice(pair * 128, (pair + 1) * 128)

    def p0():
        dg.pass_on(1, 1, 2)

    def p1():
        dg.pass_on(0, 3)

    def p2():
        sg.other()

    def p3():
        dg.pass_on(1, 3)

    def forward(jj, skip):
        for p in (0, 1):
            j = 2 * jj + p
            steps(jj, p, {0: p0, 1: p1, 2: p2, 3: p3})
            before = jnp.maximum(j - 1, 0)
            add_products(1, values[before, :, columns(1)], keys[before, :, columns(1)])
            weights_of(holds[p], 2 * jj, 0)
            add_products(0, values[j, :, columns(0)], keys[j, :, columns(0)])
            weights_of(holds[p], 2 * jj, 1)
        return skip

    lax.fori_loop(0, CHUNKS // 2, forward, 0)
    add_products(1, values[CHUNKS - 1, :, columns(1)], keys[CHUNKS - 1, :, columns(1)])
    part_out[0] = unstack_heads(acc_a, 1)
    part_out[1] = unstack_heads(acc_b, 1)
    parts.start()
    kept[0] = unstack_heads(acc_a, 0)
    kept[1] = unstack_heads(acc_b, 0)
    clear()

    def attended_rows():
        parts.arrived()
        attended = (kept[0] + part_in[0]).astype(BF16)
        gproj[:, :CH] = ((kept[1] + part_in[1]) * (1.0 / math.sqrt(HDIM))).astype(BF16)
        hid[...] = (feat[...].astype(F32) + nn(attended, wout[...])).astype(BF16)
        out_part = tn(attended, glow[...])
        part = rest_sum.part
        part[2304:2560] = out_part[:, :128]
        part[2560:2816] = out_part[:, 128:]
        query_part = tn(feat[...], gproj[:, :CH])
        part[2816:3072] = query_part[:, :128]
        part[3072:3328] = query_part[:, 128:]
        part[3328:] = jnp.zeros((REST_ROWS - 3328, 128), F32)

    def conv_rows():
        mid = hid[...]
        every = tn(mid, sides[...])
        met = [every[:, side(r)] for r in range(4)]
        part = rest_sum.part
        for a, whole in enumerate((met[2] + met[3], met[1] + met[2], met[0] + met[1])):
            even_c, odd_c, even1, odd1 = (whole[:, k * CO : (k + 1) * CO] for k in range(4))
            part[(3 * a) * CH : (3 * a + 1) * CH] = even1 + odd_c
            part[(3 * a + 1) * CH : (3 * a + 2) * CH] = even_c + odd_c
            part[(3 * a + 2) * CH : (3 * a + 3) * CH] = even_c + odd1
        rest_sum.begin()

    def block_of(j):
        t, second = where_is(j)
        return grads[t, second].reshape(CHUNK, CH)

    def transposed_scores(j, p, pair):
        rows = slice(pair * PAIR, (pair + 1) * PAIR)
        put(holds[p], 0, pair, nt(qm[rows], queries[j, :, columns(pair)]))
        put(holds[p], 1, pair, nt(dm[rows], block_of(j)[:, columns(pair)]))

    def transposed_weights(j, p, pair):
        low_w, low_g = lows[pair]
        t, second = where_is(j)
        for part in range(4):
            h = 2 * pair + part % 2
            for i in range(ROW // SUB):
                first = part * ROW + i * SUB
                to = slice(first, first + SUB)
                for b in range(RING):
                    w = jnp.exp(holds[p][tile_at(0, b, pair * PAIR + first, SUB)] - stats[t, second, b, h : h + 1, :])
                    low_w[to, b * 128 : (b + 1) * 128] = w.astype(BF16)
                    low_g[to, b * 128 : (b + 1) * 128] = (
                        w * (holds[p][tile_at(1, b, pair * PAIR + first, SUB)] - stats[t, second, b, HEADS + h : HEADS + h + 1, :])
                    ).astype(BF16)

    def first_sums():
        attended_rows()
        conv_rows()

    def before_four():
        dg.last(0)

    def backward(jj, skip, final=False):
        for p in (0, 1):
            j = 2 * jj + p
            if final and p == 0:
                dg.last(1)
            if not final:
                steps(jj, p, {0: first_sums, 2: rest_sum.scatter, 3: before_four})
            before = jnp.maximum(j - 1, 0)
            more = not (final and p == 1)
            if more:
                transposed_scores(j + 1, 1 - p, 0)
            add_products(1, block_of(before)[:, columns(1)], queries[before, :, columns(1)])
            transposed_weights(j, p, 0)
            if more:
                transposed_scores(j + 1, 1 - p, 1)
            add_products(0, block_of(j)[:, columns(0)], queries[j, :, columns(0)])
            transposed_weights(j, p, 1)
        return skip

    pl.semaphore_wait(greet, 1)
    transposed_scores(0, 0, 0)
    transposed_scores(0, 0, 1)
    sg.last()
    lax.fori_loop(0, CHUNKS // 2 - 1, backward, 0)
    backward(CHUNKS // 2 - 1, 0, True)
    add_products(1, block_of(CHUNKS - 1)[:, columns(1)], queries[CHUNKS - 1, :, columns(1)])
    first_core = c == 0
    own_part = []
    for half in (0, 1):
        gk, gv = unstack_heads(acc_b, half), unstack_heads(acc_a, half)
        pair_out[1 - half] = jnp.where(first_core, gv, gk)
        own_part.append(jnp.where(first_core, gk, gv))
    pairs.start()
    rest_sum.along_z()
    pairs.arrived()
    done_rows = [(own_part[half] + pair_in[half]).astype(BF16) for half in (0, 1)]
    gone_out[...] = done_rows[1]
    final_rows.start()
    qkv_part = tn(jnp.concatenate([feat[...], sib_feat[...]], axis=0), jnp.concatenate(done_rows, axis=0))
    qkv_sum.scatter(jnp.concatenate([qkv_part[:, :128], qkv_part[:, 128:]], axis=0))
    final_rows.arrived()
    gproj[:, CH : 2 * CH] = jnp.where(first_core, done_rows[0], gone_in[...])
    gproj[:, 2 * CH :] = jnp.where(first_core, gone_in[...], done_rows[0])
    gf[...] = ghid[...] + nt(gproj[...], wqkv[...])
    rest_sum.spread()
    qkv_sum.along_z()
    qkv_sum.spread()
    rest_sum.swap()
    qkv_sum.swap()
    rest_sum.last()

    for group in (fg, dg, sg, rest_sum, qkv_sum):
        group.finish()
    for message in (sib_f, down_fine, up_fine, sib_g, tri, parts, pairs, final_rows):
        message.sent()


def scale_out(gf_in, rest, qkv, gf, gqkv, gout, gconv):
    coarse = 1.0 / math.sqrt(2 * 64 * ROW)
    fine_scale = 1.0 / math.sqrt(2 * 128 * 256)
    gf[...] = gf_in[...]
    gconv[...] = rest[:2304].astype(F32) * fine_scale
    for k in range(2):
        gout[:, k * 128 : (k + 1) * 128] = rest[2304 + k * CH : 2304 + (k + 1) * CH].astype(F32) * coarse
        gqkv[:, k * 128 : (k + 1) * 128] = rest[2816 + k * CH : 2816 + (k + 1) * CH].astype(F32) * coarse
    for k in range(4):
        gqkv[:, CH + k * 128 : CH + (k + 1) * 128] = qkv[k * CH : (k + 1) * CH].astype(F32) * coarse


def shards(features, qkv_weight, out_weight, conv_weight, grad_output):
    messages = 2 * AG_MSGS + ST_MSGS + RS_MSGS + WIDE_MSGS + 10
    whole = pl.BlockSpec(memory_space=pltpu.VMEM)
    sums = pl.pallas_call(
        kernel,
        out_shape=[
            jax.ShapeDtypeStruct((ROW, CH), F32),
            jax.ShapeDtypeStruct((REST_ROWS, 128), BF16),
            jax.ShapeDtypeStruct((QKV_ROWS, 128), BF16),
        ],
        in_specs=[whole] * 5,
        out_specs=[whole] * 3,
        scratch_shapes=[
            pltpu.VMEM((2, RING, RING, ROW, CH), BF16),
            pltpu.VMEM((2, RING, RING, ROW, CH), BF16),
            pltpu.VMEM((2, RING, RING, 2 * HEADS, ROW), F32),
            pltpu.VMEM((ROW, CH), BF16),
            pltpu.VMEM((ROW, CH), BF16),
            pltpu.VMEM((2, 2 * ROW, CO), BF16),
            pltpu.VMEM((ROW, 16 * CO), BF16),
            pltpu.VMEM((CHUNKS, CHUNK, CH), BF16),
            pltpu.VMEM((CHUNKS, CHUNK, CH), BF16),
            pltpu.VMEM((CHUNKS, CHUNK, CH), BF16),
            pltpu.VMEM((STACK, 128), BF16),
            pltpu.VMEM((STACK, 128), BF16),
            pltpu.VMEM((CHUNKS * SLOT, 128), F32),
            pltpu.VMEM((CHUNKS * SLOT, 128), F32),
            pltpu.VMEM((PAIR, CHUNK), BF16),
            pltpu.VMEM((PAIR, CHUNK), BF16),
            pltpu.VMEM((PAIR, CHUNK), BF16),
            pltpu.VMEM((PAIR, CHUNK), BF16),
            pltpu.VMEM((STACK, 128), F32),
            pltpu.VMEM((STACK, 128), F32),
            pltpu.VMEM((STACK, 128), F32),
            pltpu.VMEM((STACK, 128), F32),
            pltpu.VMEM((STACK, 128), F32),
            pltpu.VMEM((3, ROW, 128), F32),
            pltpu.VMEM((3, ROW, 128), F32),
            pltpu.VMEM((2, ROW, CH), F32),
            pltpu.VMEM((2, ROW, CH), F32),
            pltpu.VMEM((2, ROW, CH), F32),
            pltpu.VMEM((2, ROW, CH), F32),
            pltpu.VMEM((2, ROW, CH), F32),
            pltpu.VMEM((ROW, CH), BF16),
            pltpu.VMEM((ROW, CH), BF16),
            pltpu.VMEM((ROW, CH), F32),
            pltpu.VMEM((ROW, CH), BF16),
            pltpu.VMEM((ROW, 3 * CH), BF16),
            pltpu.VMEM((ROW, CH), BF16),
            pltpu.VMEM((2 * ROW + 8, CO), F32),
            *total_scratch(REST_ROWS),
            *total_scratch(QKV_ROWS),
            pltpu.SemaphoreType.DMA((messages,)),
            pltpu.SemaphoreType.DMA((messages,)),
            pltpu.SemaphoreType.REGULAR,
        ],
        compiler_params=pltpu.CompilerParams(
            collective_id=0, has_side_effects=True, vmem_limit_bytes=63 * 1024 * 1024
        ),
    )(
        features.reshape(ROW, CH),
        qkv_weight,
        out_weight,
        conv_weight.reshape(9, CH, CO),
        grad_output.reshape(2, 2 * ROW, CO),
    )
    gf, gqkv, gout, gconv = pl.pallas_call(
        scale_out,
        out_shape=[
            jax.ShapeDtypeStruct((ROW, CH), F32),
            jax.ShapeDtypeStruct((CH, 3 * CH), F32),
            jax.ShapeDtypeStruct((CH, CH), F32),
            jax.ShapeDtypeStruct((9 * CH, CO), F32),
        ],
        in_specs=[whole] * 3,
        out_specs=[whole] * 4,
        compiler_params=pltpu.CompilerParams(vmem_limit_bytes=62 * 1024 * 1024),
    )(*sums)
    return (
        gf.reshape(1, 1, ROW, CH),
        gqkv,
        gout,
        gconv.reshape(3, 3, CH, CO),
    )


def solution(mesh):
    in_specs = (P("dp", "space", None, None), P(), P(), P(), P("dp", "space", None, None))
    out_specs = (P("dp", "space", None, None), P(), P(), P())
    return jax.shard_map(shards, mesh=mesh, in_specs=in_specs, out_specs=out_specs, check_vma=False)
```
